32 devices in a mesh: member: 2 (over y), tile: 8 (over z, x), comp: 2 (over core).
Axes of the slice: x: 2, y: 2, z: 4, core: 2. Of those that a mesh axis runs over, the one named last changes fastest.
Arguments:
- atmosphere: bfloat16 [16384, 227], P(('member', 'tile', 'comp')), parts along dimension 0, may hold values from -6 to 6
- mesh_state: bfloat16 [10240, 512], P(('member', 'tile', 'comp')), parts along dimension 0, may hold values from -6 to 6
- edge_geometry: bfloat16 [4, 81920], P(None, ('member', 'tile', 'comp')), parts along dimension 1, may hold values from -6 to 6
- neighbours: int32 [10240, 8], P(('member', 'tile', 'comp')), parts along dimension 0, may hold values from 0 to 960, as said below
- grid_node: int32 [16384], P(('member', 'tile', 'comp')), parts along dimension 0, may hold values from 0 to 319
- ocean_heat_field: float32 [8, 288, 384], P(None, ('member', 'tile', 'comp')), parts along dimension 1, may hold values from -3.5 to 3.5
- east_velocity: float32 [8, 288, 384], P(None, ('member', 'tile', 'comp')), parts along dimension 1, may hold values from -0.3 to 0.3
- north_velocity: float32 [8, 288, 384], P(None, ('member', 'tile', 'comp')), parts along dimension 1, may hold values from -0.3 to 0.3
- ocean_mask: int32 [288, 384], P(('member', 'tile', 'comp')), parts along dimension 0, may hold values from 0 to 1
- intersection_points: int32 [32, 4, 192], P(('member', 'tile', 'comp')), parts along dimension 0, may hold values from 0 to 512, as said below
- intersection_counts: int32 [32, 4], P(('member', 'tile', 'comp')), parts along dimension 0, may hold values from 1 to 192, as said below
- w_geometry: bfloat16 [4, 512], replicated, may hold values from -3 to 3
- w_encode: bfloat16 [227, 512], replicated, may hold values from -0.375 to 0.375
- w_edge_in: bfloat16 [1536, 512], replicated, may hold values from -0.15625 to 0.15625
- w_edge_out: bfloat16 [512, 512], replicated, may hold values from -0.25 to 0.25
- w_node_in: bfloat16 [1024, 512], replicated, may hold values from -0.1875 to 0.1875
- w_node_out: bfloat16 [512, 512], replicated, may hold values from -0.25 to 0.25
- w_decode: bfloat16 [512, 227], replicated, may hold values from -0.25 to 0.25
- gain_edge: float32 [512], replicated, may hold values from 0.25 to 1.75
- gain_node: float32 [512], replicated, may hold values from 0.25 to 1.75
Outputs:
- atmosphere_new: bfloat16 [16384, 227], P(('member', 'tile', 'comp')), parts along dimension 0
- ocean_new: float32 [8, 288, 384], P(None, ('member', 'tile', 'comp')), parts along dimension 1
The draws below stay inside these ranges and needn't reach their ends.
There are 2 independent parts, one for each index of `member`. The reference program is written for one: setup_inputs(seed, part) draws one part's arguments, and reference() takes and returns one part's arrays. A program takes and returns all parts, laid end to end along the dimension named above; an argument that names none is the same for every part. Nothing has to cross between parts.
Inputs may be any that keep to these rules, and one draw needn't show every extreme that they name: `neighbours`: each row holds between 5 and 8 entries below 960 first, then entries equal to 960, which mark empty slots. `intersection_counts`: each row sums to 384 and reaches 192. `intersection_points`: entry [s, o, j] is below 512 exactly when j < intersection_counts[(s - o + 2) mod 16, o], and equals 512 otherwise.
All inputs are finite; a program needn't handle non-finite values.
Results may differ from the reference program's by a relative error of at most 0.0075.
Values may be sent and summed in bfloat16 or wider, within the bound.
No kernel may reach another device: no remote copies, remote signals or barrier semaphores. Data moves between devices by JAX's collectives and lax.ppermute only.
A program may use at most 64 MiB of HBM per device.

```python
import jax
import jax.numpy as jnp
from jax import lax

C = 227
L = 512
K = 8
M_DEV = 320
G_DEV = 512
LEV = 8
OX_DEV = 9
OY = 384
STEPS = 4
W = 4
NDEV = 16
MT = 5120
GLOBAL_POINTS = 8192
OXT = 144
OB = 384
BLOCK_LIMIT = 192


def counts_law(key):
    key = jax.random.fold_in(key, 11)
    key_fullest, key_spread = jax.random.split(key)
    offsets = jnp.arange(W, dtype=jnp.int32)[None, :]
    fullest = jax.random.randint(key_fullest, (NDEV, 1), 0, W, dtype=jnp.int32)
    spread = jax.random.randint(key_spread, (NDEV, W), 50, 101, dtype=jnp.int32)
    spread = jnp.where(offsets == fullest, 0, spread)
    spare = OB - BLOCK_LIMIT - (W - 1)
    portion = spare * spread // jnp.sum(spread, axis=1, keepdims=True)
    sized = jnp.where(offsets == fullest, BLOCK_LIMIT, 1 + portion)
    remainder = OB - jnp.sum(sized, axis=1, keepdims=True)
    topped = (fullest + 1) % W
    return (sized + jnp.where(offsets == topped, remainder, 0)).astype(jnp.int32)


def draw_intersection_counts(key, part):
    return counts_law(key)


def draw_intersection_points(key, part):
    counts = counts_law(key)
    key = jax.random.fold_in(key, 5)
    points = jax.random.randint(key, (NDEV, W, BLOCK_LIMIT), 0, G_DEV, dtype=jnp.int32)
    sender = jnp.arange(NDEV, dtype=jnp.int32)[:, None]
    offsets = jnp.arange(W, dtype=jnp.int32)[None, :]
    target = (sender - (offsets - W // 2)) % NDEV
    filled = counts[target, jnp.broadcast_to(offsets, target.shape)]
    slot_index = jnp.arange(BLOCK_LIMIT, dtype=jnp.int32)[None, None, :]
    return jnp.where(slot_index < filled[:, :, None], points, G_DEV).astype(jnp.int32)


def draw_neighbours(key, part):
    key = jax.random.fold_in(key, 3)
    key_pick, key_degree = jax.random.split(key)
    chosen = jax.random.randint(key_pick, (MT, K), 0, 3 * M_DEV, dtype=jnp.int32)
    degree = jax.random.randint(key_degree, (MT, 1), K - 3, K + 1, dtype=jnp.int32)
    position = jnp.arange(K, dtype=jnp.int32)[None, :]
    return jnp.where(position < degree, chosen, 3 * M_DEV).astype(jnp.int32)


def draw_ocean_mask(key, part):
    key = jax.random.fold_in(key, 7)
    key_block, key_cell = jax.random.split(key)
    coarse = jax.random.randint(key_block, (OXT // 3, 1, OY // 3, 1), 0, 4, dtype=jnp.int32) == 0
    coarse = jnp.broadcast_to(coarse, (OXT // 3, 3, OY // 3, 3)).reshape(OXT, OY)
    single = jax.random.randint(key_cell, (OXT, OY), 0, 8, dtype=jnp.int32) == 0
    return jnp.where(coarse | single, 0, 1).astype(jnp.int32)


def draw_ocean_heat_field(key, part):
    key = jax.random.fold_in(key, 9)
    return jnp.clip(jax.random.normal(key, (LEV, OXT, OY), jnp.float32), -3.5, 3.5)


def place_ends(result, own_key, low, largest):
    longest = result.shape.index(max(result.shape))
    spots = []
    for shift in (0, 1):
        where = [jax.random.randint(jax.random.fold_in(own_key, axis), (), 0, length) for axis, length in enumerate(result.shape)]
        where[longest] = (where[longest] + shift) % result.shape[longest]
        spots.append(tuple(where))
    return result.at[spots[0]].set(low).at[spots[1]].set(largest)


def shard_levels(rng, shape, cuts, smallest, top_value):
    def one(axis_at, blocks):
        steps = jax.random.uniform(jax.random.fold_in(jax.random.fold_in(rng, 6), axis_at), (blocks,), jnp.float32, smallest / len(cuts), top_value / len(cuts))
        return jnp.repeat(jnp.exp(steps), shape[axis_at] // blocks).reshape((-1,) + (1,) * (len(shape) - axis_at - 1))

    level = one(*cuts[0])
    for cut in cuts[1:]:
        level = level * one(*cut)
    return level


def normal_values(own_key, shape, scale, limit, shards=(), kind=jnp.bfloat16):
    gain = shard_levels(own_key, shape, shards, -0.22, 0.18) if shards else 1.0
    drawn = jax.random.normal(own_key, shape, jnp.float32) * scale * gain
    return jnp.minimum(jnp.maximum(drawn, -limit), limit).astype(kind)


def setup_inputs(seed: int = 0, part: int = 0) -> dict:
    streams_of = jax.random.split(jax.random.key(seed), 21)
    part_keys = jax.random.split(jax.random.fold_in(streams_of[20], part), 21)
    atmosphere = normal_values(part_keys[0], (GLOBAL_POINTS, C), 1.0, 6.0, ((0, 16),))
    mesh_state = normal_values(part_keys[1], (MT, L), 1.0, 6.0, ((0, 16),))
    edge_geometry = normal_values(part_keys[2], (4, MT * K), 1.0, 6.0, ((1, 16),))
    neighbours = draw_neighbours(jax.random.fold_in(jax.random.fold_in(streams_of[20], part), 71), part)
    grid_node = place_ends(jax.random.randint(part_keys[4], (GLOBAL_POINTS,), 0, M_DEV), jax.random.fold_in(part_keys[4], 1), 0, M_DEV - 1).astype(jnp.int32)
    ocean_heat_field = draw_ocean_heat_field(jax.random.fold_in(jax.random.fold_in(streams_of[20], part), 71), part)
    east_velocity = jnp.clip(jax.random.uniform(part_keys[6], (LEV, OXT, OY), jnp.float32, -0.3, 0.3) * shard_levels(part_keys[6], (LEV, OXT, OY), ((1, 16),), -0.4, 0.0), -0.3, 0.3)
    north_velocity = jnp.clip(jax.random.uniform(part_keys[7], (LEV, OXT, OY), jnp.float32, -0.3, 0.3) * shard_levels(part_keys[7], (LEV, OXT, OY), ((1, 16),), -0.4, 0.0), -0.3, 0.3)
    ocean_mask = draw_ocean_mask(jax.random.fold_in(jax.random.fold_in(streams_of[20], part), 71), part)
    intersection_points = draw_intersection_points(jax.random.fold_in(jax.random.fold_in(streams_of[20], part), 71), part)
    intersection_counts = draw_intersection_counts(jax.random.fold_in(jax.random.fold_in(streams_of[20], part), 71), part)
    w_geometry = normal_values(streams_of[11], (4, L), 4 ** -0.5, 3.0)
    w_encode = normal_values(streams_of[12], (C, L), C ** -0.5, 0.375)
    w_edge_in = normal_values(streams_of[13], (3 * L, L), (3 * L) ** -0.5, 0.15625)
    w_edge_out = normal_values(streams_of[14], (L, L), L ** -0.5, 0.25)
    w_node_in = normal_values(streams_of[15], (2 * L, L), (2 * L) ** -0.5, 0.1875)
    w_node_out = normal_values(streams_of[16], (L, L), L ** -0.5, 0.25)
    w_decode = normal_values(streams_of[17], (L, C), L ** -0.5, 0.25)
    gain_edge = jnp.clip(1.0 + 0.15 * jax.random.normal(streams_of[18], (L,), jnp.float32), 0.25, 1.75)
    gain_node = jnp.clip(1.0 + 0.15 * jax.random.normal(streams_of[19], (L,), jnp.float32), 0.25, 1.75)
    return {"atmosphere": atmosphere, "mesh_state": mesh_state, "edge_geometry": edge_geometry, "neighbours": neighbours, "grid_node": grid_node, "ocean_heat_field": ocean_heat_field, "east_velocity": east_velocity, "north_velocity": north_velocity, "ocean_mask": ocean_mask, "intersection_points": intersection_points, "intersection_counts": intersection_counts, "w_geometry": w_geometry, "w_encode": w_encode, "w_edge_in": w_edge_in, "w_edge_out": w_edge_out, "w_node_in": w_node_in, "w_node_out": w_node_out, "w_decode": w_decode, "gain_edge": gain_edge, "gain_node": gain_node}


COEFF_H = 0.15
COEFF_V = 0.1
COEFF_Q = 0.5
EPSILON = 1e-05

def layer_norm(values, gain_row):
    average = lax.optimization_barrier(jnp.mean(values, axis=-1, keepdims=True))
    centred = values - average
    variance = lax.optimization_barrier(jnp.mean(centred * centred, axis=-1, keepdims=True))
    return centred * lax.rsqrt(variance + EPSILON) * gain_row

def ocean_step(field_wide, east_wide, north_wide, wet_wide, forcing_wide):
    east_open = wet_wide[:-1] * wet_wide[1:]
    east_face = 0.5 * (east_wide[:, :-1] + east_wide[:, 1:])
    east_flux = east_open * (east_face * 0.5 * (field_wide[:, :-1] + field_wide[:, 1:]) - COEFF_H * (field_wide[:, 1:] - field_wide[:, :-1]))
    east_change = east_flux[:, 1:] - east_flux[:, :-1]
    centre = field_wide[:, 1:-1]
    north_here = north_wide[:, 1:-1]
    wet_here = wet_wide[1:-1]
    north_open = wet_here[:, :-1] * wet_here[:, 1:]
    north_face = 0.5 * (north_here[:, :, :-1] + north_here[:, :, 1:])
    north_flux = north_open * (north_face * 0.5 * (centre[:, :, :-1] + centre[:, :, 1:]) - COEFF_H * (centre[:, :, 1:] - centre[:, :, :-1]))
    wall_zeros = jnp.zeros(north_flux.shape[:2] + (1,), north_flux.dtype)
    north_flux = jnp.concatenate([wall_zeros, north_flux, wall_zeros], axis=2)
    north_change = north_flux[:, :, 1:] - north_flux[:, :, :-1]
    mixing = COEFF_V * (centre[1:] - centre[:-1]) * wet_here
    level_zeros = jnp.zeros((1,) + mixing.shape[1:], mixing.dtype)
    mixing = jnp.concatenate([level_zeros, mixing, level_zeros], axis=0)
    vertical = mixing[1:] - mixing[:-1]
    tendency = vertical - east_change - north_change
    surface = COEFF_Q * forcing_wide[1:-1] * wet_here
    tendency = jnp.concatenate([tendency[:1] + surface[None], tendency[1:]], axis=0)
    return wet_here * (centre + tendency)

def wrap_pad(array, axis_x):
    count = array.shape[axis_x]
    leading = lax.slice_in_dim(array, count - 1, count, axis=axis_x)
    trailing = lax.slice_in_dim(array, 0, 1, axis=axis_x)
    return jnp.concatenate([leading, array, trailing], axis=axis_x)

def reference(atmosphere, mesh_state, edge_geometry, neighbours, grid_node, ocean_heat_field, east_velocity, north_velocity, ocean_mask, intersection_points, intersection_counts, w_geometry, w_encode, w_edge_in, w_edge_out, w_node_in, w_node_out, w_decode, gain_edge, gain_node):
    device_list = NDEV
    wet_fraction = ocean_mask.astype(jnp.float32)
    upper_level_heat = (ocean_heat_field[0] * wet_fraction).reshape(device_list, OX_DEV // 3, 3, OY // 3, 3).sum(axis=(2, 4)).reshape(device_list, OB)
    wet_point_count = wet_fraction.reshape(device_list, OX_DEV // 3, 3, OY // 3, 3).sum(axis=(2, 4)).reshape(device_list, OB)
    block_surface_temps = upper_level_heat / jnp.maximum(wet_point_count, 1.0)
    block_wet = jnp.where(wet_point_count > 0.5, 1.0, 0.0)
    offsets = jnp.arange(W, dtype=jnp.int32) - W // 2
    device_ids = jnp.arange(device_list, dtype=jnp.int32)
    sources = (device_ids[:, None] + offsets[None, :]) % device_list
    start_positions = jnp.cumsum(intersection_counts, axis=1) - intersection_counts
    slot_index = jnp.arange(BLOCK_LIMIT, dtype=jnp.int32)
    active_positions = slot_index[None, None, :] < intersection_counts[:, :, None]
    block_labels = jnp.where(active_positions, start_positions[:, :, None] + slot_index[None, None, :], OB)
    offset_grid = jnp.broadcast_to(jnp.arange(W, dtype=jnp.int32)[None, :], sources.shape)
    local_points = intersection_points[sources, offset_grid]
    point_labels = jnp.where(active_positions, sources[:, :, None] * G_DEV + local_points, GLOBAL_POINTS)
    surface_temp_padded = jnp.concatenate([block_surface_temps, jnp.zeros((device_list, 1), jnp.float32)], axis=1)
    wet_pad = jnp.concatenate([block_wet, jnp.zeros((device_list, 1), jnp.float32)], axis=1)
    outgoing_surface_temps = jnp.take_along_axis(surface_temp_padded, block_labels.reshape(device_list, -1), axis=1)
    outgoing_wet_flags = jnp.take_along_axis(wet_pad, block_labels.reshape(device_list, -1), axis=1)
    surface_temp_sum = jnp.zeros((GLOBAL_POINTS + 1,), jnp.float32).at[point_labels.reshape(-1)].add(outgoing_surface_temps.reshape(-1))[:GLOBAL_POINTS]
    surface_temp_count = jnp.zeros((GLOBAL_POINTS + 1,), jnp.float32).at[point_labels.reshape(-1)].add(outgoing_wet_flags.reshape(-1))[:GLOBAL_POINTS]
    starting_state = atmosphere[:, 0].astype(jnp.float32)
    surface_temp_updated = jnp.where(surface_temp_count > 0.5, surface_temp_sum / jnp.maximum(surface_temp_count, 1.0), starting_state)
    coupled_system = atmosphere.at[:, 0].set(surface_temp_updated.astype(jnp.bfloat16))
    encoded = jnp.dot(coupled_system, w_encode, preferred_element_type=jnp.float32).astype(jnp.bfloat16)
    grid_owner = jnp.arange(GLOBAL_POINTS, dtype=jnp.int32) // G_DEV
    global_node = (grid_owner * M_DEV + grid_node).astype(jnp.int32)
    pooled = jax.ops.segment_sum(encoded.astype(jnp.float32), global_node, num_segments=MT)
    pooled_count = jax.ops.segment_sum(jnp.ones((GLOBAL_POINTS,), jnp.float32), global_node, num_segments=MT)
    latent = (mesh_state.astype(jnp.float32) + pooled / jnp.maximum(pooled_count, 1.0)[:, None]).astype(jnp.bfloat16)
    features = latent.shape[1]

    def process(device):
        first_node = (device * M_DEV).astype(jnp.int32)
        own_nodes = lax.dynamic_slice_in_dim(latent, first_node, M_DEV, 0)
        link_rows = lax.dynamic_slice_in_dim(neighbours, first_node, M_DEV, 0)
        geometry = lax.dynamic_slice_in_dim(edge_geometry, (first_node * K).astype(jnp.int32), M_DEV * K, 1)
        real_edge = link_rows < 3 * M_DEV
        sender_ids = jnp.where(real_edge, (first_node + link_rows - M_DEV) % MT, first_node).astype(jnp.int32)
        edge_latent = jax.nn.silu(lax.dot_general(geometry, w_geometry, (((0,), (0,)), ((), ())), preferred_element_type=jnp.float32)).astype(jnp.bfloat16)
        senders = jnp.take(latent, sender_ids.reshape(-1), axis=0)
        receivers = jnp.repeat(own_nodes, K, axis=0)
        joined = jnp.concatenate([edge_latent, senders, receivers], axis=1)
        edge_hidden = jax.nn.silu(jnp.dot(joined, w_edge_in, preferred_element_type=jnp.float32)).astype(jnp.bfloat16)
        edge_out = jnp.dot(edge_hidden, w_edge_out, preferred_element_type=jnp.float32)
        edge_new = edge_latent.astype(jnp.float32) + layer_norm(edge_out, gain_edge)
        edge_new = edge_new * real_edge.reshape(-1, 1).astype(jnp.float32)
        aggregate = lax.optimization_barrier(jnp.sum(edge_new.reshape(M_DEV, K, features), axis=1)).astype(jnp.bfloat16)
        node_input = jnp.concatenate([own_nodes, aggregate], axis=1)
        node_hidden = jax.nn.silu(jnp.dot(node_input, w_node_in, preferred_element_type=jnp.float32)).astype(jnp.bfloat16)
        node_out = jnp.dot(node_hidden, w_node_out, preferred_element_type=jnp.float32)
        return (own_nodes.astype(jnp.float32) + layer_norm(node_out, gain_node)).astype(jnp.bfloat16)
    node_new = lax.map(process, jnp.arange(device_list, dtype=jnp.int32)).reshape(MT, features)
    picked = jnp.take(node_new, global_node, axis=0)
    atmosphere_new = (coupled_system.astype(jnp.float32) + jnp.dot(picked, w_decode, preferred_element_type=jnp.float32)).astype(jnp.bfloat16)
    flux_pad = jnp.concatenate([atmosphere_new[:, 1], jnp.zeros((1,), jnp.bfloat16)]).astype(jnp.float32)
    arriving = jnp.where(active_positions, jnp.take(flux_pad, point_labels.reshape(-1)).reshape(active_positions.shape), 0.0)
    block_flux = jnp.zeros((device_list, OB + 1), jnp.float32).at[device_ids[:, None, None], block_labels].add(arriving)[:, :OB]
    forcing = jnp.broadcast_to(block_flux.reshape(device_list, OX_DEV // 3, 1, OY // 3, 1), (device_list, OX_DEV // 3, 3, OY // 3, 3)).reshape(OXT, OY)
    current = ocean_heat_field
    east_wide = wrap_pad(east_velocity, 1)
    north_wide = wrap_pad(north_velocity, 1)
    wet_wide = wrap_pad(wet_fraction, 0)
    forcing_wide = wrap_pad(forcing, 0)
    for step_index in range(STEPS):
        current = ocean_step(wrap_pad(current, 1), east_wide, north_wide, wet_wide, forcing_wide)
    return (atmosphere_new, current)
```

```python
import functools

import jax
import jax.numpy as jnp
from jax import lax
from jax.experimental import pallas as pl
from jax.experimental.pallas import tpu as pltpu
from jax.sharding import PartitionSpec as P

K = 8
STEPS = 4
W = 4
EDGE = 4

COEFF_H = 0.15
COEFF_V = 0.1
COEFF_Q = 0.5
EPSILON = 1e-05

F32 = jnp.float32
BF16 = jnp.bfloat16
AXES = ("tile", "comp")


def shifted(block, distance):
    count = lax.axis_size(AXES)
    return lax.ppermute(block, AXES, [((i - distance) % count, i) for i in range(count)])


def dot(a, b):
    return jnp.dot(a, b, preferred_element_type=F32)


def dot_nt(a, b):
    return lax.dot_general(a, b, (((1,), (1,)), ((), ())), preferred_element_type=F32)


def silu(v):
    return 0.5 * v * (1.0 + jnp.tanh(0.5 * v))


def one_hot(test):
    return jnp.where(test, 1.0, 0.0).astype(BF16)


def iota(shape, dim):
    return lax.broadcasted_iota(jnp.int32, shape, dim)


def pack_kernel(counts, heat, east, north, mask, low_out, high_out, blocks_out):
    columns, rows = mask.shape
    wet = mask[...].astype(F32)
    top = heat[0] * wet
    triples = columns // 3

    def over_columns(x):
        return jnp.concatenate(
            [x[3 * t : 3 * t + 1] + x[3 * t + 1 : 3 * t + 2] + x[3 * t + 2 : 3 * t + 3] for t in range(triples)],
            axis=0,
        )

    sums = over_columns(top)
    first = sums.astype(BF16).astype(F32)
    second = (sums - first).astype(BF16).astype(F32)
    third = sums - first - second
    parts = jnp.concatenate(
        [first, second, third, over_columns(wet), jnp.zeros((16 - 4 * triples, rows), F32)], axis=0
    ).astype(BF16)
    pick = one_hot(iota((rows, rows // 3), 0) // 3 == iota((rows, rows // 3), 1))
    folded = dot(parts, pick)

    def flat(x):
        return jnp.concatenate([x[t : t + 1] for t in range(triples)], axis=1)

    t = triples
    total = flat(folded[:t] + folded[t : 2 * t] + folded[2 * t : 3 * t])
    number = flat(folded[3 * t : 4 * t])
    mean = total / jnp.maximum(number, 1.0)
    mean_high = mean.astype(BF16).astype(F32)
    flags = jnp.where(number > 0.5, 1.0, 0.0)
    lane = iota((1, rows), 1)
    held = jnp.zeros((1, rows), F32)
    for o in range(W):
        held = jnp.where(lane == o, counts[0, o].astype(F32), held)
    bundle = jnp.concatenate(
        [mean_high, mean - mean_high, flags, held, jnp.zeros((4, rows), F32)], axis=0
    )
    blank = jnp.zeros((4, rows), F32)
    for out, begin in ((low_out, 0), (high_out, columns - EDGE)):
        pieces = [source[:, c, :] for source in (heat, east, north) for c in range(begin, begin + EDGE)]
        pieces += [wet[begin : begin + EDGE], blank, bundle]
        out[...] = jnp.concatenate(pieces, axis=0).astype(BF16)
    blocks_out[...] = jnp.concatenate([bundle, jnp.zeros((8, rows), F32)], axis=0).astype(BF16)


def embed_kernel(geometry, w_geometry, w_in, latent_out, part_out, turned):
    edges = geometry.shape[1]
    nodes = edges // K
    flat = jnp.concatenate([geometry[...].astype(F32), jnp.zeros((4, edges), F32)], axis=0)
    turned[:, :8] = flat.T
    weights = w_in[...]
    features = w_geometry.shape[1]
    w_geo = jnp.concatenate([w_geometry[...].astype(F32), jnp.zeros((4, features), F32)], axis=0).astype(BF16)
    for k in range(K):
        points = turned[pl.ds(k, nodes, stride=K), :8].astype(BF16)
        value = silu(dot(points, w_geo)).astype(BF16)
        latent_out[k] = value
        part_out[k] = dot(value, weights).astype(BF16)


def rolled_points(points, starts):
    rows = 2 * points.shape[1]
    empty = jnp.full((1, rows - points.shape[1]), 1 << 20, jnp.int32)
    return [
        pltpu.roll(jnp.concatenate([points[o : o + 1, :], empty], axis=1), starts[o], 1) for o in range(W)
    ]


def before(bundle_rows, o):
    lane = iota((1, bundle_rows.shape[1]), 1)
    return jnp.sum(jnp.where(lane < o, bundle_rows[3:4], 0.0)).astype(jnp.int32)


def latent_kernel(
    counts, far, above, own, below, points, atmosphere, w_encode, grid_node, mesh_state,
    latent_out, coupled_out, placed_out,
):
    parts = [
        far[...].astype(F32)[:8],
        above[...].astype(F32)[-8:],
        own[...].astype(F32)[:8],
        below[...].astype(F32)[-8:],
    ]
    starts = [0, before(parts[1], 1), counts[0, 0] + counts[0, 1], before(parts[3], 3)]
    placed = jnp.concatenate(rolled_points(points, starts), axis=1)
    placed_out[...] = placed
    n_points = atmosphere.shape[0]
    values = jnp.concatenate(parts, axis=1).astype(BF16)
    match = one_hot(iota((n_points, placed.shape[1]), 0) == placed)
    sums = dot_nt(match, values)
    total = sums[:, 0:1] + sums[:, 1:2]
    number = sums[:, 2:3]
    state = atmosphere[...].astype(F32)
    surface = jnp.where(number > 0.5, total / jnp.maximum(number, 1.0), state[:, 0:1])
    coupled = jnp.where(iota(state.shape, 1) == 0, surface, state).astype(BF16)
    coupled_out[...] = coupled
    encoded = dot(coupled, w_encode[...]).astype(BF16)
    member = jnp.where(iota((mesh_state.shape[0], n_points), 0) == grid_node[...], 1.0, 0.0)
    population = jnp.sum(member, axis=1, keepdims=True)
    pooled = dot(member.astype(BF16), encoded)
    latent_out[...] = (mesh_state[...].astype(F32) + pooled / jnp.maximum(population, 1.0)).astype(BF16)


def slot_senders(neighbours, k):
    lane = iota(neighbours.shape, 1)
    return jnp.sum(jnp.where(lane == k, neighbours, 0.0), axis=1, keepdims=True).astype(jnp.int32)


def own_kernel(latent, w_in, part, edge_latent, neighbours, pre_out, base_out, sender):
    nodes, features = latent.shape
    value = latent[...]
    sender[...] = dot(value, w_in[features : 2 * features]).astype(BF16)
    receiver = dot(value, w_in[2 * features :])
    listed = neighbours[...].astype(F32)

    def step(k, base):
        at = slot_senders(listed, k)
        match = one_hot(iota((nodes, nodes), 1) + nodes == at)
        pre_out[k] = (part[k].astype(F32) + receiver + dot(match, sender[...])).astype(BF16)
        return base + jnp.where(at < 3 * nodes, edge_latent[k].astype(F32), 0.0)

    base_out[...] = lax.fori_loop(0, K, step, jnp.zeros((nodes, features), F32))


def normal(values):
    average = jnp.mean(values, axis=-1, keepdims=True)
    centred = values - average
    variance = jnp.mean(centred * centred, axis=-1, keepdims=True)
    return centred, lax.rsqrt(variance + EPSILON)


def mesh_kernel(
    low, high, latent, w_in, w_out, pre, base, neighbours, w_node_in, w_node_out, w_decode,
    gain_edge, gain_node, grid_node, coupled, placed, state_out, flux_out, sender, total,
):
    nodes, features = latent.shape
    w_sender = w_in[features : 2 * features]
    sender[:nodes] = dot(low[...], w_sender).astype(BF16)
    sender[nodes:] = dot(high[...], w_sender).astype(BF16)
    listed = neighbours[...].astype(F32)
    total[...] = jnp.zeros((nodes, features), F32)

    def step(k, carry):
        at = slot_senders(listed, k)
        place = jnp.where(at < nodes, at, jnp.where(at >= 2 * nodes, at - nodes, -1))
        match = one_hot(iota((nodes, 2 * nodes), 1) == place)
        hidden = silu(pre[k].astype(F32) + dot(match, sender[...])).astype(BF16)
        centred, scale = normal(dot(hidden, w_out[...]))
        total[...] += centred * jnp.where(at < 3 * nodes, scale, 0.0)
        return carry

    lax.fori_loop(0, K, step, 0)
    aggregate = (base[...] + total[...] * gain_edge[...]).astype(BF16)
    own = latent[...]
    hidden = silu(dot(own, w_node_in[:features]) + dot(aggregate, w_node_in[features:])).astype(BF16)
    centred, scale = normal(dot(hidden, w_node_out[...]))
    node_new = (own.astype(F32) + centred * scale * gain_node[...]).astype(BF16)
    n_points = coupled.shape[0]
    member = one_hot(iota((nodes, n_points), 0) == grid_node[...])
    picked = lax.dot_general(member, node_new, (((0,), (0,)), ((), ())), preferred_element_type=F32)
    state = (coupled[...].astype(F32) + dot(picked.astype(BF16), w_decode[...])).astype(BF16)
    state_out[...] = state
    channels = state.shape[1]
    flux = dot_nt(one_hot(iota((8, channels), 1) == 1), state).astype(BF16)
    match = one_hot(iota((n_points, placed.shape[1]), 0) == placed[...])
    spread = dot(flux, match)
    rows = placed.shape[1] // W
    out = jnp.zeros((8, rows), F32)
    for o in range(W):
        out = jnp.where(iota((8, rows), 0) == o, spread[:, o * rows : (o + 1) * rows], out)
    flux_out[...] = jnp.concatenate([out, jnp.zeros((8, rows), F32)], axis=0).astype(BF16)


def ready_kernel(heat, east, north, mask, low, high, field_out, wet_out, px_out, qx_out, py_out, qy_out, mix_out):
    columns, rows = mask.shape
    levels = heat.shape[0]
    below, above = low[...].astype(F32), high[...].astype(F32)
    own_wet = mask[...].astype(F32)

    def wide(source, at):
        left = [below[8 * (at * EDGE + c) : 8 * (at * EDGE + c) + 8] for c in range(EDGE)]
        right = [above[8 * (at * EDGE + c) : 8 * (at * EDGE + c) + 8] for c in range(EDGE)]
        return left + [source[:, c, :] for c in range(columns)] + right

    base = 3 * 8 * EDGE
    wet = [below[base + c : base + c + 1] for c in range(EDGE)]
    wet += [own_wet[c : c + 1] for c in range(columns)]
    wet += [above[base + c : base + c + 1] for c in range(EDGE)]
    wet = [jnp.broadcast_to(w, (levels, rows)) for w in wet]
    field, u, v = wide(heat, 0), wide(east, 1), wide(north, 2)
    lane = iota((levels, rows), 1)
    level = iota((levels, rows), 0)
    count = len(field)
    for c in range(count):
        field_out[c] = field[c]
        wet_out[c] = wet[c]
        mix_out[c] = jnp.where(level < levels - 1, COEFF_V * wet[c], 0.0)
        if c + 1 < count:
            opened = wet[c] * wet[c + 1]
            face = 0.25 * (u[c] + u[c + 1])
            px_out[c] = opened * (face + COEFF_H)
            qx_out[c] = opened * (face - COEFF_H)
        opened = jnp.where(lane < rows - 1, wet[c] * pltpu.roll(wet[c], rows - 1, 1), 0.0)
        face = 0.25 * (v[c] + pltpu.roll(v[c], rows - 1, 1))
        py_out[c] = opened * (face + COEFF_H)
        qy_out[c] = opened * (face - COEFF_H)


def ocean_kernel(f_m3, f_m2, f_m1, f_0, f_p1, f_p2, field_in, wet, px, qx, py, qy, mix, out):
    count, levels, rows = field_in.shape
    columns = count - 2 * EDGE
    triples = columns // 3
    span = rows // 3
    fluxes = [f[...].astype(F32) for f in (f_m3, f_m2, f_m1, f_0, f_p1, f_p2)]

    def gathered(begin):
        return sum(fluxes[begin + o][o : o + 1] for o in range(W))

    own = gathered(1)
    blocks = [gathered(0)[:, (triples - 1) * span :]]
    blocks += [own[:, t * span : (t + 1) * span] for t in range(triples)]
    blocks += [gathered(2)[:, :span]]
    blocks += [jnp.zeros((16 - len(blocks), span), F32)]
    expand = one_hot(iota((span, rows), 1) // 3 == iota((span, rows), 0))
    cells = COEFF_Q * dot(jnp.concatenate(blocks, axis=0).astype(BF16), expand)
    level = iota((levels, rows), 0)
    surface = [
        jnp.where(level == 0, jnp.broadcast_to(cells[t : t + 1], (levels, rows)), 0.0)
        for t in range(triples + 2)
    ]
    field = [field_in[c] for c in range(count)]
    for step in range(STEPS):
        begin, end = step + 1, count - step - 1
        across = {c: px[c] * field[c] + qx[c] * field[c + 1] for c in range(begin - 1, end)}
        later = [None] * count
        for c in range(begin, end):
            here = field[c]
            along = py[c] * here + qy[c] * pltpu.roll(here, rows - 1, 1)
            mixed = mix[c] * (pltpu.roll(here, levels - 1, 0) - here)
            group = (c - EDGE + 3) // 3
            change = (
                (across[c - 1] - across[c])
                + (pltpu.roll(along, 1, 1) - along)
                + (mixed - pltpu.roll(mixed, 1, 0))
            )
            later[c] = wet[c] * (here + change + surface[group])
        field = later
    for c in range(columns):
        out[:, c, :] = field[EDGE + c]


def call(kernel, outs, inputs, smem=0, scratch=(), flops=0, bytes_accessed=1 << 20, name=None):
    vmem = pl.BlockSpec(memory_space=pltpu.VMEM)
    specs = [pl.BlockSpec(memory_space=pltpu.SMEM)] * smem + [vmem] * (len(inputs) - smem)
    return pl.pallas_call(
        kernel,
        out_shape=[jax.ShapeDtypeStruct(s, t) for s, t in outs],
        in_specs=specs,
        out_specs=[vmem] * len(outs),
        scratch_shapes=list(scratch),
        compiler_params=pltpu.CompilerParams(vmem_limit_bytes=40 << 20),
        cost_estimate=pl.CostEstimate(flops=flops, bytes_accessed=bytes_accessed, transcendentals=0),
        name=name,
    )(*inputs)


def body(
    atmosphere,
    mesh_state,
    edge_geometry,
    neighbours,
    grid_node,
    ocean_heat_field,
    east_velocity,
    north_velocity,
    ocean_mask,
    intersection_points,
    intersection_counts,
    w_geometry,
    w_encode,
    w_edge_in,
    w_edge_out,
    w_node_in,
    w_node_out,
    w_decode,
    gain_edge,
    gain_node,
):
    levels, columns, rows = ocean_heat_field.shape
    nodes, features = mesh_state.shape
    n_points, channels = atmosphere.shape
    ends = (3 * levels * EDGE + 16, rows)
    few = (16, rows)
    low, high, blocks = call(
        pack_kernel,
        [(ends, BF16), (ends, BF16), (few, BF16)],
        [intersection_counts, ocean_heat_field, east_velocity, north_velocity, ocean_mask],
        smem=1,
        name="pack",
    )
    far = shifted(blocks, -2)
    above = shifted(low, -1)
    below = shifted(high, 1)
    edge_latent, part = call(
        embed_kernel,
        [((K, nodes, features), BF16), ((K, nodes, features), BF16)],
        [edge_geometry, w_geometry, w_edge_in[:features]],
        scratch=[pltpu.VMEM((K * nodes, 128), F32)],
        flops=2 * K * nodes * features * features,
        bytes_accessed=8 << 20,
        name="embed",
    )
    grid_row = grid_node.reshape(1, n_points)
    latent, coupled, placed = call(
        latent_kernel,
        [((nodes, features), BF16), ((n_points, channels), BF16), ((1, W * rows), jnp.int32)],
        [
            intersection_counts, far, above, blocks, below, intersection_points[0], atmosphere,
            w_encode, grid_row, mesh_state,
        ],
        smem=1,
        name="latents",
    )
    latent_low = shifted(latent, 1)
    latent_high = shifted(latent, -1)
    pre, base = call(
        own_kernel,
        [((K, nodes, features), BF16), ((nodes, features), F32)],
        [latent, w_edge_in, part, edge_latent, neighbours],
        scratch=[pltpu.VMEM((nodes, features), BF16)],
        flops=2 * K * nodes * nodes * features,
        bytes_accessed=10 << 20,
        name="own",
    )
    wide = (columns + 2 * EDGE, levels, rows)
    ready = call(
        ready_kernel,
        [(wide, F32)] * 7,
        [ocean_heat_field, east_velocity, north_velocity, ocean_mask, below, above],
        bytes_accessed=4 << 20,
        name="ready",
    )
    state, flux = call(
        mesh_kernel,
        [((n_points, channels), BF16), (few, BF16)],
        [
            latent_low, latent_high, latent, w_edge_in, w_edge_out, pre, base, neighbours,
            w_node_in, w_node_out, w_decode, gain_edge.reshape(1, features),
            gain_node.reshape(1, features), grid_row, coupled, placed,
        ],
        scratch=[pltpu.VMEM((2 * nodes, features), BF16), pltpu.VMEM((nodes, features), F32)],
        flops=2 * K * nodes * 3 * nodes * features,
        bytes_accessed=10 << 20,
        name="mesh",
    )
    arrived = [flux if d == 0 else shifted(flux, d) for d in (3, 2, 1, 0, -1, -2)]
    (ocean_new,) = call(
        ocean_kernel,
        [((levels, columns, rows), F32)],
        [*arrived, *ready],
        bytes_accessed=4 << 20,
        name="ocean",
    )
    return (state, ocean_new)


def solution(mesh):
    ranges = ("member", "tile", "comp")
    placed = (
        P(ranges, None),
        P(ranges, None),
        P(None, ranges),
        P(ranges, None),
        P(ranges),
        P(None, ranges, None),
        P(None, ranges, None),
        P(None, ranges, None),
        P(ranges, None),
        P(ranges, None, None),
        P(ranges, None),
        P(),
        P(),
        P(),
        P(),
        P(),
        P(),
        P(),
        P(),
        P(),
    )
    return jax.shard_map(
        body,
        mesh=mesh,
        in_specs=placed,
        out_specs=(P(ranges, None), P(None, ranges, None)),
        check_vma=False,
    )
```

```python
import jax
import jax.numpy as jnp
from jax import lax
from jax.experimental import pallas as pl
from jax.experimental.pallas import tpu as pltpu
from jax.sharding import PartitionSpec as P

K = 8
STEPS = 4
W = 4
EDGE = 4

COEFF_H = 0.15
COEFF_V = 0.1
COEFF_Q = 0.5
EPSILON = 1e-05

F32 = jnp.float32
BF16 = jnp.bfloat16
AXES = ("tile", "comp")


def shifted(block, distance):
    count = lax.axis_size(AXES)
    return lax.ppermute(block, AXES, [((i - distance) % count, i) for i in range(count)])


def dot(a, b):
    return jnp.dot(a, b, preferred_element_type=F32)


def dot_nt(a, b):
    return lax.dot_general(a, b, (((1,), (1,)), ((), ())), preferred_element_type=F32)


def silu(v):
    return 0.5 * v * (1.0 + jnp.tanh(0.5 * v))


def one_hot(test):
    return jnp.where(test, 1.0, 0.0).astype(BF16)


def iota(shape, dim):
    return lax.broadcasted_iota(jnp.int32, shape, dim)


def started(pairs, sems):
    copies = [pltpu.make_async_copy(a, b, sems.at[i]) for i, (a, b) in enumerate(pairs)]
    for copy in copies:
        copy.start()
    return copies


def pack_kernel(
    counts_in, heat_in, east_in, north_in, mask_in, low_out, high_out, blocks_out,
    counts, heat, east, north, mask, sems,
):
    copies = started(
        ((counts_in, counts), (heat_in, heat), (mask_in, mask), (east_in, east), (north_in, north)), sems
    )
    for copy in copies:
        copy.wait()
    columns, rows = mask.shape
    wet = mask[...].astype(F32)
    triples = columns // 3

    def over_columns(x):
        return jnp.concatenate([x[3 * t] + x[3 * t + 1] + x[3 * t + 2] for t in range(triples)], axis=0)

    wet_rows = [wet[c : c + 1] for c in range(columns)]
    sums = over_columns([heat[c, 0:1] * wet_rows[c] for c in range(columns)])
    first = sums.astype(BF16).astype(F32)
    second = (sums - first).astype(BF16).astype(F32)
    third = sums - first - second
    parts = jnp.concatenate(
        [first, second, third, over_columns(wet_rows), jnp.zeros((16 - 4 * triples, rows), F32)], axis=0
    ).astype(BF16)
    pick = one_hot(iota((rows, rows // 3), 0) // 3 == iota((rows, rows // 3), 1))
    folded = dot(parts, pick)

    def flat(x):
        return jnp.concatenate([x[t : t + 1] for t in range(triples)], axis=1)

    t = triples
    total = flat(folded[:t] + folded[t : 2 * t] + folded[2 * t : 3 * t])
    number = flat(folded[3 * t : 4 * t])
    mean = total / jnp.maximum(number, 1.0)
    mean_high = mean.astype(BF16).astype(F32)
    flags = jnp.where(number > 0.5, 1.0, 0.0)
    lane = iota((1, rows), 1)
    held = jnp.zeros((1, rows), F32)
    for o in range(W):
        held = jnp.where(lane == o, counts[0, o].astype(F32), held)
    bundle = jnp.concatenate(
        [mean_high, mean - mean_high, flags, held, jnp.zeros((4, rows), F32)], axis=0
    )
    blank = jnp.zeros((4, rows), F32)
    for out, begin in ((low_out, 0), (high_out, columns - EDGE)):
        pieces = [source[c] for source in (heat, east, north) for c in range(begin, begin + EDGE)]
        pieces += [wet[begin : begin + EDGE], blank, bundle]
        out[...] = jnp.concatenate(pieces, axis=0).astype(BF16)
    blocks_out[...] = jnp.concatenate([bundle, jnp.zeros((8, rows), F32)], axis=0).astype(BF16)


def members(nodes, grid_row):
    return one_hot(iota((nodes, grid_row.shape[1]), 0) == grid_row)


def embed_kernel(
    geometry_in, w_geometry_in, w_in_in, atmosphere_in, w_encode_in, grid_row_in, mesh_state_in,
    latent_out, part_out, plain_out,
    turned, geometry, w_geometry, weights, atmosphere, w_encode, grid_row, mesh_state, sems,
):
    first = w_in_in.at[pl.ds(0, weights.shape[0])]
    copies = started(
        (
            (geometry_in, geometry),
            (w_geometry_in, w_geometry),
            (grid_row_in, grid_row),
            (atmosphere_in, atmosphere),
            (w_encode_in, w_encode),
            (mesh_state_in, mesh_state),
            (first, weights),
        ),
        sems,
    )
    for copy in copies:
        copy.wait()
    edges = geometry.shape[1]
    nodes = edges // K
    features = w_geometry.shape[1]
    flat = jnp.concatenate([geometry[...].astype(F32), jnp.zeros((4, edges), F32)], axis=0)
    turned[:, :8] = flat.T
    member = members(nodes, grid_row[...])
    population = jnp.sum(member.astype(F32), axis=1, keepdims=True)
    state = atmosphere[...]
    state = jnp.where(iota(state.shape, 0) == 0, 0.0, state.astype(F32)).astype(BF16)
    pooled = dot_nt(member, state) / jnp.maximum(population, 1.0)
    pooled_high = pooled.astype(BF16)
    pooled_low = (pooled - pooled_high.astype(F32)).astype(BF16)
    encode = w_encode[...]
    plain_out[...] = mesh_state[...].astype(F32) + dot(pooled_high, encode) + dot(pooled_low, encode)
    w_geo = jnp.concatenate([w_geometry[...].astype(F32), jnp.zeros((4, features), F32)], axis=0).astype(BF16)
    for k in range(K):
        points = turned[pl.ds(k, nodes, stride=K), :8].astype(BF16)
        value = silu(dot(points, w_geo)).astype(BF16)
        latent_out[k] = value
        part_out[k] = dot(value, weights[...]).astype(BF16)


def rolled_points(points, starts):
    rows = 2 * points.shape[1]
    empty = jnp.full((1, rows - points.shape[1]), 1 << 20, jnp.int32)
    return [
        pltpu.roll(jnp.concatenate([points[o : o + 1, :], empty], axis=1), starts[o], 1) for o in range(W)
    ]


def before(bundle_rows, o):
    lane = iota((1, bundle_rows.shape[1]), 1)
    return jnp.sum(jnp.where(lane < o, bundle_rows[3:4], 0.0)).astype(jnp.int32)


def latent_kernel(
    far, above, own, below, points, atmosphere, w_encode, grid_row, plain,
    latent_out, surface_out, placed_out,
):
    parts = [
        far[...].astype(F32)[:8],
        above[...].astype(F32)[-8:],
        own[...].astype(F32)[:8],
        below[...].astype(F32)[-8:],
    ]
    starts = [0, before(parts[1], 1), before(parts[2], 2), before(parts[3], 3)]
    placed = jnp.concatenate(rolled_points(points, starts), axis=1)
    placed_out[...] = placed
    n_points = grid_row.shape[1]
    values = jnp.concatenate(parts, axis=1).astype(BF16)
    match = one_hot(iota((n_points, placed.shape[1]), 0) == placed)
    sums = dot_nt(values, match)
    total = sums[0:1] + sums[1:2]
    number = sums[2:3]
    surface = jnp.where(
        number > 0.5, total / jnp.maximum(number, 1.0), atmosphere[0:16].astype(F32)[0:1]
    )
    surface_out[...] = surface
    pair = jnp.concatenate([surface, jnp.ones((7, n_points), F32)], axis=0).astype(BF16)
    pooled = dot_nt(members(plain.shape[0], grid_row[...]), pair)
    share = pooled[:, 0:1] / jnp.maximum(pooled[:, 1:2], 1.0)
    latent_out[...] = (plain[...] + share * w_encode[0:16].astype(F32)[0:1]).astype(BF16)


def listed_slots(neighbours):
    return neighbours[...].astype(F32).T


def slot_senders(listed, k):
    lane = iota(listed.shape, 1)
    return jnp.sum(jnp.where(lane == k, listed, 0.0), axis=1, keepdims=True).astype(jnp.int32)


def own_kernel(latent, w_in, part, edge_latent, neighbours, pre_out, base_out, sender):
    nodes, features = latent.shape
    value = latent[...]
    sender[...] = dot(value, w_in[features : 2 * features]).astype(BF16)
    receiver = dot(value, w_in[2 * features :])
    listed = listed_slots(neighbours)

    def step(k, base):
        at = slot_senders(listed, k)
        match = one_hot(iota((nodes, nodes), 1) + nodes == at)
        pre_out[k] = (part[k].astype(F32) + receiver + dot(match, sender[...])).astype(BF16)
        return base + jnp.where(at < 3 * nodes, edge_latent[k].astype(F32), 0.0)

    base_out[...] = lax.fori_loop(0, K, step, jnp.zeros((nodes, features), F32))


def normal(values):
    average = jnp.mean(values, axis=-1, keepdims=True)
    centred = values - average
    variance = jnp.mean(centred * centred, axis=-1, keepdims=True)
    return centred, lax.rsqrt(variance + EPSILON)


def mesh_kernel(
    low, high, latent, w_in, w_out, pre, base, neighbours, w_node_in, w_node_out, w_decode,
    gain_edge, gain_node, grid_row, atmosphere, surface, placed, state_out, flux_out, sender, total,
):
    nodes, features = latent.shape
    w_sender = w_in[features : 2 * features]
    sender[:nodes] = dot(low[...], w_sender).astype(BF16)
    sender[nodes:] = dot(high[...], w_sender).astype(BF16)
    listed = listed_slots(neighbours)
    total[...] = jnp.zeros((nodes, features), F32)

    def step(k, carry):
        at = slot_senders(listed, k)
        place = jnp.where(at < nodes, at, jnp.where(at >= 2 * nodes, at - nodes, -1))
        match = one_hot(iota((nodes, 2 * nodes), 1) == place)
        hidden = silu(pre[k].astype(F32) + dot(match, sender[...])).astype(BF16)
        centred, scale = normal(dot(hidden, w_out[...]))
        total[...] += centred * jnp.where(at < 3 * nodes, scale, 0.0)
        return carry

    lax.fori_loop(0, K, step, 0)
    aggregate = (base[...] + total[...] * gain_edge[...]).astype(BF16)
    own = latent[...]
    hidden = silu(dot(own, w_node_in[:features]) + dot(aggregate, w_node_in[features:])).astype(BF16)
    centred, scale = normal(dot(hidden, w_node_out[...]))
    node_new = (own.astype(F32) + centred * scale * gain_node[...]).astype(BF16)
    change = dot_nt(w_decode[...], node_new)
    change_high = change.astype(BF16)
    change_low = (change - change_high.astype(F32)).astype(BF16)
    member = members(nodes, grid_row[...])
    state = atmosphere[...].astype(F32)
    state = jnp.where(iota(state.shape, 0) == 0, surface[...].astype(BF16).astype(F32), state)
    state = state + dot(change_high, member) + dot(change_low, member)
    state_out[...] = state.astype(BF16)
    n_points = state.shape[1]
    flux = jnp.broadcast_to(state[1:2], (8, n_points)).astype(BF16)
    match = one_hot(iota((n_points, placed.shape[1]), 0) == placed[...])
    spread = dot(flux, match)
    rows = placed.shape[1] // W
    out = jnp.zeros((8, rows), F32)
    for o in range(W):
        out = jnp.where(iota((8, rows), 0) == o, spread[:, o * rows : (o + 1) * rows], out)
    flux_out[...] = jnp.concatenate([out, jnp.zeros((8, rows), F32)], axis=0).astype(BF16)


def ready_kernel(heat, east, north, mask, low, high, field_out, wet_out, px_out, qx_out, py_out, qy_out, mix_out):
    columns, rows = mask.shape
    levels = heat.shape[1]
    below, above = low[...].astype(F32), high[...].astype(F32)
    own_wet = mask[...].astype(F32)

    def wide(source, at):
        left = [below[8 * (at * EDGE + c) : 8 * (at * EDGE + c) + 8] for c in range(EDGE)]
        right = [above[8 * (at * EDGE + c) : 8 * (at * EDGE + c) + 8] for c in range(EDGE)]
        return left + [source[c] for c in range(columns)] + right

    base = 3 * 8 * EDGE
    wet = [below[base + c : base + c + 1] for c in range(EDGE)]
    wet += [own_wet[c : c + 1] for c in range(columns)]
    wet += [above[base + c : base + c + 1] for c in range(EDGE)]
    wet = [jnp.broadcast_to(w, (levels, rows)) for w in wet]
    field, u, v = wide(heat, 0), wide(east, 1), wide(north, 2)
    lane = iota((levels, rows), 1)
    level = iota((levels, rows), 0)
    count = len(field)
    for c in range(count):
        field_out[c] = field[c]
        wet_out[c] = wet[c]
        mix_out[c] = jnp.where(level < levels - 1, COEFF_V * wet[c], 0.0)
        if c + 1 < count:
            opened = wet[c] * wet[c + 1]
            face = 0.25 * (u[c] + u[c + 1])
            px_out[c] = opened * (face + COEFF_H)
            qx_out[c] = opened * (face - COEFF_H)
        opened = jnp.where(lane < rows - 1, wet[c] * pltpu.roll(wet[c], rows - 1, 1), 0.0)
        face = 0.25 * (v[c] + pltpu.roll(v[c], rows - 1, 1))
        py_out[c] = opened * (face + COEFF_H)
        qy_out[c] = opened * (face - COEFF_H)


def ocean_kernel(f_m3, f_m2, f_m1, f_0, f_p1, f_p2, field_in, wet, px, qx, py, qy, mix, out):
    count, levels, rows = field_in.shape
    columns = count - 2 * EDGE
    triples = columns // 3
    span = rows // 3
    fluxes = [f[...].astype(F32) for f in (f_m3, f_m2, f_m1, f_0, f_p1, f_p2)]

    def gathered(begin):
        return sum(fluxes[begin + o][o : o + 1] for o in range(W))

    own = gathered(1)
    blocks = [gathered(0)[:, (triples - 1) * span :]]
    blocks += [own[:, t * span : (t + 1) * span] for t in range(triples)]
    blocks += [gathered(2)[:, :span]]
    blocks += [jnp.zeros((16 - len(blocks), span), F32)]
    expand = one_hot(iota((span, rows), 1) // 3 == iota((span, rows), 0))
    cells = COEFF_Q * dot(jnp.concatenate(blocks, axis=0).astype(BF16), expand)
    level = iota((levels, rows), 0)
    surface = [
        jnp.where(level == 0, jnp.broadcast_to(cells[t : t + 1], (levels, rows)), 0.0)
        for t in range(triples + 2)
    ]
    field = [field_in[c] for c in range(count)]
    for step in range(STEPS):
        begin, end = step + 1, count - step - 1
        across = {c: px[c] * field[c] + qx[c] * field[c + 1] for c in range(begin - 1, end)}
        later = [None] * count
        for c in range(begin, end):
            here = field[c]
            along = py[c] * here + qy[c] * pltpu.roll(here, rows - 1, 1)
            mixed = mix[c] * (pltpu.roll(here, levels - 1, 0) - here)
            group = (c - EDGE + 3) // 3
            change = (
                (across[c - 1] - across[c])
                + (pltpu.roll(along, 1, 1) - along)
                + (mixed - pltpu.roll(mixed, 1, 0))
            )
            later[c] = wet[c] * (here + change + surface[group])
        field = later
    for c in range(columns):
        out[c] = field[EDGE + c]


VMEM = pl.BlockSpec(memory_space=pltpu.VMEM)
HBM = pl.BlockSpec(memory_space=pltpu.HBM)


def call(kernel, outs, inputs, spec=VMEM, scratch=(), flops=0, bytes_accessed=1 << 20, name=None):
    if spec is HBM:
        inputs = [pltpu.with_memory_space_constraint(x, pltpu.HBM) for x in inputs]
    return pl.pallas_call(
        kernel,
        out_shape=[jax.ShapeDtypeStruct(s, t) for s, t in outs],
        in_specs=[spec] * len(inputs),
        out_specs=[VMEM] * len(outs),
        scratch_shapes=list(scratch),
        compiler_params=pltpu.CompilerParams(vmem_limit_bytes=40 << 20),
        cost_estimate=pl.CostEstimate(flops=flops, bytes_accessed=bytes_accessed, transcendentals=0),
        name=name,
    )(*inputs)


def body(
    atmosphere,
    mesh_state,
    edge_geometry,
    neighbours,
    grid_node,
    ocean_heat_field,
    east_velocity,
    north_velocity,
    ocean_mask,
    intersection_points,
    intersection_counts,
    w_geometry,
    w_encode,
    w_edge_in,
    w_edge_out,
    w_node_in,
    w_node_out,
    w_decode,
    gain_edge,
    gain_node,
):
    levels, columns, rows = ocean_heat_field.shape
    nodes, features = mesh_state.shape
    n_points, channels = atmosphere.shape
    heat, east, north = (
        x.transpose(1, 0, 2) for x in (ocean_heat_field, east_velocity, north_velocity)
    )
    atmosphere_t = atmosphere.T
    slots = neighbours.T
    grid_row = grid_node.reshape(1, n_points)
    ends = (3 * levels * EDGE + 16, rows)
    few = (16, rows)
    own_ocean = (columns, levels, rows)
    low, high, blocks = call(
        pack_kernel,
        [(ends, BF16), (ends, BF16), (few, BF16)],
        [intersection_counts, heat, east, north, ocean_mask],
        spec=HBM,
        scratch=[
            pltpu.SMEM((1, W), jnp.int32),
            pltpu.VMEM(own_ocean, F32),
            pltpu.VMEM(own_ocean, F32),
            pltpu.VMEM(own_ocean, F32),
            pltpu.VMEM((columns, rows), jnp.int32),
            pltpu.SemaphoreType.DMA((5,)),
        ],
        name="pack",
    )
    far = shifted(blocks, -2)
    above = shifted(low, -1)
    below = shifted(high, 1)
    edge_latent, part, plain = call(
        embed_kernel,
        [((K, nodes, features), BF16), ((K, nodes, features), BF16), ((nodes, features), F32)],
        [edge_geometry, w_geometry, w_edge_in, atmosphere_t, w_encode, grid_row, mesh_state],
        spec=HBM,
        scratch=[
            pltpu.VMEM((K * nodes, 128), F32),
            pltpu.VMEM(edge_geometry.shape, BF16),
            pltpu.VMEM(w_geometry.shape, BF16),
            pltpu.VMEM((features, features), BF16),
            pltpu.VMEM((channels, n_points), BF16),
            pltpu.VMEM(w_encode.shape, BF16),
            pltpu.VMEM((1, n_points), jnp.int32),
            pltpu.VMEM((nodes, features), BF16),
            pltpu.SemaphoreType.DMA((7,)),
        ],
        flops=2 * K * nodes * features * features,
        bytes_accessed=8 << 20,
        name="embed",
    )
    latent, surface, placed = call(
        latent_kernel,
        [((nodes, features), BF16), ((1, n_points), F32), ((1, W * rows), jnp.int32)],
        [far, above, blocks, below, intersection_points[0], atmosphere_t, w_encode, grid_row, plain],
        name="latents",
    )
    latent_low = shifted(latent, 1)
    latent_high = shifted(latent, -1)
    pre, base = call(
        own_kernel,
        [((K, nodes, features), BF16), ((nodes, features), F32)],
        [latent, w_edge_in, part, edge_latent, slots],
        scratch=[pltpu.VMEM((nodes, features), BF16)],
        flops=2 * K * nodes * nodes * features,
        bytes_accessed=10 << 20,
        name="own",
    )
    wide = (columns + 2 * EDGE, levels, rows)
    ready = call(
        ready_kernel,
        [(wide, F32)] * 7,
        [heat, east, north, ocean_mask, below, above],
        bytes_accessed=4 << 20,
        name="ready",
    )
    state, flux = call(
        mesh_kernel,
        [((channels, n_points), BF16), (few, BF16)],
        [
            latent_low, latent_high, latent, w_edge_in, w_edge_out, pre, base, slots,
            w_node_in, w_node_out, w_decode.T, gain_edge.reshape(1, features),
            gain_node.reshape(1, features), grid_row, atmosphere_t, surface, placed,
        ],
        scratch=[pltpu.VMEM((2 * nodes, features), BF16), pltpu.VMEM((nodes, features), F32)],
        flops=2 * K * nodes * 3 * nodes * features,
        bytes_accessed=10 << 20,
        name="mesh",
    )
    arrived = [flux if d == 0 else shifted(flux, d) for d in (3, 2, 1, 0, -1, -2)]
    (ocean_new,) = call(
        ocean_kernel,
        [(own_ocean, F32)],
        [*arrived, *ready],
        bytes_accessed=4 << 20,
        name="ocean",
    )
    return (state.T, ocean_new.transpose(1, 0, 2))


def solution(mesh):
    ranges = ("member", "tile", "comp")
    placed = (
        P(ranges, None),
        P(ranges, None),
        P(None, ranges),
        P(ranges, None),
        P(ranges),
        P(None, ranges, None),
        P(None, ranges, None),
        P(None, ranges, None),
        P(ranges, None),
        P(ranges, None, None),
        P(ranges, None),
        P(),
        P(),
        P(),
        P(),
        P(),
        P(),
        P(),
        P(),
        P(),
    )
    return jax.shard_map(
        body,
        mesh=mesh,
        in_specs=placed,
        out_specs=(P(ranges, None), P(None, ranges, None)),
        check_vma=False,
    )
```

```python
import jax
import jax.numpy as jnp
from jax import lax
from jax.experimental import pallas as pl
from jax.experimental.pallas import tpu as pltpu
from jax.sharding import PartitionSpec as P

K = 8
STEPS = 4
W = 4
EDGE = 4

COEFF_H = 0.15
COEFF_V = 0.1
COEFF_Q = 0.5
EPSILON = 1e-05

F32 = jnp.float32
BF16 = jnp.bfloat16
AXES = ("tile", "comp")


def shifted(block, distance):
    count = lax.axis_size(AXES)
    return lax.ppermute(block, AXES, [((i - distance) % count, i) for i in range(count)])


def dot(a, b):
    return jnp.dot(a, b, preferred_element_type=F32)


def dot_nt(a, b):
    return lax.dot_general(a, b, (((1,), (1,)), ((), ())), preferred_element_type=F32)


def silu(v):
    return 0.5 * v * (1.0 + jnp.tanh(0.5 * v))


def one_hot(test):
    return jnp.where(test, 1.0, 0.0).astype(BF16)


def iota(shape, dim):
    return lax.broadcasted_iota(jnp.int32, shape, dim)


def started(pairs, sems):
    copies = [pltpu.make_async_copy(a, b, sems.at[i]) for i, (a, b) in enumerate(pairs)]
    for copy in copies:
        copy.start()
    return copies


def pack_kernel(
    counts_in, heat_in, east_in, north_in, mask_in, low_out, high_out, blocks_out,
    counts, heat, east, north, mask, sems,
):
    copies = started(
        ((counts_in, counts), (heat_in, heat), (mask_in, mask), (east_in, east), (north_in, north)), sems
    )
    for copy in copies:
        copy.wait()
    columns, rows = mask.shape
    wet = mask[...].astype(F32)
    triples = columns // 3

    def over_columns(x):
        return jnp.concatenate([x[3 * t] + x[3 * t + 1] + x[3 * t + 2] for t in range(triples)], axis=0)

    wet_rows = [wet[c : c + 1] for c in range(columns)]
    sums = over_columns([heat[c, 0:1] * wet_rows[c] for c in range(columns)])
    first = sums.astype(BF16).astype(F32)
    second = (sums - first).astype(BF16).astype(F32)
    third = sums - first - second
    parts = jnp.concatenate(
        [first, second, third, over_columns(wet_rows), jnp.zeros((16 - 4 * triples, rows), F32)], axis=0
    ).astype(BF16)
    pick = one_hot(iota((rows, rows // 3), 0) // 3 == iota((rows, rows // 3), 1))
    folded = dot(parts, pick)

    def flat(x):
        return jnp.concatenate([x[t : t + 1] for t in range(triples)], axis=1)

    t = triples
    total = flat(folded[:t] + folded[t : 2 * t] + folded[2 * t : 3 * t])
    number = flat(folded[3 * t : 4 * t])
    mean = total / jnp.maximum(number, 1.0)
    mean_high = mean.astype(BF16).astype(F32)
    flags = jnp.where(number > 0.5, 1.0, 0.0)
    lane = iota((1, rows), 1)
    held = jnp.zeros((1, rows), F32)
    for o in range(W):
        held = jnp.where(lane == o, counts[0, o].astype(F32), held)
    bundle = jnp.concatenate(
        [mean_high, mean - mean_high, flags, held, jnp.zeros((4, rows), F32)], axis=0
    )
    blank = jnp.zeros((4, rows), F32)
    for out, begin in ((low_out, 0), (high_out, columns - EDGE)):
        pieces = [source[c] for source in (heat, east, north) for c in range(begin, begin + EDGE)]
        pieces += [wet[begin : begin + EDGE], blank, bundle]
        out[...] = jnp.concatenate(pieces, axis=0).astype(BF16)
    blocks_out[...] = jnp.concatenate([bundle, jnp.zeros((8, rows), F32)], axis=0).astype(BF16)


def members(nodes, grid_row):
    return one_hot(iota((nodes, grid_row.shape[1]), 0) == grid_row)


def embed_kernel(
    geometry_in, w_geometry_in, atmosphere_in, w_encode_in, grid_row_in, mesh_state_in,
    latent_out, plain_out,
    turned, geometry, w_geometry, atmosphere, w_encode, grid_row, mesh_state, sems,
):
    copies = started(
        (
            (geometry_in, geometry),
            (w_geometry_in, w_geometry),
            (grid_row_in, grid_row),
            (atmosphere_in, atmosphere),
            (w_encode_in, w_encode),
            (mesh_state_in, mesh_state),
        ),
        sems,
    )
    for copy in copies:
        copy.wait()
    edges = geometry.shape[1]
    nodes = edges // K
    features = w_geometry.shape[1]
    flat = jnp.concatenate([geometry[...].astype(F32), jnp.zeros((4, edges), F32)], axis=0)
    turned[:, :8] = flat.T
    member = members(nodes, grid_row[...])
    population = jnp.sum(member.astype(F32), axis=1, keepdims=True)
    state = atmosphere[...]
    state = jnp.where(iota(state.shape, 0) == 0, 0.0, state.astype(F32)).astype(BF16)
    pooled = dot_nt(member, state) / jnp.maximum(population, 1.0)
    pooled_high = pooled.astype(BF16)
    pooled_low = (pooled - pooled_high.astype(F32)).astype(BF16)
    encode = w_encode[...]
    plain_out[...] = mesh_state[...].astype(F32) + dot(pooled_high, encode) + dot(pooled_low, encode)
    w_geo = jnp.concatenate([w_geometry[...].astype(F32), jnp.zeros((4, features), F32)], axis=0).astype(BF16)
    for k in range(K):
        points = turned[pl.ds(k, nodes, stride=K), :8].astype(BF16)
        latent_out[k] = silu(dot(points, w_geo)).astype(BF16)


def rolled_points(points, starts):
    rows = 2 * points.shape[1]
    empty = jnp.full((1, rows - points.shape[1]), 1 << 20, jnp.int32)
    return [
        pltpu.roll(jnp.concatenate([points[o : o + 1, :], empty], axis=1), starts[o], 1) for o in range(W)
    ]


def before(bundle_rows, o):
    lane = iota((1, bundle_rows.shape[1]), 1)
    return jnp.sum(jnp.where(lane < o, bundle_rows[3:4], 0.0)).astype(jnp.int32)


def latent_kernel(
    far, above, own, below, points, atmosphere, w_encode, grid_row, plain,
    latent_out, surface_out, placed_out,
):
    parts = [
        far[...].astype(F32)[:8],
        above[...].astype(F32)[-8:],
        own[...].astype(F32)[:8],
        below[...].astype(F32)[-8:],
    ]
    starts = [0, before(parts[1], 1), before(parts[2], 2), before(parts[3], 3)]
    placed = jnp.concatenate(rolled_points(points, starts), axis=1)
    placed_out[...] = placed
    n_points = grid_row.shape[1]
    values = jnp.concatenate(parts, axis=1).astype(BF16)
    match = one_hot(iota((n_points, placed.shape[1]), 0) == placed)
    sums = dot_nt(values, match)
    total = sums[0:1] + sums[1:2]
    number = sums[2:3]
    surface = jnp.where(
        number > 0.5, total / jnp.maximum(number, 1.0), atmosphere[0:16].astype(F32)[0:1]
    )
    surface_out[...] = surface
    pair = jnp.concatenate([surface, jnp.ones((7, n_points), F32)], axis=0).astype(BF16)
    pooled = dot_nt(members(plain.shape[0], grid_row[...]), pair)
    share = pooled[:, 0:1] / jnp.maximum(pooled[:, 1:2], 1.0)
    latent_out[...] = (plain[...] + share * w_encode[0:16].astype(F32)[0:1]).astype(BF16)


def listed_slots(neighbours):
    return neighbours[...].astype(F32).T


def slot_senders(listed, k):
    lane = iota(listed.shape, 1)
    return jnp.sum(jnp.where(lane == k, listed, 0.0), axis=1, keepdims=True).astype(jnp.int32)


def own_kernel(latent, w_in, edge_latent, neighbours, w_node_in, pre_out, base_out, node_out, sender):
    nodes, features = latent.shape
    value = latent[...]
    sender[...] = dot(value, w_in[features : 2 * features]).astype(BF16)
    receiver = dot(value, w_in[2 * features :])
    node_out[...] = dot(value, w_node_in[:features])
    listed = listed_slots(neighbours)

    def step(k, base):
        at = slot_senders(listed, k)
        edge = edge_latent[k]
        match = one_hot(iota((nodes, nodes), 1) + nodes == at)
        joined = dot(edge, w_in[:features]) + dot(match, sender[...])
        pre_out[k] = (joined + receiver).astype(BF16)
        return base + jnp.where(at < 3 * nodes, edge.astype(F32), 0.0)

    base_out[...] = lax.fori_loop(0, K, step, jnp.zeros((nodes, features), F32), unroll=True)


def normal(values):
    average = jnp.mean(values, axis=-1, keepdims=True)
    centred = values - average
    variance = jnp.mean(centred * centred, axis=-1, keepdims=True)
    return centred, lax.rsqrt(variance + EPSILON)


def mesh_kernel(
    low, high, latent, w_in, w_out, pre, base, node_part, neighbours, w_node_in, w_node_out, w_decode,
    gain_edge, gain_node, grid_row, atmosphere, placed, node_out, flux_out, sender, total,
):
    nodes, features = latent.shape
    w_sender = w_in[features : 2 * features]
    sender[:nodes] = dot(low[...], w_sender).astype(BF16)
    sender[nodes:] = dot(high[...], w_sender).astype(BF16)
    listed = listed_slots(neighbours)
    total[...] = jnp.zeros((nodes, features), F32)

    def step(k, carry):
        at = slot_senders(listed, k)
        place = jnp.where(at < nodes, at, jnp.where(at >= 2 * nodes, at - nodes, -1))
        match = one_hot(iota((nodes, 2 * nodes), 1) == place)
        hidden = silu(pre[k].astype(F32) + dot(match, sender[...])).astype(BF16)
        centred, scale = normal(dot(hidden, w_out[...]))
        total[...] += centred * jnp.where(at < 3 * nodes, scale, 0.0)
        return carry

    lax.fori_loop(0, K, step, 0, unroll=True)
    aggregate = (base[...] + total[...] * gain_edge[...]).astype(BF16)
    hidden = silu(node_part[...] + dot(aggregate, w_node_in[features:])).astype(BF16)
    centred, scale = normal(dot(hidden, w_node_out[...]))
    node_new = (latent[...].astype(F32) + centred * scale * gain_node[...]).astype(BF16)
    node_out[...] = node_new
    flux = two_parts(dot_nt(w_decode[0:16], node_new)[1:2])
    flux = dot(flux, members(nodes, grid_row[...]))
    flux = atmosphere[0:16].astype(F32)[1:2] + flux[0:1] + flux[1:2]
    n_points = flux.shape[1]
    match = one_hot(iota((n_points, placed.shape[1]), 0) == placed[...])
    spread = dot(jnp.broadcast_to(flux, (8, n_points)).astype(BF16), match)
    rows = placed.shape[1] // W
    out = jnp.zeros((8, rows), F32)
    for o in range(W):
        out = jnp.where(iota((8, rows), 0) == o, spread[:, o * rows : (o + 1) * rows], out)
    flux_out[...] = jnp.concatenate([out, jnp.zeros((8, rows), F32)], axis=0).astype(BF16)


def two_parts(row):
    high = row.astype(BF16).astype(F32)
    return jnp.concatenate([high, row - high, jnp.zeros((6, row.shape[1]), F32)], axis=0).astype(BF16)


def decode_kernel(node_new, w_decode, grid_row, atmosphere, surface, state_out):
    change = dot_nt(w_decode[...], node_new[...])
    change_high = change.astype(BF16)
    change_low = (change - change_high.astype(F32)).astype(BF16)
    member = members(node_new.shape[0], grid_row[...])
    state = atmosphere[...].astype(F32)
    state = jnp.where(iota(state.shape, 0) == 0, surface[...].astype(BF16).astype(F32), state)
    state_out[...] = (state + dot(change_high, member) + dot(change_low, member)).astype(BF16)


def ready_kernel(heat, east, north, mask, low, high, field_out, wet_out, px_out, qx_out, py_out, qy_out, mix_out):
    columns, rows = mask.shape
    levels = heat.shape[1]
    below, above = low[...].astype(F32), high[...].astype(F32)
    own_wet = mask[...].astype(F32)

    def wide(source, at):
        left = [below[8 * (at * EDGE + c) : 8 * (at * EDGE + c) + 8] for c in range(EDGE)]
        right = [above[8 * (at * EDGE + c) : 8 * (at * EDGE + c) + 8] for c in range(EDGE)]
        return left + [source[c] for c in range(columns)] + right

    base = 3 * 8 * EDGE
    wet = [below[base + c : base + c + 1] for c in range(EDGE)]
    wet += [own_wet[c : c + 1] for c in range(columns)]
    wet += [above[base + c : base + c + 1] for c in range(EDGE)]
    wet = [jnp.broadcast_to(w, (levels, rows)) for w in wet]
    field, u, v = wide(heat, 0), wide(east, 1), wide(north, 2)
    lane = iota((levels, rows), 1)
    level = iota((levels, rows), 0)
    count = len(field)
    for c in range(count):
        field_out[c] = field[c]
        wet_out[c] = wet[c]
        mix_out[c] = jnp.where(level < levels - 1, COEFF_V * wet[c], 0.0)
        if c + 1 < count:
            opened = wet[c] * wet[c + 1]
            face = 0.25 * (u[c] + u[c + 1])
            px_out[c] = opened * (face + COEFF_H)
            qx_out[c] = opened * (face - COEFF_H)
        opened = jnp.where(lane < rows - 1, wet[c] * pltpu.roll(wet[c], rows - 1, 1), 0.0)
        face = 0.25 * (v[c] + pltpu.roll(v[c], rows - 1, 1))
        py_out[c] = opened * (face + COEFF_H)
        qy_out[c] = opened * (face - COEFF_H)


def ocean_kernel(f_p1, f_p2, f_m3, f_m2, f_m1, f_0, field_in, wet, px, qx, py, qy, mix, out):
    count, levels, rows = field_in.shape
    columns = count - 2 * EDGE
    triples = columns // 3
    span = rows // 3
    fluxes = [f[...].astype(F32) for f in (f_m3, f_m2, f_m1, f_0, f_p1, f_p2)]

    def gathered(begin):
        return sum(fluxes[begin + o][o : o + 1] for o in range(W))

    own = gathered(1)
    blocks = [gathered(0)[:, (triples - 1) * span :]]
    blocks += [own[:, t * span : (t + 1) * span] for t in range(triples)]
    blocks += [gathered(2)[:, :span]]
    blocks += [jnp.zeros((16 - len(blocks), span), F32)]
    expand = one_hot(iota((span, rows), 1) // 3 == iota((span, rows), 0))
    cells = COEFF_Q * dot(jnp.concatenate(blocks, axis=0).astype(BF16), expand)
    level = iota((levels, rows), 0)
    surface = [
        jnp.where(level == 0, jnp.broadcast_to(cells[t : t + 1], (levels, rows)), 0.0)
        for t in range(triples + 2)
    ]
    field = [field_in[c] for c in range(count)]
    for step in range(STEPS):
        begin, end = step + 1, count - step - 1
        across = {c: px[c] * field[c] + qx[c] * field[c + 1] for c in range(begin - 1, end)}
        later = [None] * count
        for c in range(begin, end):
            here = field[c]
            along = py[c] * here + qy[c] * pltpu.roll(here, rows - 1, 1)
            mixed = mix[c] * (pltpu.roll(here, levels - 1, 0) - here)
            group = (c - EDGE + 3) // 3
            change = (
                (across[c - 1] - across[c])
                + (pltpu.roll(along, 1, 1) - along)
                + (mixed - pltpu.roll(mixed, 1, 0))
            )
            later[c] = wet[c] * (here + change + surface[group])
        field = later
    for c in range(columns):
        out[c] = field[EDGE + c]


VMEM = pl.BlockSpec(memory_space=pltpu.VMEM)
HBM = pl.BlockSpec(memory_space=pltpu.HBM)


def call(kernel, outs, inputs, spec=VMEM, scratch=(), flops=0, bytes_accessed=1 << 20, name=None):
    if spec is HBM:
        inputs = [pltpu.with_memory_space_constraint(x, pltpu.HBM) for x in inputs]
    return pl.pallas_call(
        kernel,
        out_shape=[jax.ShapeDtypeStruct(s, t) for s, t in outs],
        in_specs=[spec] * len(inputs),
        out_specs=[VMEM] * len(outs),
        scratch_shapes=list(scratch),
        compiler_params=pltpu.CompilerParams(vmem_limit_bytes=40 << 20),
        cost_estimate=pl.CostEstimate(flops=flops, bytes_accessed=bytes_accessed, transcendentals=0),
        name=name,
    )(*inputs)


def body(
    atmosphere,
    mesh_state,
    edge_geometry,
    neighbours,
    grid_node,
    ocean_heat_field,
    east_velocity,
    north_velocity,
    ocean_mask,
    intersection_points,
    intersection_counts,
    w_geometry,
    w_encode,
    w_edge_in,
    w_edge_out,
    w_node_in,
    w_node_out,
    w_decode,
    gain_edge,
    gain_node,
):
    levels, columns, rows = ocean_heat_field.shape
    nodes, features = mesh_state.shape
    n_points, channels = atmosphere.shape
    heat, east, north = (
        x.transpose(1, 0, 2) for x in (ocean_heat_field, east_velocity, north_velocity)
    )
    atmosphere_t = atmosphere.T
    slots = neighbours.T
    grid_row = grid_node.reshape(1, n_points)
    decode_t = w_decode.T
    ends = (3 * levels * EDGE + 16, rows)
    few = (16, rows)
    own_ocean = (columns, levels, rows)
    low, high, blocks = call(
        pack_kernel,
        [(ends, BF16), (ends, BF16), (few, BF16)],
        [intersection_counts, heat, east, north, ocean_mask],
        spec=HBM,
        scratch=[
            pltpu.SMEM((1, W), jnp.int32),
            pltpu.VMEM(own_ocean, F32),
            pltpu.VMEM(own_ocean, F32),
            pltpu.VMEM(own_ocean, F32),
            pltpu.VMEM((columns, rows), jnp.int32),
            pltpu.SemaphoreType.DMA((5,)),
        ],
        name="pack",
    )
    far = shifted(blocks, -2)
    above = shifted(low, -1)
    below = shifted(high, 1)
    edge_latent, plain = call(
        embed_kernel,
        [((K, nodes, features), BF16), ((nodes, features), F32)],
        [edge_geometry, w_geometry, atmosphere_t, w_encode, grid_row, mesh_state],
        spec=HBM,
        scratch=[
            pltpu.VMEM((K * nodes, 128), F32),
            pltpu.VMEM(edge_geometry.shape, BF16),
            pltpu.VMEM(w_geometry.shape, BF16),
            pltpu.VMEM((channels, n_points), BF16),
            pltpu.VMEM(w_encode.shape, BF16),
            pltpu.VMEM((1, n_points), jnp.int32),
            pltpu.VMEM((nodes, features), BF16),
            pltpu.SemaphoreType.DMA((6,)),
        ],
        flops=2 * K * nodes * features * features,
        bytes_accessed=8 << 20,
        name="embed",
    )
    latent, surface, placed = call(
        latent_kernel,
        [((nodes, features), BF16), ((1, n_points), F32), ((1, W * rows), jnp.int32)],
        [far, above, blocks, below, intersection_points[0], atmosphere_t, w_encode, grid_row, plain],
        name="latents",
    )
    latent_low = shifted(latent, 1)
    latent_high = shifted(latent, -1)
    pre, base, node_part = call(
        own_kernel,
        [((K, nodes, features), BF16), ((nodes, features), F32), ((nodes, features), F32)],
        [latent, w_edge_in, edge_latent, slots, w_node_in],
        scratch=[pltpu.VMEM((nodes, features), BF16)],
        flops=2 * K * nodes * (nodes + features) * features,
        bytes_accessed=10 << 20,
        name="own",
    )
    wide = (columns + 2 * EDGE, levels, rows)
    ready = call(
        ready_kernel,
        [(wide, F32)] * 7,
        [heat, east, north, ocean_mask, below, above],
        bytes_accessed=4 << 20,
        name="ready",
    )
    node_new, flux = call(
        mesh_kernel,
        [((nodes, features), BF16), (few, BF16)],
        [
            latent_low, latent_high, latent, w_edge_in, w_edge_out, pre, base, node_part, slots,
            w_node_in, w_node_out, decode_t, gain_edge.reshape(1, features),
            gain_node.reshape(1, features), grid_row, atmosphere_t, placed,
        ],
        scratch=[pltpu.VMEM((2 * nodes, features), BF16), pltpu.VMEM((nodes, features), F32)],
        flops=2 * K * nodes * 3 * nodes * features,
        bytes_accessed=10 << 20,
        name="mesh",
    )
    sent = {d: shifted(flux, d) for d in (1, 2, 3, -1, -2)}
    sent[0] = flux
    arrived = [sent[d] for d in (-1, -2, 3, 2, 1, 0)]
    (state,) = call(
        decode_kernel,
        [((channels, n_points), BF16)],
        [node_new, decode_t, grid_row, atmosphere_t, surface],
        flops=6 * nodes * channels * n_points,
        name="decode",
    )
    (ocean_new,) = call(
        ocean_kernel,
        [(own_ocean, F32)],
        [*arrived, *ready],
        bytes_accessed=4 << 20,
        name="ocean",
    )
    return (state.T, ocean_new.transpose(1, 0, 2))


def solution(mesh):
    ranges = ("member", "tile", "comp")
    placed = (
        P(ranges, None),
        P(ranges, None),
        P(None, ranges),
        P(ranges, None),
        P(ranges),
        P(None, ranges, None),
        P(None, ranges, None),
        P(None, ranges, None),
        P(ranges, None),
        P(ranges, None, None),
        P(ranges, None),
        P(),
        P(),
        P(),
        P(),
        P(),
        P(),
        P(),
        P(),
        P(),
    )
    return jax.shard_map(
        body,
        mesh=mesh,
        in_specs=placed,
        out_specs=(P(ranges, None), P(None, ranges, None)),
        check_vma=False,
    )
```

```python
import jax
import jax.numpy as jnp
from jax import lax
from jax.experimental import pallas as pl
from jax.experimental.pallas import tpu as pltpu
from jax.sharding import PartitionSpec as P

K = 8
STEPS = 4
W = 4
EDGE = 4

COEFF_H = 0.15
COEFF_V = 0.1
COEFF_Q = 0.5
EPSILON = 1e-05

F32 = jnp.float32
BF16 = jnp.bfloat16
AXES = ("tile", "comp")


def shifted(block, distance):
    count = lax.axis_size(AXES)
    return lax.ppermute(block, AXES, [((i - distance) % count, i) for i in range(count)])


def dot(a, b):
    return jnp.dot(a, b, preferred_element_type=F32)


def dot_nt(a, b):
    return lax.dot_general(a, b, (((1,), (1,)), ((), ())), preferred_element_type=F32)


def silu(v):
    return 0.5 * v * (1.0 + jnp.tanh(0.5 * v))


def one_hot(test):
    return jnp.where(test, 1.0, 0.0).astype(BF16)


def iota(shape, dim):
    return lax.broadcasted_iota(jnp.int32, shape, dim)


def started(pairs, sems):
    copies = [pltpu.make_async_copy(a, b, sems.at[i]) for i, (a, b) in enumerate(pairs)]
    for copy in copies:
        copy.start()
    return copies


def pack_kernel(
    counts_in, heat_in, east_in, north_in, mask_in, low_out, high_out, blocks_out,
    counts, heat, east, north, mask, sems,
):
    copies = started(
        ((counts_in, counts), (heat_in, heat), (mask_in, mask), (east_in, east), (north_in, north)), sems
    )
    for copy in copies:
        copy.wait()
    columns, rows = mask.shape
    wet = mask[...].astype(F32)
    triples = columns // 3

    def over_columns(x):
        return jnp.concatenate([x[3 * t] + x[3 * t + 1] + x[3 * t + 2] for t in range(triples)], axis=0)

    wet_rows = [wet[c : c + 1] for c in range(columns)]
    sums = over_columns([heat[c, 0:1] * wet_rows[c] for c in range(columns)])
    first = sums.astype(BF16).astype(F32)
    second = (sums - first).astype(BF16).astype(F32)
    third = sums - first - second
    parts = jnp.concatenate(
        [first, second, third, over_columns(wet_rows), jnp.zeros((16 - 4 * triples, rows), F32)], axis=0
    ).astype(BF16)
    pick = one_hot(iota((rows, rows // 3), 0) // 3 == iota((rows, rows // 3), 1))
    folded = dot(parts, pick)

    def flat(x):
        return jnp.concatenate([x[t : t + 1] for t in range(triples)], axis=1)

    t = triples
    total = flat(folded[:t] + folded[t : 2 * t] + folded[2 * t : 3 * t])
    number = flat(folded[3 * t : 4 * t])
    mean = total / jnp.maximum(number, 1.0)
    mean_high = mean.astype(BF16).astype(F32)
    flags = jnp.where(number > 0.5, 1.0, 0.0)
    lane = iota((1, rows), 1)
    held = jnp.zeros((1, rows), F32)
    for o in range(W):
        held = jnp.where(lane == o, counts[0, o].astype(F32), held)
    bundle = jnp.concatenate(
        [mean_high, mean - mean_high, flags, held, jnp.zeros((4, rows), F32)], axis=0
    )
    blank = jnp.zeros((4, rows), F32)
    for out, begin in ((low_out, 0), (high_out, columns - EDGE)):
        pieces = [source[c] for source in (heat, east, north) for c in range(begin, begin + EDGE)]
        pieces += [wet[begin : begin + EDGE], blank, bundle]
        out[...] = jnp.concatenate(pieces, axis=0).astype(BF16)
    blocks_out[...] = jnp.concatenate([bundle, jnp.zeros((8, rows), F32)], axis=0).astype(BF16)


def members(nodes, grid_row):
    return one_hot(iota((nodes, grid_row.shape[1]), 0) == grid_row)


def plain_kernel(
    atmosphere_in, w_encode_in, grid_row_in, mesh_state_in, plain_out,
    atmosphere, w_encode, grid_row, mesh_state, sems,
):
    copies = started(
        (
            (grid_row_in, grid_row),
            (atmosphere_in, atmosphere),
            (w_encode_in, w_encode),
            (mesh_state_in, mesh_state),
        ),
        sems,
    )
    for copy in copies:
        copy.wait()
    member = members(mesh_state.shape[0], grid_row[...])
    population = jnp.sum(member.astype(F32), axis=1, keepdims=True)
    state = atmosphere[...]
    state = jnp.where(iota(state.shape, 0) == 0, 0.0, state.astype(F32)).astype(BF16)
    pooled = dot_nt(member, state) / jnp.maximum(population, 1.0)
    pooled_high = pooled.astype(BF16)
    pooled_low = (pooled - pooled_high.astype(F32)).astype(BF16)
    encode = w_encode[...]
    plain_out[...] = mesh_state[...].astype(F32) + dot(pooled_high, encode) + dot(pooled_low, encode)


def rolled_points(points, starts):
    rows = 2 * points.shape[1]
    empty = jnp.full((1, rows - points.shape[1]), 1 << 20, jnp.int32)
    return [
        pltpu.roll(jnp.concatenate([points[o : o + 1, :], empty], axis=1), starts[o], 1) for o in range(W)
    ]


def before(bundle_rows, o):
    lane = iota((1, bundle_rows.shape[1]), 1)
    return jnp.sum(jnp.where(lane < o, bundle_rows[3:4], 0.0)).astype(jnp.int32)


def latent_kernel(
    below, above, far, own, points, atmosphere, w_encode, grid_row, plain,
    latent_out, surface_out, placed_out,
):
    parts = [
        far[...].astype(F32)[:8],
        above[...].astype(F32)[-8:],
        own[...].astype(F32)[:8],
        below[...].astype(F32)[-8:],
    ]
    starts = [0, before(parts[1], 1), before(parts[2], 2), before(parts[3], 3)]
    placed = jnp.concatenate(rolled_points(points, starts), axis=1)
    placed_out[...] = placed
    n_points = grid_row.shape[1]
    values = jnp.concatenate(parts, axis=1).astype(BF16)
    match = one_hot(iota((n_points, placed.shape[1]), 0) == placed)
    sums = dot_nt(values, match)
    total = sums[0:1] + sums[1:2]
    number = sums[2:3]
    surface = jnp.where(
        number > 0.5, total / jnp.maximum(number, 1.0), atmosphere[0:16].astype(F32)[0:1]
    )
    surface_out[...] = surface
    pair = jnp.concatenate([surface, jnp.ones((7, n_points), F32)], axis=0).astype(BF16)
    pooled = dot_nt(members(plain.shape[0], grid_row[...]), pair)
    share = pooled[:, 0:1] / jnp.maximum(pooled[:, 1:2], 1.0)
    latent_out[...] = (plain[...] + share * w_encode[0:16].astype(F32)[0:1]).astype(BF16)


def listed_slots(neighbours):
    return neighbours[...].astype(F32).T


def slot_senders(listed, k):
    lane = iota(listed.shape, 1)
    return jnp.sum(jnp.where(lane == k, listed, 0.0), axis=1, keepdims=True).astype(jnp.int32)


def own_kernel(
    latent, w_in, geometry, w_geometry, neighbours, w_node_in, pre_out, base_out, node_out, sender, turned,
):
    nodes, features = latent.shape
    value = latent[...]
    sender[...] = dot(value, w_in[features : 2 * features]).astype(BF16)
    receiver = dot(value, w_in[2 * features :])
    node_out[...] = dot(value, w_node_in[:features])
    listed = listed_slots(neighbours)
    blank = jnp.zeros((4, geometry.shape[1]), F32)
    turned[:, :8] = jnp.concatenate([geometry[...].astype(F32), blank], axis=0).T
    blank = jnp.zeros((4, features), F32)
    w_geo = jnp.concatenate([w_geometry[...].astype(F32), blank], axis=0).astype(BF16)
    base = jnp.zeros((nodes, features), F32)
    for k in range(K):
        at = slot_senders(listed, k)
        edge = silu(dot(turned[pl.ds(k, nodes, stride=K), :8].astype(BF16), w_geo)).astype(BF16)
        match = one_hot(iota((nodes, nodes), 1) + nodes == at)
        joined = dot(edge, w_in[:features]) + dot(match, sender[...])
        pre_out[k] = (joined + receiver).astype(BF16)
        base = base + jnp.where(at < 3 * nodes, edge.astype(F32), 0.0)
    base_out[...] = base


def normal(values):
    average = jnp.mean(values, axis=-1, keepdims=True)
    centred = values - average
    variance = jnp.mean(centred * centred, axis=-1, keepdims=True)
    return centred, lax.rsqrt(variance + EPSILON)


def mesh_kernel(
    low, high, latent, w_in, w_out, pre, base, node_part, neighbours, w_node_in, w_node_out, w_decode,
    gain_edge, gain_node, grid_row, atmosphere, placed, node_out, flux_out, sender, total,
):
    nodes, features = latent.shape
    w_sender = w_in[features : 2 * features]
    sender[:nodes] = dot(low[...], w_sender).astype(BF16)
    sender[nodes:] = dot(high[...], w_sender).astype(BF16)
    listed = listed_slots(neighbours)
    total[...] = jnp.zeros((nodes, features), F32)

    def step(k, carry):
        at = slot_senders(listed, k)
        place = jnp.where(at < nodes, at, jnp.where(at >= 2 * nodes, at - nodes, -1))
        match = one_hot(iota((nodes, 2 * nodes), 1) == place)
        hidden = silu(pre[k].astype(F32) + dot(match, sender[...])).astype(BF16)
        centred, scale = normal(dot(hidden, w_out[...]))
        total[...] += centred * jnp.where(at < 3 * nodes, scale, 0.0)
        return carry

    lax.fori_loop(0, K, step, 0, unroll=True)
    aggregate = (base[...] + total[...] * gain_edge[...]).astype(BF16)
    hidden = silu(node_part[...] + dot(aggregate, w_node_in[features:])).astype(BF16)
    centred, scale = normal(dot(hidden, w_node_out[...]))
    node_new = (latent[...].astype(F32) + centred * scale * gain_node[...]).astype(BF16)
    node_out[...] = node_new
    flux = two_parts(dot_nt(w_decode[0:16], node_new)[1:2])
    flux = dot(flux, members(nodes, grid_row[...]))
    flux = atmosphere[0:16].astype(F32)[1:2] + flux[0:1] + flux[1:2]
    n_points = flux.shape[1]
    match = one_hot(iota((n_points, placed.shape[1]), 0) == placed[...])
    spread = dot(jnp.broadcast_to(flux, (8, n_points)).astype(BF16), match)
    rows = placed.shape[1] // W
    out = jnp.zeros((8, rows), F32)
    for o in range(W):
        out = jnp.where(iota((8, rows), 0) == o, spread[:, o * rows : (o + 1) * rows], out)
    flux_out[...] = jnp.concatenate([out, jnp.zeros((8, rows), F32)], axis=0).astype(BF16)


def two_parts(row):
    high = row.astype(BF16).astype(F32)
    return jnp.concatenate([high, row - high, jnp.zeros((6, row.shape[1]), F32)], axis=0).astype(BF16)


def decode_kernel(node_new, w_decode, grid_row, atmosphere, surface, state_out):
    change = dot_nt(w_decode[...], node_new[...])
    change_high = change.astype(BF16)
    change_low = (change - change_high.astype(F32)).astype(BF16)
    member = members(node_new.shape[0], grid_row[...])
    state = atmosphere[...].astype(F32)
    state = jnp.where(iota(state.shape, 0) == 0, surface[...].astype(BF16).astype(F32), state)
    state_out[...] = (state + dot(change_high, member) + dot(change_low, member)).astype(BF16)


def ready_kernel(heat, east, north, mask, low, high, field_out, wet_out, px_out, qx_out, py_out, qy_out, mix_out):
    columns, rows = mask.shape
    levels = heat.shape[1]
    below, above = low[...].astype(F32), high[...].astype(F32)
    own_wet = mask[...].astype(F32)

    def wide(source, at):
        left = [below[8 * (at * EDGE + c) : 8 * (at * EDGE + c) + 8] for c in range(EDGE)]
        right = [above[8 * (at * EDGE + c) : 8 * (at * EDGE + c) + 8] for c in range(EDGE)]
        return left + [source[c] for c in range(columns)] + right

    base = 3 * 8 * EDGE
    wet = [below[base + c : base + c + 1] for c in range(EDGE)]
    wet += [own_wet[c : c + 1] for c in range(columns)]
    wet += [above[base + c : base + c + 1] for c in range(EDGE)]
    wet = [jnp.broadcast_to(w, (levels, rows)) for w in wet]
    field, u, v = wide(heat, 0), wide(east, 1), wide(north, 2)
    lane = iota((levels, rows), 1)
    level = iota((levels, rows), 0)
    count = len(field)
    for c in range(count):
        field_out[c] = field[c]
        wet_out[c] = wet[c]
        mix_out[c] = jnp.where(level < levels - 1, COEFF_V * wet[c], 0.0)
        if c + 1 < count:
            opened = wet[c] * wet[c + 1]
            face = 0.25 * (u[c] + u[c + 1])
            px_out[c] = opened * (face + COEFF_H)
            qx_out[c] = opened * (face - COEFF_H)
        opened = jnp.where(lane < rows - 1, wet[c] * pltpu.roll(wet[c], rows - 1, 1), 0.0)
        face = 0.25 * (v[c] + pltpu.roll(v[c], rows - 1, 1))
        py_out[c] = opened * (face + COEFF_H)
        qy_out[c] = opened * (face - COEFF_H)


def ocean_kernel(f_m1, f_m2, f_m3, f_p2, f_p1, f_0, field_in, wet, px, qx, py, qy, mix, out):
    count, levels, rows = field_in.shape
    columns = count - 2 * EDGE
    triples = columns // 3
    span = rows // 3
    fluxes = [f[...].astype(F32) for f in (f_m3, f_m2, f_m1, f_0, f_p1, f_p2)]

    def gathered(begin):
        return sum(fluxes[begin + o][o : o + 1] for o in range(W))

    own = gathered(1)
    blocks = [gathered(0)[:, (triples - 1) * span :]]
    blocks += [own[:, t * span : (t + 1) * span] for t in range(triples)]
    blocks += [gathered(2)[:, :span]]
    blocks += [jnp.zeros((16 - len(blocks), span), F32)]
    expand = one_hot(iota((span, rows), 1) // 3 == iota((span, rows), 0))
    cells = COEFF_Q * dot(jnp.concatenate(blocks, axis=0).astype(BF16), expand)
    level = iota((levels, rows), 0)
    surface = [
        jnp.where(level == 0, jnp.broadcast_to(cells[t : t + 1], (levels, rows)), 0.0)
        for t in range(triples + 2)
    ]
    field = [field_in[c] for c in range(count)]
    for step in range(STEPS):
        begin, end = step + 1, count - step - 1
        across = {c: px[c] * field[c] + qx[c] * field[c + 1] for c in range(begin - 1, end)}
        later = [None] * count
        for c in range(begin, end):
            here = field[c]
            along = py[c] * here + qy[c] * pltpu.roll(here, rows - 1, 1)
            mixed = mix[c] * (pltpu.roll(here, levels - 1, 0) - here)
            group = (c - EDGE + 3) // 3
            change = (
                (across[c - 1] - across[c])
                + (pltpu.roll(along, 1, 1) - along)
                + (mixed - pltpu.roll(mixed, 1, 0))
            )
            later[c] = wet[c] * (here + change + surface[group])
        field = later
    for c in range(columns):
        out[c] = field[EDGE + c]


VMEM = pl.BlockSpec(memory_space=pltpu.VMEM)
HBM = pl.BlockSpec(memory_space=pltpu.HBM)


def call(kernel, outs, inputs, spec=VMEM, scratch=(), flops=0, bytes_accessed=1 << 20, name=None):
    if spec is HBM:
        inputs = [pltpu.with_memory_space_constraint(x, pltpu.HBM) for x in inputs]
    return pl.pallas_call(
        kernel,
        out_shape=[jax.ShapeDtypeStruct(s, t) for s, t in outs],
        in_specs=[spec] * len(inputs),
        out_specs=[VMEM] * len(outs),
        scratch_shapes=list(scratch),
        compiler_params=pltpu.CompilerParams(vmem_limit_bytes=40 << 20),
        cost_estimate=pl.CostEstimate(flops=flops, bytes_accessed=bytes_accessed, transcendentals=0),
        name=name,
    )(*inputs)


def body(
    atmosphere,
    mesh_state,
    edge_geometry,
    neighbours,
    grid_node,
    ocean_heat_field,
    east_velocity,
    north_velocity,
    ocean_mask,
    intersection_points,
    intersection_counts,
    w_geometry,
    w_encode,
    w_edge_in,
    w_edge_out,
    w_node_in,
    w_node_out,
    w_decode,
    gain_edge,
    gain_node,
):
    levels, columns, rows = ocean_heat_field.shape
    nodes, features = mesh_state.shape
    n_points, channels = atmosphere.shape
    heat, east, north = (
        x.transpose(1, 0, 2) for x in (ocean_heat_field, east_velocity, north_velocity)
    )
    atmosphere_t = atmosphere.T
    slots = neighbours.T
    grid_row = grid_node.reshape(1, n_points)
    decode_t = w_decode.T
    ends = (3 * levels * EDGE + 16, rows)
    few = (16, rows)
    own_ocean = (columns, levels, rows)
    low, high, blocks = call(
        pack_kernel,
        [(ends, BF16), (ends, BF16), (few, BF16)],
        [intersection_counts, heat, east, north, ocean_mask],
        spec=HBM,
        scratch=[
            pltpu.SMEM((1, W), jnp.int32),
            pltpu.VMEM(own_ocean, F32),
            pltpu.VMEM(own_ocean, F32),
            pltpu.VMEM(own_ocean, F32),
            pltpu.VMEM((columns, rows), jnp.int32),
            pltpu.SemaphoreType.DMA((5,)),
        ],
        name="pack",
    )
    below = shifted(high, 1)
    above = shifted(low, -1)
    far = shifted(blocks, -2)
    (plain,) = call(
        plain_kernel,
        [((nodes, features), F32)],
        [atmosphere_t, w_encode, grid_row, mesh_state],
        spec=HBM,
        scratch=[
            pltpu.VMEM((channels, n_points), BF16),
            pltpu.VMEM(w_encode.shape, BF16),
            pltpu.VMEM((1, n_points), jnp.int32),
            pltpu.VMEM((nodes, features), BF16),
            pltpu.SemaphoreType.DMA((4,)),
        ],
        flops=6 * nodes * channels * n_points,
        bytes_accessed=2 << 20,
        name="plain",
    )
    latent, surface, placed = call(
        latent_kernel,
        [((nodes, features), BF16), ((1, n_points), F32), ((1, W * rows), jnp.int32)],
        [below, above, far, blocks, intersection_points[0], atmosphere_t, w_encode, grid_row, plain],
        name="latents",
    )
    latent_low = shifted(latent, 1)
    latent_high = shifted(latent, -1)
    pre, base, node_part = call(
        own_kernel,
        [((K, nodes, features), BF16), ((nodes, features), F32), ((nodes, features), F32)],
        [latent, w_edge_in, edge_geometry, w_geometry, slots, w_node_in],
        scratch=[pltpu.VMEM((nodes, features), BF16), pltpu.VMEM((K * nodes, 128), F32)],
        flops=2 * K * nodes * (nodes + features) * features,
        bytes_accessed=10 << 20,
        name="own",
    )
    wide = (columns + 2 * EDGE, levels, rows)
    ready = call(
        ready_kernel,
        [(wide, F32)] * 7,
        [heat, east, north, ocean_mask, below, above],
        bytes_accessed=4 << 20,
        name="ready",
    )
    node_new, flux = call(
        mesh_kernel,
        [((nodes, features), BF16), (few, BF16)],
        [
            latent_low, latent_high, latent, w_edge_in, w_edge_out, pre, base, node_part, slots,
            w_node_in, w_node_out, decode_t, gain_edge.reshape(1, features),
            gain_node.reshape(1, features), grid_row, atmosphere_t, placed,
        ],
        scratch=[pltpu.VMEM((2 * nodes, features), BF16), pltpu.VMEM((nodes, features), F32)],
        flops=2 * K * nodes * 3 * nodes * features,
        bytes_accessed=10 << 20,
        name="mesh",
    )
    sent = {d: shifted(flux, d) for d in (1, 2, 3, -1, -2)}
    sent[0] = flux
    arrived = [sent[d] for d in (1, 2, 3, -2, -1, 0)]
    (state,) = call(
        decode_kernel,
        [((channels, n_points), BF16)],
        [node_new, decode_t, grid_row, atmosphere_t, surface],
        flops=6 * nodes * channels * n_points,
        name="decode",
    )
    (ocean_new,) = call(
        ocean_kernel,
        [(own_ocean, F32)],
        [*arrived, *ready],
        bytes_accessed=4 << 20,
        name="ocean",
    )
    return (state.T, ocean_new.transpose(1, 0, 2))


def solution(mesh):
    ranges = ("member", "tile", "comp")
    placed = (
        P(ranges, None),
        P(ranges, None),
        P(None, ranges),
        P(ranges, None),
        P(ranges),
        P(None, ranges, None),
        P(None, ranges, None),
        P(None, ranges, None),
        P(ranges, None),
        P(ranges, None, None),
        P(ranges, None),
        P(),
        P(),
        P(),
        P(),
        P(),
        P(),
        P(),
        P(),
        P(),
    )
    return jax.shard_map(
        body,
        mesh=mesh,
        in_specs=placed,
        out_specs=(P(ranges, None), P(None, ranges, None)),
        check_vma=False,
    )
```

```python
import jax
import jax.numpy as jnp
from jax import lax
from jax.experimental import pallas as pl
from jax.experimental.pallas import tpu as pltpu
from jax.sharding import PartitionSpec as P

K = 8
STEPS = 4
W = 4
EDGE = 4

COEFF_H = 0.15
COEFF_V = 0.1
COEFF_Q = 0.5
EPSILON = 1e-05

F32 = jnp.float32
BF16 = jnp.bfloat16
AXES = ("tile", "comp")


def shifted(block, distance):
    count = lax.axis_size(AXES)
    return lax.ppermute(block, AXES, [((i - distance) % count, i) for i in range(count)])


def dot(a, b):
    return jnp.dot(a, b, preferred_element_type=F32)


def dot_nt(a, b):
    return lax.dot_general(a, b, (((1,), (1,)), ((), ())), preferred_element_type=F32)


def silu(v):
    return 0.5 * v * (1.0 + jnp.tanh(0.5 * v))


def one_hot(test):
    return jnp.where(test, 1.0, 0.0).astype(BF16)


def iota(shape, dim):
    return lax.broadcasted_iota(jnp.int32, shape, dim)


def started(pairs, sems):
    copies = [pltpu.make_async_copy(a, b, sems.at[i]) for i, (a, b) in enumerate(pairs)]
    for copy in copies:
        copy.start()
    return copies


def pack_kernel(
    counts_in, heat_in, east_in, north_in, mask_in, low_out, high_out, blocks_out,
    counts, heat, east, north, mask, sems,
):
    copies = started(
        ((counts_in, counts), (heat_in, heat), (mask_in, mask), (east_in, east), (north_in, north)), sems
    )
    for copy in copies:
        copy.wait()
    columns, rows = mask.shape
    wet = mask[...].astype(F32)
    triples = columns // 3

    def over_columns(x):
        return jnp.concatenate([x[3 * t] + x[3 * t + 1] + x[3 * t + 2] for t in range(triples)], axis=0)

    wet_rows = [wet[c : c + 1] for c in range(columns)]
    sums = over_columns([heat[c, 0:1] * wet_rows[c] for c in range(columns)])
    first = sums.astype(BF16).astype(F32)
    second = (sums - first).astype(BF16).astype(F32)
    third = sums - first - second
    parts = jnp.concatenate(
        [first, second, third, over_columns(wet_rows), jnp.zeros((16 - 4 * triples, rows), F32)], axis=0
    ).astype(BF16)
    pick = one_hot(iota((rows, rows // 3), 0) // 3 == iota((rows, rows // 3), 1))
    folded = dot(parts, pick)

    def flat(x):
        return jnp.concatenate([x[t : t + 1] for t in range(triples)], axis=1)

    t = triples
    total = flat(folded[:t] + folded[t : 2 * t] + folded[2 * t : 3 * t])
    number = flat(folded[3 * t : 4 * t])
    mean = total / jnp.maximum(number, 1.0)
    mean_high = mean.astype(BF16).astype(F32)
    flags = jnp.where(number > 0.5, 1.0, 0.0)
    lane = iota((1, rows), 1)
    held = jnp.zeros((1, rows), F32)
    for o in range(W):
        held = jnp.where(lane == o, counts[0, o].astype(F32), held)
    bundle = jnp.concatenate(
        [mean_high, mean - mean_high, flags, held, jnp.zeros((4, rows), F32)], axis=0
    )
    blank = jnp.zeros((4, rows), F32)
    for out, begin in ((low_out, 0), (high_out, columns - EDGE)):
        pieces = [source[c] for source in (heat, east, north) for c in range(begin, begin + EDGE)]
        pieces += [wet[begin : begin + EDGE], blank, bundle]
        out[...] = jnp.concatenate(pieces, axis=0).astype(BF16)
    blocks_out[...] = jnp.concatenate([bundle, jnp.zeros((8, rows), F32)], axis=0).astype(BF16)


def members(nodes, grid_row):
    return one_hot(iota((nodes, grid_row.shape[1]), 0) == grid_row)


def plain_kernel(
    atmosphere_in, w_encode_in, grid_row_in, mesh_state_in, plain_out,
    atmosphere, w_encode, grid_row, mesh_state, sems,
):
    copies = started(
        (
            (grid_row_in, grid_row),
            (atmosphere_in, atmosphere),
            (w_encode_in, w_encode),
            (mesh_state_in, mesh_state),
        ),
        sems,
    )
    for copy in copies:
        copy.wait()
    member = members(mesh_state.shape[0], grid_row[...])
    population = jnp.sum(member.astype(F32), axis=1, keepdims=True)
    state = atmosphere[...]
    state = jnp.where(iota(state.shape, 0) == 0, 0.0, state.astype(F32)).astype(BF16)
    pooled = dot_nt(member, state) / jnp.maximum(population, 1.0)
    pooled_high = pooled.astype(BF16)
    pooled_low = (pooled - pooled_high.astype(F32)).astype(BF16)
    encode = w_encode[...]
    plain_out[...] = mesh_state[...].astype(F32) + dot(pooled_high, encode) + dot(pooled_low, encode)


def rolled_points(points, starts):
    rows = 2 * points.shape[1]
    empty = jnp.full((1, rows - points.shape[1]), 1 << 20, jnp.int32)
    return [
        pltpu.roll(jnp.concatenate([points[o : o + 1, :], empty], axis=1), starts[o], 1) for o in range(W)
    ]


def before(bundle_rows, o):
    lane = iota((1, bundle_rows.shape[1]), 1)
    return jnp.sum(jnp.where(lane < o, bundle_rows[3:4], 0.0)).astype(jnp.int32)


def latent_kernel(
    below, above, far, own, points, atmosphere, w_encode, grid_row, plain,
    latent_out, surface_out, placed_out,
):
    parts = [
        far[...].astype(F32)[:8],
        above[...].astype(F32)[-8:],
        own[...].astype(F32)[:8],
        below[...].astype(F32)[-8:],
    ]
    starts = [0, before(parts[1], 1), before(parts[2], 2), before(parts[3], 3)]
    placed = jnp.concatenate(rolled_points(points, starts), axis=1)
    placed_out[...] = placed
    n_points = grid_row.shape[1]
    values = jnp.concatenate(parts, axis=1).astype(BF16)
    match = one_hot(iota((n_points, placed.shape[1]), 0) == placed)
    sums = dot_nt(values, match)
    total = sums[0:1] + sums[1:2]
    number = sums[2:3]
    surface = jnp.where(
        number > 0.5, total / jnp.maximum(number, 1.0), atmosphere[0:16].astype(F32)[0:1]
    )
    surface_out[...] = surface
    pair = jnp.concatenate([surface, jnp.ones((7, n_points), F32)], axis=0).astype(BF16)
    pooled = dot_nt(members(plain.shape[0], grid_row[...]), pair)
    share = pooled[:, 0:1] / jnp.maximum(pooled[:, 1:2], 1.0)
    latent_out[...] = (plain[...] + share * w_encode[0:16].astype(F32)[0:1]).astype(BF16)


def listed_slots(neighbours):
    return neighbours[...].astype(F32).T


def slot_senders(listed, k):
    lane = iota(listed.shape, 1)
    return jnp.sum(jnp.where(lane == k, listed, 0.0), axis=1, keepdims=True).astype(jnp.int32)


def own_kernel(
    latent, w_in, geometry, w_geometry, neighbours, w_node_in, pre_out, base_out, node_out, sender, turned,
):
    nodes, features = latent.shape
    value = latent[...]
    sender[...] = dot(value, w_in[features : 2 * features]).astype(BF16)
    receiver = dot(value, w_in[2 * features :])
    node_out[...] = dot(value, w_node_in[:features])
    listed = listed_slots(neighbours)
    blank = jnp.zeros((4, geometry.shape[1]), F32)
    turned[:, :8] = jnp.concatenate([geometry[...].astype(F32), blank], axis=0).T
    blank = jnp.zeros((4, features), F32)
    w_geo = jnp.concatenate([w_geometry[...].astype(F32), blank], axis=0).astype(BF16)
    base = jnp.zeros((nodes, features), F32)
    for k in range(K):
        at = slot_senders(listed, k)
        edge = silu(dot(turned[pl.ds(k, nodes, stride=K), :8].astype(BF16), w_geo)).astype(BF16)
        match = one_hot(iota((nodes, nodes), 1) + nodes == at)
        joined = dot(edge, w_in[:features]) + dot(match, sender[...])
        pre_out[k] = (joined + receiver).astype(BF16)
        base = base + jnp.where(at < 3 * nodes, edge.astype(F32), 0.0)
    base_out[...] = base


def normal(values):
    average = jnp.mean(values, axis=-1, keepdims=True)
    centred = values - average
    variance = jnp.mean(centred * centred, axis=-1, keepdims=True)
    return centred, lax.rsqrt(variance + EPSILON)


def mesh_kernel(
    low, high, latent, w_in, w_out, pre, base, node_part, neighbours, w_node_in, w_node_out, w_decode,
    gain_edge, gain_node, grid_row, atmosphere, placed, node_out, flux_out, sender, total,
):
    nodes, features = latent.shape
    w_sender = w_in[features : 2 * features]
    sender[:nodes] = dot(low[...], w_sender).astype(BF16)
    sender[nodes:] = dot(high[...], w_sender).astype(BF16)
    listed = listed_slots(neighbours)
    total[...] = jnp.zeros((nodes, features), F32)

    def step(k, carry):
        at = slot_senders(listed, k)
        place = jnp.where(at < nodes, at, jnp.where(at >= 2 * nodes, at - nodes, -1))
        match = one_hot(iota((nodes, 2 * nodes), 1) == place)
        hidden = silu(pre[k].astype(F32) + dot(match, sender[...])).astype(BF16)
        centred, scale = normal(dot(hidden, w_out[...]))
        total[...] += centred * jnp.where(at < 3 * nodes, scale, 0.0)
        return carry

    lax.fori_loop(0, K, step, 0, unroll=True)
    aggregate = (base[...] + total[...] * gain_edge[...]).astype(BF16)
    hidden = silu(node_part[...] + dot(aggregate, w_node_in[features:])).astype(BF16)
    centred, scale = normal(dot(hidden, w_node_out[...]))
    node_new = (latent[...].astype(F32) + centred * scale * gain_node[...]).astype(BF16)
    node_out[...] = node_new
    flux = two_parts(dot_nt(w_decode[0:16], node_new)[1:2])
    flux = dot(flux, members(nodes, grid_row[...]))
    flux = atmosphere[0:16].astype(F32)[1:2] + flux[0:1] + flux[1:2]
    n_points = flux.shape[1]
    match = one_hot(iota((n_points, placed.shape[1]), 0) == placed[...])
    spread = dot(jnp.broadcast_to(flux, (8, n_points)).astype(BF16), match)
    rows = placed.shape[1] // W
    out = jnp.zeros((8, rows), F32)
    for o in range(W):
        out = jnp.where(iota((8, rows), 0) == o, spread[:, o * rows : (o + 1) * rows], out)
    flux_out[...] = jnp.concatenate([out, jnp.zeros((8, rows), F32)], axis=0).astype(BF16)


def two_parts(row):
    high = row.astype(BF16).astype(F32)
    return jnp.concatenate([high, row - high, jnp.zeros((6, row.shape[1]), F32)], axis=0).astype(BF16)


def decode_kernel(node_new, w_decode, grid_row, atmosphere, surface, state_out):
    change = dot_nt(w_decode[...], node_new[...])
    change_high = change.astype(BF16)
    change_low = (change - change_high.astype(F32)).astype(BF16)
    member = members(node_new.shape[0], grid_row[...])
    state = atmosphere[...].astype(F32)
    state = jnp.where(iota(state.shape, 0) == 0, surface[...].astype(BF16).astype(F32), state)
    state_out[...] = (state + dot(change_high, member) + dot(change_low, member)).astype(BF16)


def ready_kernel(heat, east, north, mask, low, high, field_out, wet_out, px_out, qx_out, py_out, qy_out, mix_out):
    columns, rows = mask.shape
    levels = heat.shape[1]
    below, above = low[...].astype(F32), high[...].astype(F32)
    own_wet = mask[...].astype(F32)

    def wide(source, at):
        left = [below[8 * (at * EDGE + c) : 8 * (at * EDGE + c) + 8] for c in range(EDGE)]
        right = [above[8 * (at * EDGE + c) : 8 * (at * EDGE + c) + 8] for c in range(EDGE)]
        return left + [source[c] for c in range(columns)] + right

    base = 3 * 8 * EDGE
    wet = [below[base + c : base + c + 1] for c in range(EDGE)]
    wet += [own_wet[c : c + 1] for c in range(columns)]
    wet += [above[base + c : base + c + 1] for c in range(EDGE)]
    wet = [jnp.broadcast_to(w, (levels, rows)) for w in wet]
    field, u, v = wide(heat, 0), wide(east, 1), wide(north, 2)
    lane = iota((levels, rows), 1)
    level = iota((levels, rows), 0)
    count = len(field)
    for c in range(count):
        field_out[c] = field[c]
        wet_out[c] = wet[c]
        mix_out[c] = jnp.where(level < levels - 1, COEFF_V * wet[c], 0.0)
        if c + 1 < count:
            opened = wet[c] * wet[c + 1]
            face = 0.25 * (u[c] + u[c + 1])
            px_out[c] = opened * (face + COEFF_H)
            qx_out[c] = opened * (face - COEFF_H)
        opened = jnp.where(lane < rows - 1, wet[c] * pltpu.roll(wet[c], rows - 1, 1), 0.0)
        face = 0.25 * (v[c] + pltpu.roll(v[c], rows - 1, 1))
        py_out[c] = opened * (face + COEFF_H)
        qy_out[c] = opened * (face - COEFF_H)


def ocean_kernel(f_m1, f_m2, f_m3, f_p2, f_p1, f_0, field_in, wet, px, qx, py, qy, mix, out):
    count, levels, rows = field_in.shape
    columns = count - 2 * EDGE
    triples = columns // 3
    span = rows // 3
    fluxes = [f[...].astype(F32) for f in (f_m3, f_m2, f_m1, f_0, f_p1, f_p2)]

    def gathered(begin):
        return sum(fluxes[begin + o][o : o + 1] for o in range(W))

    own = gathered(1)
    blocks = [gathered(0)[:, (triples - 1) * span :]]
    blocks += [own[:, t * span : (t + 1) * span] for t in range(triples)]
    blocks += [gathered(2)[:, :span]]
    blocks += [jnp.zeros((16 - len(blocks), span), F32)]
    expand = one_hot(iota((span, rows), 1) // 3 == iota((span, rows), 0))
    cells = COEFF_Q * dot(jnp.concatenate(blocks, axis=0).astype(BF16), expand)
    level = iota((levels, rows), 0)
    surface = [
        jnp.where(level == 0, jnp.broadcast_to(cells[t : t + 1], (levels, rows)), 0.0)
        for t in range(triples + 2)
    ]
    field = [field_in[c] for c in range(count)]
    for step in range(STEPS):
        begin, end = step + 1, count - step - 1
        across = {c: px[c] * field[c] + qx[c] * field[c + 1] for c in range(begin - 1, end)}
        later = [None] * count
        for c in range(begin, end):
            here = field[c]
            along = py[c] * here + qy[c] * pltpu.roll(here, rows - 1, 1)
            mixed = mix[c] * (pltpu.roll(here, levels - 1, 0) - here)
            group = (c - EDGE + 3) // 3
            change = (
                (across[c - 1] - across[c])
                + (pltpu.roll(along, 1, 1) - along)
                + (mixed - pltpu.roll(mixed, 1, 0))
            )
            later[c] = wet[c] * (here + change + surface[group])
        field = later
    for c in range(columns):
        out[c] = field[EDGE + c]


VMEM = pl.BlockSpec(memory_space=pltpu.VMEM)
HBM = pl.BlockSpec(memory_space=pltpu.HBM)


def call(kernel, outs, inputs, spec=VMEM, scratch=(), flops=0, bytes_accessed=1 << 20, name=None):
    if spec is HBM:
        inputs = [pltpu.with_memory_space_constraint(x, pltpu.HBM) for x in inputs]
    return pl.pallas_call(
        kernel,
        out_shape=[jax.ShapeDtypeStruct(s, t) for s, t in outs],
        in_specs=[spec] * len(inputs),
        out_specs=[VMEM] * len(outs),
        scratch_shapes=list(scratch),
        compiler_params=pltpu.CompilerParams(vmem_limit_bytes=40 << 20),
        cost_estimate=pl.CostEstimate(flops=flops, bytes_accessed=bytes_accessed, transcendentals=0),
        name=name,
    )(*inputs)


def body(
    atmosphere,
    mesh_state,
    edge_geometry,
    neighbours,
    grid_node,
    ocean_heat_field,
    east_velocity,
    north_velocity,
    ocean_mask,
    intersection_points,
    intersection_counts,
    w_geometry,
    w_encode,
    w_edge_in,
    w_edge_out,
    w_node_in,
    w_node_out,
    w_decode,
    gain_edge,
    gain_node,
):
    levels, columns, rows = ocean_heat_field.shape
    nodes, features = mesh_state.shape
    n_points, channels = atmosphere.shape
    heat, east, north = (
        x.transpose(1, 0, 2) for x in (ocean_heat_field, east_velocity, north_velocity)
    )
    atmosphere_t = atmosphere.T
    slots = neighbours.T
    grid_row = grid_node.reshape(1, n_points)
    decode_t = w_decode.T
    ends = (3 * levels * EDGE + 16, rows)
    few = (16, rows)
    own_ocean = (columns, levels, rows)
    low, high, blocks = call(
        pack_kernel,
        [(ends, BF16), (ends, BF16), (few, BF16)],
        [intersection_counts, heat, east, north, ocean_mask],
        spec=HBM,
        scratch=[
            pltpu.SMEM((1, W), jnp.int32),
            pltpu.VMEM(own_ocean, F32),
            pltpu.VMEM(own_ocean, F32),
            pltpu.VMEM(own_ocean, F32),
            pltpu.VMEM((columns, rows), jnp.int32),
            pltpu.SemaphoreType.DMA((5,)),
        ],
        name="pack",
    )
    below = shifted(high, 1)
    above = shifted(low, -1)
    far = shifted(blocks, -2)
    (plain,) = call(
        plain_kernel,
        [((nodes, features), F32)],
        [atmosphere_t, w_encode, grid_row, mesh_state],
        spec=HBM,
        scratch=[
            pltpu.VMEM((channels, n_points), BF16),
            pltpu.VMEM(w_encode.shape, BF16),
            pltpu.VMEM((1, n_points), jnp.int32),
            pltpu.VMEM((nodes, features), BF16),
            pltpu.SemaphoreType.DMA((4,)),
        ],
        flops=2 * K * nodes * features * features,
        bytes_accessed=8 << 20,
        name="plain",
    )
    latent, surface, placed = call(
        latent_kernel,
        [((nodes, features), BF16), ((1, n_points), F32), ((1, W * rows), jnp.int32)],
        [below, above, far, blocks, intersection_points[0], atmosphere_t, w_encode, grid_row, plain],
        name="latents",
    )
    latent_low = shifted(latent, 1)
    latent_high = shifted(latent, -1)
    pre, base, node_part = call(
        own_kernel,
        [((K, nodes, features), BF16), ((nodes, features), F32), ((nodes, features), F32)],
        [latent, w_edge_in, edge_geometry, w_geometry, slots, w_node_in],
        scratch=[pltpu.VMEM((nodes, features), BF16), pltpu.VMEM((K * nodes, 128), F32)],
        flops=2 * K * nodes * (nodes + features) * features,
        bytes_accessed=10 << 20,
        name="own",
    )
    wide = (columns + 2 * EDGE, levels, rows)
    ready = call(
        ready_kernel,
        [(wide, F32)] * 7,
        [heat, east, north, ocean_mask, below, above],
        bytes_accessed=4 << 20,
        name="ready",
    )
    node_new, flux = call(
        mesh_kernel,
        [((nodes, features), BF16), (few, BF16)],
        [
            latent_low, latent_high, latent, w_edge_in, w_edge_out, pre, base, node_part, slots,
            w_node_in, w_node_out, decode_t, gain_edge.reshape(1, features),
            gain_node.reshape(1, features), grid_row, atmosphere_t, placed,
        ],
        scratch=[pltpu.VMEM((2 * nodes, features), BF16), pltpu.VMEM((nodes, features), F32)],
        flops=2 * K * nodes * 3 * nodes * features,
        bytes_accessed=10 << 20,
        name="mesh",
    )
    sent = {d: shifted(flux, d) for d in (1, 2, 3, -1, -2)}
    sent[0] = flux
    arrived = [sent[d] for d in (1, 2, 3, -2, -1, 0)]
    (state,) = call(
        decode_kernel,
        [((channels, n_points), BF16)],
        [node_new, decode_t, grid_row, atmosphere_t, surface],
        flops=6 * nodes * channels * n_points,
        name="decode",
    )
    (ocean_new,) = call(
        ocean_kernel,
        [(own_ocean, F32)],
        [*arrived, *ready],
        bytes_accessed=4 << 20,
        name="ocean",
    )
    return (state.T, ocean_new.transpose(1, 0, 2))


def solution(mesh):
    ranges = ("member", "tile", "comp")
    placed = (
        P(ranges, None),
        P(ranges, None),
        P(None, ranges),
        P(ranges, None),
        P(ranges),
        P(None, ranges, None),
        P(None, ranges, None),
        P(None, ranges, None),
        P(ranges, None),
        P(ranges, None, None),
        P(ranges, None),
        P(),
        P(),
        P(),
        P(),
        P(),
        P(),
        P(),
        P(),
        P(),
    )
    return jax.shard_map(
        body,
        mesh=mesh,
        in_specs=placed,
        out_specs=(P(ranges, None), P(None, ranges, None)),
        check_vma=False,
    )
```

```python
import jax
import jax.numpy as jnp
from jax import lax
from jax.experimental import pallas as pl
from jax.experimental.pallas import tpu as pltpu
from jax.sharding import PartitionSpec as P

K = 8
STEPS = 4
W = 4
EDGE = 4

COEFF_H = 0.15
COEFF_V = 0.1
COEFF_Q = 0.5
EPSILON = 1e-05

F32 = jnp.float32
BF16 = jnp.bfloat16
AXES = ("tile", "comp")


INNER, OUTER = (1, -1), (-1, 1)
NEAR, FAR = (2, 2, -2, -2), (-2, -2, 2, 2)


def sent(block, offsets):
    count = lax.axis_size(AXES)
    route = [(i, (i + offsets[i % len(offsets)]) % count) for i in range(count)]
    return lax.ppermute(block, AXES, route)


def is_even():
    return lax.axis_index("comp") == 0


def pair_is_even():
    return lax.rem(lax.axis_index("tile"), 2) == 0


def dot(a, b):
    return jnp.dot(a, b, preferred_element_type=F32)


def dot_nt(a, b):
    return lax.dot_general(a, b, (((1,), (1,)), ((), ())), preferred_element_type=F32)


def silu(v):
    return 0.5 * v * (1.0 + jnp.tanh(0.5 * v))


def one_hot(test):
    return jnp.where(test, 1.0, 0.0).astype(BF16)


def iota(shape, dim):
    return lax.broadcasted_iota(jnp.int32, shape, dim)


def started(pairs, sems):
    copies = [pltpu.make_async_copy(a, b, sems.at[i]) for i, (a, b) in enumerate(pairs)]
    for copy in copies:
        copy.start()
    return copies


def pack_kernel(
    counts_in, heat_in, east_in, north_in, mask_in, inner_out, outer_out, blocks_out,
    counts, heat, east, north, mask, sems,
):
    copies = started(
        ((counts_in, counts), (heat_in, heat), (mask_in, mask), (east_in, east), (north_in, north)), sems
    )
    for copy in copies:
        copy.wait()
    columns, rows = mask.shape
    wet = mask[...].astype(F32)
    triples = columns // 3

    def over_columns(x):
        return jnp.concatenate([x[3 * t] + x[3 * t + 1] + x[3 * t + 2] for t in range(triples)], axis=0)

    wet_rows = [wet[c : c + 1] for c in range(columns)]
    sums = over_columns([heat[c, 0:1] * wet_rows[c] for c in range(columns)])
    first = sums.astype(BF16).astype(F32)
    second = (sums - first).astype(BF16).astype(F32)
    third = sums - first - second
    parts = jnp.concatenate(
        [first, second, third, over_columns(wet_rows), jnp.zeros((16 - 4 * triples, rows), F32)], axis=0
    ).astype(BF16)
    pick = one_hot(iota((rows, rows // 3), 0) // 3 == iota((rows, rows // 3), 1))
    folded = dot(parts, pick)

    def flat(x):
        return jnp.concatenate([x[t : t + 1] for t in range(triples)], axis=1)

    t = triples
    total = flat(folded[:t] + folded[t : 2 * t] + folded[2 * t : 3 * t])
    number = flat(folded[3 * t : 4 * t])
    mean = total / jnp.maximum(number, 1.0)
    mean_high = mean.astype(BF16).astype(F32)
    flags = jnp.where(number > 0.5, 1.0, 0.0)
    lane = iota((1, rows), 1)
    held = jnp.zeros((1, rows), F32)
    for o in range(W):
        held = jnp.where(lane == o, counts[0, o].astype(F32), held)
    bundle = jnp.concatenate(
        [mean_high, mean - mean_high, flags, held, jnp.zeros((4, rows), F32)], axis=0
    )
    blank = jnp.zeros((4, rows), F32)
    ends = []
    for begin in (0, columns - EDGE):
        pieces = [source[c] for source in (heat, east, north) for c in range(begin, begin + EDGE)]
        pieces += [wet[begin : begin + EDGE], blank, bundle]
        ends.append(jnp.concatenate(pieces, axis=0))
    even = is_even()
    inner_out[...] = jnp.where(even, ends[1], ends[0]).astype(BF16)
    outer_out[...] = jnp.where(even, ends[0], ends[1]).astype(BF16)
    blocks_out[...] = jnp.concatenate([bundle, jnp.zeros((8, rows), F32)], axis=0).astype(BF16)


def members(nodes, grid_row):
    return one_hot(iota((nodes, grid_row.shape[1]), 0) == grid_row)


def plain_kernel(
    atmosphere_in, w_encode_in, grid_row_in, mesh_state_in, plain_out,
    atmosphere, w_encode, grid_row, mesh_state, sems,
):
    copies = started(
        (
            (grid_row_in, grid_row),
            (atmosphere_in, atmosphere),
            (w_encode_in, w_encode),
            (mesh_state_in, mesh_state),
        ),
        sems,
    )
    for copy in copies:
        copy.wait()
    member = members(mesh_state.shape[0], grid_row[...])
    population = jnp.sum(member.astype(F32), axis=1, keepdims=True)
    state = atmosphere[...]
    state = jnp.where(iota(state.shape, 0) == 0, 0.0, state.astype(F32)).astype(BF16)
    pooled = dot_nt(member, state) / jnp.maximum(population, 1.0)
    pooled_high = pooled.astype(BF16)
    pooled_low = (pooled - pooled_high.astype(F32)).astype(BF16)
    encode = w_encode[...]
    plain_out[...] = mesh_state[...].astype(F32) + dot(pooled_high, encode) + dot(pooled_low, encode)


def rolled_points(points, starts):
    rows = 2 * points.shape[1]
    empty = jnp.full((1, rows - points.shape[1]), 1 << 20, jnp.int32)
    return [
        pltpu.roll(jnp.concatenate([points[o : o + 1, :], empty], axis=1), starts[o], 1) for o in range(W)
    ]


def before(bundle_rows, o):
    lane = iota((1, bundle_rows.shape[1]), 1)
    return jnp.sum(jnp.where(lane < o, bundle_rows[3:4], 0.0)).astype(jnp.int32)


def latent_kernel(
    outer, far, inner, own, points, atmosphere, w_encode, grid_row, plain,
    latent_out, surface_out, placed_out,
):
    pair = [x[...].astype(F32)[-8:] for x in (inner, outer)]
    even = is_even()
    parts = [
        far[...].astype(F32)[:8],
        jnp.where(even, pair[0], pair[1]),
        own[...].astype(F32)[:8],
        jnp.where(even, pair[1], pair[0]),
    ]
    starts = [0, before(parts[1], 1), before(parts[2], 2), before(parts[3], 3)]
    placed = jnp.concatenate(rolled_points(points, starts), axis=1)
    placed_out[...] = placed
    n_points = grid_row.shape[1]
    values = jnp.concatenate(parts, axis=1).astype(BF16)
    match = one_hot(iota((n_points, placed.shape[1]), 0) == placed)
    sums = dot_nt(values, match)
    total = sums[0:1] + sums[1:2]
    number = sums[2:3]
    surface = jnp.where(
        number > 0.5, total / jnp.maximum(number, 1.0), atmosphere[0:16].astype(F32)[0:1]
    )
    surface_out[...] = surface
    pair = jnp.concatenate([surface, jnp.ones((7, n_points), F32)], axis=0).astype(BF16)
    pooled = dot_nt(members(plain.shape[0], grid_row[...]), pair)
    share = pooled[:, 0:1] / jnp.maximum(pooled[:, 1:2], 1.0)
    latent_out[...] = (plain[...] + share * w_encode[0:16].astype(F32)[0:1]).astype(BF16)


def listed_slots(neighbours):
    return neighbours[...].astype(F32).T


def slot_senders(listed, k):
    lane = iota(listed.shape, 1)
    return jnp.sum(jnp.where(lane == k, listed, 0.0), axis=1, keepdims=True).astype(jnp.int32)


def own_kernel(
    latent, w_in, geometry, w_geometry, neighbours, w_node_in, pre_out, base_out, node_out, sender, turned,
):
    nodes, features = latent.shape
    value = latent[...]
    sender[...] = dot(value, w_in[features : 2 * features]).astype(BF16)
    receiver = dot(value, w_in[2 * features :])
    node_out[...] = dot(value, w_node_in[:features])
    listed = listed_slots(neighbours)
    blank = jnp.zeros((4, geometry.shape[1]), F32)
    turned[:, :8] = jnp.concatenate([geometry[...].astype(F32), blank], axis=0).T
    blank = jnp.zeros((4, features), F32)
    w_geo = jnp.concatenate([w_geometry[...].astype(F32), blank], axis=0).astype(BF16)
    base = jnp.zeros((nodes, features), F32)
    for k in range(K):
        at = slot_senders(listed, k)
        edge = silu(dot(turned[pl.ds(k, nodes, stride=K), :8].astype(BF16), w_geo)).astype(BF16)
        match = one_hot(iota((nodes, nodes), 1) + nodes == at)
        joined = dot(edge, w_in[:features]) + dot(match, sender[...])
        pre_out[k] = (joined + receiver).astype(BF16)
        base = base + jnp.where(at < 3 * nodes, edge.astype(F32), 0.0)
    base_out[...] = base


def normal(values):
    average = jnp.mean(values, axis=-1, keepdims=True)
    centred = values - average
    variance = jnp.mean(centred * centred, axis=-1, keepdims=True)
    return centred, lax.rsqrt(variance + EPSILON)


def mesh_kernel(
    inner, outer, latent, w_in, w_out, pre, base, node_part, neighbours, w_node_in, w_node_out, w_decode,
    gain_edge, gain_node, grid_row, atmosphere, placed, node_out, flux_out, sender, total,
):
    nodes, features = latent.shape
    w_sender = w_in[features : 2 * features]
    sender[:nodes] = dot(inner[...], w_sender).astype(BF16)
    sender[nodes:] = dot(outer[...], w_sender).astype(BF16)
    below = jnp.where(is_even(), nodes, 0)
    above = nodes - below
    listed = listed_slots(neighbours)
    total[...] = jnp.zeros((nodes, features), F32)

    def step(k, carry):
        at = slot_senders(listed, k)
        place = jnp.where(at < nodes, at + below, jnp.where(at >= 2 * nodes, at - 2 * nodes + above, -1))
        place = jnp.where(at < 3 * nodes, place, -1)
        match = one_hot(iota((nodes, 2 * nodes), 1) == place)
        hidden = silu(pre[k].astype(F32) + dot(match, sender[...])).astype(BF16)
        centred, scale = normal(dot(hidden, w_out[...]))
        total[...] += centred * jnp.where(at < 3 * nodes, scale, 0.0)
        return carry

    lax.fori_loop(0, K, step, 0, unroll=True)
    aggregate = (base[...] + total[...] * gain_edge[...]).astype(BF16)
    hidden = silu(node_part[...] + dot(aggregate, w_node_in[features:])).astype(BF16)
    centred, scale = normal(dot(hidden, w_node_out[...]))
    node_new = (latent[...].astype(F32) + centred * scale * gain_node[...]).astype(BF16)
    node_out[...] = node_new
    flux = two_parts(dot_nt(w_decode[0:16], node_new)[1:2])
    flux = dot(flux, members(nodes, grid_row[...]))
    flux = atmosphere[0:16].astype(F32)[1:2] + flux[0:1] + flux[1:2]
    n_points = flux.shape[1]
    match = one_hot(iota((n_points, placed.shape[1]), 0) == placed[...])
    spread = dot(jnp.broadcast_to(flux, (8, n_points)).astype(BF16), match)
    rows = placed.shape[1] // W
    out = jnp.zeros((8, rows), F32)
    for o in range(W):
        out = jnp.where(iota((8, rows), 0) == o, spread[:, o * rows : (o + 1) * rows], out)
    flux_out[...] = jnp.concatenate([out, jnp.zeros((8, rows), F32)], axis=0).astype(BF16)


def two_parts(row):
    high = row.astype(BF16).astype(F32)
    return jnp.concatenate([high, row - high, jnp.zeros((6, row.shape[1]), F32)], axis=0).astype(BF16)


def decode_kernel(node_new, w_decode, grid_row, atmosphere, surface, state_out):
    change = dot_nt(w_decode[...], node_new[...])
    change_high = change.astype(BF16)
    change_low = (change - change_high.astype(F32)).astype(BF16)
    member = members(node_new.shape[0], grid_row[...])
    state = atmosphere[...].astype(F32)
    state = jnp.where(iota(state.shape, 0) == 0, surface[...].astype(BF16).astype(F32), state)
    state_out[...] = (state + dot(change_high, member) + dot(change_low, member)).astype(BF16)


def ready_kernel(heat, east, north, mask, inner, outer, field_out, wet_out, px_out, qx_out, py_out, qy_out, mix_out):
    columns, rows = mask.shape
    levels = heat.shape[1]
    pair = inner[...].astype(F32), outer[...].astype(F32)
    even = is_even()
    below, above = jnp.where(even, pair[1], pair[0]), jnp.where(even, pair[0], pair[1])
    own_wet = mask[...].astype(F32)

    def wide(source, at):
        left = [below[8 * (at * EDGE + c) : 8 * (at * EDGE + c) + 8] for c in range(EDGE)]
        right = [above[8 * (at * EDGE + c) : 8 * (at * EDGE + c) + 8] for c in range(EDGE)]
        return left + [source[c] for c in range(columns)] + right

    base = 3 * 8 * EDGE
    wet = [below[base + c : base + c + 1] for c in range(EDGE)]
    wet += [own_wet[c : c + 1] for c in range(columns)]
    wet += [above[base + c : base + c + 1] for c in range(EDGE)]
    wet = [jnp.broadcast_to(w, (levels, rows)) for w in wet]
    field, u, v = wide(heat, 0), wide(east, 1), wide(north, 2)
    lane = iota((levels, rows), 1)
    level = iota((levels, rows), 0)
    count = len(field)
    for c in range(count):
        field_out[c] = field[c]
        wet_out[c] = wet[c]
        mix_out[c] = jnp.where(level < levels - 1, COEFF_V * wet[c], 0.0)
        if c + 1 < count:
            opened = wet[c] * wet[c + 1]
            face = 0.25 * (u[c] + u[c + 1])
            px_out[c] = opened * (face + COEFF_H)
            qx_out[c] = opened * (face - COEFF_H)
        opened = jnp.where(lane < rows - 1, wet[c] * pltpu.roll(wet[c], rows - 1, 1), 0.0)
        face = 0.25 * (v[c] + pltpu.roll(v[c], rows - 1, 1))
        py_out[c] = opened * (face + COEFF_H)
        qy_out[c] = opened * (face - COEFF_H)


def ocean_kernel(third, far, outer, near, inner, here_flux, field_in, wet, px, qx, py, qy, mix, out):
    count, levels, rows = field_in.shape
    columns = count - 2 * EDGE
    triples = columns // 3
    span = rows // 3
    third, far, outer, near, inner, here_flux = (
        x[...].astype(F32) for x in (third, far, outer, near, inner, here_flux)
    )
    even, pair_even = is_even(), pair_is_even()
    fluxes = [
        third,
        jnp.where(pair_even, far, near),
        jnp.where(even, outer, inner),
        here_flux,
        jnp.where(even, inner, outer),
        jnp.where(pair_even, near, far),
    ]

    def gathered(begin):
        return sum(fluxes[begin + o][o : o + 1] for o in range(W))

    own = gathered(1)
    blocks = [gathered(0)[:, (triples - 1) * span :]]
    blocks += [own[:, t * span : (t + 1) * span] for t in range(triples)]
    blocks += [gathered(2)[:, :span]]
    blocks += [jnp.zeros((16 - len(blocks), span), F32)]
    expand = one_hot(iota((span, rows), 1) // 3 == iota((span, rows), 0))
    cells = COEFF_Q * dot(jnp.concatenate(blocks, axis=0).astype(BF16), expand)
    level = iota((levels, rows), 0)
    surface = [
        jnp.where(level == 0, jnp.broadcast_to(cells[t : t + 1], (levels, rows)), 0.0)
        for t in range(triples + 2)
    ]
    field = [field_in[c] for c in range(count)]
    for step in range(STEPS):
        begin, end = step + 1, count - step - 1
        across = {c: px[c] * field[c] + qx[c] * field[c + 1] for c in range(begin - 1, end)}
        later = [None] * count
        for c in range(begin, end):
            here = field[c]
            along = py[c] * here + qy[c] * pltpu.roll(here, rows - 1, 1)
            mixed = mix[c] * (pltpu.roll(here, levels - 1, 0) - here)
            group = (c - EDGE + 3) // 3
            change = (
                (across[c - 1] - across[c])
                + (pltpu.roll(along, 1, 1) - along)
                + (mixed - pltpu.roll(mixed, 1, 0))
            )
            later[c] = wet[c] * (here + change + surface[group])
        field = later
    for c in range(columns):
        out[c] = field[EDGE + c]


VMEM = pl.BlockSpec(memory_space=pltpu.VMEM)
HBM = pl.BlockSpec(memory_space=pltpu.HBM)


def call(kernel, outs, inputs, spec=VMEM, scratch=(), flops=0, bytes_accessed=1 << 20, name=None):
    if spec is HBM:
        inputs = [pltpu.with_memory_space_constraint(x, pltpu.HBM) for x in inputs]
    return pl.pallas_call(
        kernel,
        out_shape=[jax.ShapeDtypeStruct(s, t) for s, t in outs],
        in_specs=[spec] * len(inputs),
        out_specs=[VMEM] * len(outs),
        scratch_shapes=list(scratch),
        compiler_params=pltpu.CompilerParams(vmem_limit_bytes=40 << 20),
        cost_estimate=pl.CostEstimate(flops=flops, bytes_accessed=bytes_accessed, transcendentals=0),
        name=name,
    )(*inputs)


def body(
    atmosphere,
    mesh_state,
    edge_geometry,
    neighbours,
    grid_node,
    ocean_heat_field,
    east_velocity,
    north_velocity,
    ocean_mask,
    intersection_points,
    intersection_counts,
    w_geometry,
    w_encode,
    w_edge_in,
    w_edge_out,
    w_node_in,
    w_node_out,
    w_decode,
    gain_edge,
    gain_node,
):
    levels, columns, rows = ocean_heat_field.shape
    nodes, features = mesh_state.shape
    n_points, channels = atmosphere.shape
    heat, east, north = (
        x.transpose(1, 0, 2) for x in (ocean_heat_field, east_velocity, north_velocity)
    )
    atmosphere_t = atmosphere.T
    slots = neighbours.T
    grid_row = grid_node.reshape(1, n_points)
    decode_t = w_decode.T
    ends = (3 * levels * EDGE + 16, rows)
    few = (16, rows)
    own_ocean = (columns, levels, rows)
    to_inner, to_outer, blocks = call(
        pack_kernel,
        [(ends, BF16), (ends, BF16), (few, BF16)],
        [intersection_counts, heat, east, north, ocean_mask],
        spec=HBM,
        scratch=[
            pltpu.SMEM((1, W), jnp.int32),
            pltpu.VMEM(own_ocean, F32),
            pltpu.VMEM(own_ocean, F32),
            pltpu.VMEM(own_ocean, F32),
            pltpu.VMEM((columns, rows), jnp.int32),
            pltpu.SemaphoreType.DMA((5,)),
        ],
        name="pack",
    )
    outer = sent(to_outer, OUTER)
    far = sent(blocks, (-2,))
    inner = sent(to_inner, INNER)
    (plain,) = call(
        plain_kernel,
        [((nodes, features), F32)],
        [atmosphere_t, w_encode, grid_row, mesh_state],
        spec=HBM,
        scratch=[
            pltpu.VMEM((channels, n_points), BF16),
            pltpu.VMEM(w_encode.shape, BF16),
            pltpu.VMEM((1, n_points), jnp.int32),
            pltpu.VMEM((nodes, features), BF16),
            pltpu.SemaphoreType.DMA((4,)),
        ],
        flops=2 * K * nodes * features * features,
        bytes_accessed=8 << 20,
        name="plain",
    )
    latent, surface, placed = call(
        latent_kernel,
        [((nodes, features), BF16), ((1, n_points), F32), ((1, W * rows), jnp.int32)],
        [outer, far, inner, blocks, intersection_points[0], atmosphere_t, w_encode, grid_row, plain],
        name="latents",
    )
    latent_inner = sent(latent, INNER)
    latent_outer = sent(latent, OUTER)
    pre, base, node_part = call(
        own_kernel,
        [((K, nodes, features), BF16), ((nodes, features), F32), ((nodes, features), F32)],
        [latent, w_edge_in, edge_geometry, w_geometry, slots, w_node_in],
        scratch=[pltpu.VMEM((nodes, features), BF16), pltpu.VMEM((K * nodes, 128), F32)],
        flops=2 * K * nodes * (nodes + features) * features,
        bytes_accessed=10 << 20,
        name="own",
    )
    wide = (columns + 2 * EDGE, levels, rows)
    ready = call(
        ready_kernel,
        [(wide, F32)] * 7,
        [heat, east, north, ocean_mask, inner, outer],
        bytes_accessed=4 << 20,
        name="ready",
    )
    node_new, flux = call(
        mesh_kernel,
        [((nodes, features), BF16), (few, BF16)],
        [
            latent_inner, latent_outer, latent, w_edge_in, w_edge_out, pre, base, node_part, slots,
            w_node_in, w_node_out, decode_t, gain_edge.reshape(1, features),
            gain_node.reshape(1, features), grid_row, atmosphere_t, placed,
        ],
        scratch=[pltpu.VMEM((2 * nodes, features), BF16), pltpu.VMEM((nodes, features), F32)],
        flops=2 * K * nodes * 3 * nodes * features,
        bytes_accessed=10 << 20,
        name="mesh",
    )
    arrived = [sent(flux, route) for route in ((3,), FAR, OUTER, NEAR, INNER)]
    (state,) = call(
        decode_kernel,
        [((channels, n_points), BF16)],
        [node_new, decode_t, grid_row, atmosphere_t, surface],
        flops=6 * nodes * channels * n_points,
        name="decode",
    )
    (ocean_new,) = call(
        ocean_kernel,
        [(own_ocean, F32)],
        [*arrived, flux, *ready],
        bytes_accessed=4 << 20,
        name="ocean",
    )
    return (state.T, ocean_new.transpose(1, 0, 2))


def solution(mesh):
    ranges = ("member", "tile", "comp")
    placed = (
        P(ranges, None),
        P(ranges, None),
        P(None, ranges),
        P(ranges, None),
        P(ranges),
        P(None, ranges, None),
        P(None, ranges, None),
        P(None, ranges, None),
        P(ranges, None),
        P(ranges, None, None),
        P(ranges, None),
        P(),
        P(),
        P(),
        P(),
        P(),
        P(),
        P(),
        P(),
        P(),
    )
    return jax.shard_map(
        body,
        mesh=mesh,
        in_specs=placed,
        out_specs=(P(ranges, None), P(None, ranges, None)),
        check_vma=False,
    )
```

```python
import jax
import jax.numpy as jnp
from jax import lax
from jax.experimental import pallas as pl
from jax.experimental.pallas import tpu as pltpu
from jax.sharding import PartitionSpec as P

K = 8
STEPS = 4
W = 4
EDGE = 4

COEFF_H = 0.15
COEFF_V = 0.1
COEFF_Q = 0.5
EPSILON = 1e-05

F32 = jnp.float32
BF16 = jnp.bfloat16
AXES = ("tile", "comp")


INNER, OUTER = (1, -1), (-1, 1)
NEAR, FAR = (2, 2, -2, -2), (-2, -2, 2, 2)


def sent(block, offsets):
    count = lax.axis_size(AXES)
    route = [(i, (i + offsets[i % len(offsets)]) % count) for i in range(count)]
    return lax.ppermute(block, AXES, route)


def is_even():
    return lax.axis_index("comp") == 0


def pair_is_even():
    return lax.rem(lax.axis_index("tile"), 2) == 0


def dot(a, b):
    return jnp.dot(a, b, preferred_element_type=F32)


def dot_nt(a, b):
    return lax.dot_general(a, b, (((1,), (1,)), ((), ())), preferred_element_type=F32)


def silu(v):
    half = 0.5 * v
    return half + half * jnp.tanh(half)


def one_hot(test):
    return jnp.where(test, 1.0, 0.0).astype(BF16)


def iota(shape, dim):
    return lax.broadcasted_iota(jnp.int32, shape, dim)


def started(pairs, sems):
    copies = [pltpu.make_async_copy(a, b, sems.at[i]) for i, (a, b) in enumerate(pairs)]
    for copy in copies:
        copy.start()
    return copies


def pack_kernel(
    counts_in, heat_in, east_in, north_in, mask_in, inner_out, outer_out, blocks_out,
    counts, heat, east, north, mask, sems,
):
    copies = started(
        ((counts_in, counts), (heat_in, heat), (mask_in, mask), (east_in, east), (north_in, north)), sems
    )
    for copy in copies:
        copy.wait()
    columns, rows = mask.shape
    wet = mask[...].astype(F32)
    triples = columns // 3

    def over_columns(x):
        return jnp.concatenate([x[3 * t] + x[3 * t + 1] + x[3 * t + 2] for t in range(triples)], axis=0)

    wet_rows = [wet[c : c + 1] for c in range(columns)]
    sums = over_columns([heat[c, 0:1] * wet_rows[c] for c in range(columns)])
    first = sums.astype(BF16).astype(F32)
    second = (sums - first).astype(BF16).astype(F32)
    third = sums - first - second
    parts = jnp.concatenate(
        [first, second, third, over_columns(wet_rows), jnp.zeros((16 - 4 * triples, rows), F32)], axis=0
    ).astype(BF16)
    pick = one_hot(iota((rows, rows // 3), 0) // 3 == iota((rows, rows // 3), 1))
    folded = dot(parts, pick)

    def flat(x):
        return jnp.concatenate([x[t : t + 1] for t in range(triples)], axis=1)

    t = triples
    total = flat(folded[:t] + folded[t : 2 * t] + folded[2 * t : 3 * t])
    number = flat(folded[3 * t : 4 * t])
    mean = total / jnp.maximum(number, 1.0)
    mean_high = mean.astype(BF16).astype(F32)
    flags = jnp.where(number > 0.5, 1.0, 0.0)
    lane = iota((1, rows), 1)
    held = jnp.zeros((1, rows), F32)
    for o in range(W):
        held = jnp.where(lane == o, counts[0, o].astype(F32), held)
    bundle = jnp.concatenate(
        [mean_high, mean - mean_high, flags, held, jnp.zeros((4, rows), F32)], axis=0
    )
    blank = jnp.zeros((4, rows), F32)
    ends = []
    for begin in (0, columns - EDGE):
        pieces = [source[c] for source in (heat, east, north) for c in range(begin, begin + EDGE)]
        pieces += [wet[begin : begin + EDGE], blank, bundle]
        ends.append(jnp.concatenate(pieces, axis=0))
    even = is_even()
    inner_out[...] = jnp.where(even, ends[1], ends[0]).astype(BF16)
    outer_out[...] = jnp.where(even, ends[0], ends[1]).astype(BF16)
    blocks_out[...] = jnp.concatenate([bundle, jnp.zeros((8, rows), F32)], axis=0).astype(BF16)


def members(nodes, grid_row):
    return one_hot(iota((nodes, grid_row.shape[1]), 0) == grid_row)


def plain_kernel(atmosphere, w_encode, grid_row, mesh_state, plain_out):
    member = members(mesh_state.shape[0], grid_row[...])
    population = jnp.sum(member.astype(F32), axis=1, keepdims=True)
    state = atmosphere[...]
    state = jnp.where(iota(state.shape, 0) == 0, 0.0, state.astype(F32)).astype(BF16)
    pooled = dot_nt(member, state) / jnp.maximum(population, 1.0)
    pooled_high = pooled.astype(BF16)
    pooled_low = (pooled - pooled_high.astype(F32)).astype(BF16)
    encode = w_encode[...]
    plain_out[...] = mesh_state[...].astype(F32) + dot(pooled_high, encode) + dot(pooled_low, encode)


def rolled_points(points, starts):
    rows = 2 * points.shape[1]
    empty = jnp.full((1, rows - points.shape[1]), 1 << 20, jnp.int32)
    return [
        pltpu.roll(jnp.concatenate([points[o : o + 1, :], empty], axis=1), starts[o], 1) for o in range(W)
    ]


def before(bundle_rows, o):
    lane = iota((1, bundle_rows.shape[1]), 1)
    return jnp.sum(jnp.where(lane < o, bundle_rows[3:4], 0.0)).astype(jnp.int32)


def latent_kernel(
    outer, far, inner, own, points, atmosphere, w_encode, grid_row, plain,
    latent_out, surface_out, placed_out,
):
    pair = [x[...].astype(F32)[-8:] for x in (inner, outer)]
    even = is_even()
    parts = [
        far[...].astype(F32)[:8],
        jnp.where(even, pair[0], pair[1]),
        own[...].astype(F32)[:8],
        jnp.where(even, pair[1], pair[0]),
    ]
    starts = [0, before(parts[1], 1), before(parts[2], 2), before(parts[3], 3)]
    placed = jnp.concatenate(rolled_points(points, starts), axis=1)
    placed_out[...] = placed
    n_points = grid_row.shape[1]
    values = jnp.concatenate(parts, axis=1).astype(BF16)
    match = one_hot(iota((n_points, placed.shape[1]), 0) == placed)
    sums = dot_nt(values, match)
    total = sums[0:1] + sums[1:2]
    number = sums[2:3]
    surface = jnp.where(
        number > 0.5, total / jnp.maximum(number, 1.0), atmosphere[0:16].astype(F32)[0:1]
    )
    surface_out[...] = surface
    pair = jnp.concatenate([surface, jnp.ones((7, n_points), F32)], axis=0).astype(BF16)
    pooled = dot_nt(members(plain.shape[0], grid_row[...]), pair)
    share = pooled[:, 0:1] / jnp.maximum(pooled[:, 1:2], 1.0)
    latent_out[...] = (plain[...] + share * w_encode[0:16].astype(F32)[0:1]).astype(BF16)


def listed_slots(neighbours):
    return neighbours[...].astype(F32).T


def slot_senders(listed, k):
    lane = iota(listed.shape, 1)
    return jnp.sum(jnp.where(lane == k, listed, 0.0), axis=1, keepdims=True).astype(jnp.int32)


def own_kernel(
    latent, w_in, geometry, w_geometry, neighbours, w_node_in, pre_out, base_out, node_out, sender, turned,
):
    nodes, features = latent.shape
    value = latent[...]
    sender[...] = dot(value, w_in[features : 2 * features]).astype(BF16)
    receiver = dot(value, w_in[2 * features :])
    node_out[...] = dot(value, w_node_in[:features])
    listed = listed_slots(neighbours)
    blank = jnp.zeros((4, geometry.shape[1]), F32)
    turned[:, :8] = jnp.concatenate([geometry[...].astype(F32), blank], axis=0).T
    blank = jnp.zeros((4, features), F32)
    w_geo = jnp.concatenate([w_geometry[...].astype(F32), blank], axis=0).astype(BF16)
    base = jnp.zeros((nodes, features), F32)
    for k in range(K):
        at = slot_senders(listed, k)
        edge = silu(dot(turned[pl.ds(k, nodes, stride=K), :8].astype(BF16), w_geo)).astype(BF16)
        match = one_hot(iota((nodes, nodes), 1) + nodes == at)
        joined = dot(edge, w_in[:features]) + dot(match, sender[...])
        pre_out[k] = (joined + receiver).astype(BF16)
        base = base + jnp.where(at < 3 * nodes, edge.astype(F32), 0.0)
    base_out[...] = base


def normal(values):
    average = jnp.mean(values, axis=-1, keepdims=True)
    centred = values - average
    variance = jnp.mean(centred * centred, axis=-1, keepdims=True)
    return centred, lax.rsqrt(variance + EPSILON)


def mesh_kernel(
    inner, outer, latent, w_in, w_out, pre, base, node_part, neighbours, w_node_in, w_node_out, w_decode,
    gain_edge, gain_node, grid_row, atmosphere, placed, node_out, flux_out, sender, total,
):
    nodes, features = latent.shape
    w_sender = w_in[features : 2 * features]
    sender[:nodes] = dot(inner[...], w_sender).astype(BF16)
    sender[nodes:] = dot(outer[...], w_sender).astype(BF16)
    below = jnp.where(is_even(), nodes, 0)
    above = nodes - below
    listed = listed_slots(neighbours)
    total[...] = jnp.zeros((nodes, features), F32)

    def step(k, carry):
        at = slot_senders(listed, k)
        place = jnp.where(at < nodes, at + below, jnp.where(at >= 2 * nodes, at - 2 * nodes + above, -1))
        place = jnp.where(at < 3 * nodes, place, -1)
        match = one_hot(iota((nodes, 2 * nodes), 1) == place)
        hidden = silu((pre[k].astype(F32) + dot(match, sender[...])).astype(BF16))
        centred, scale = normal(dot(hidden, w_out[...]))
        total[...] += centred * jnp.where(at < 3 * nodes, scale, 0.0)
        return carry

    lax.fori_loop(0, K, step, 0, unroll=True)
    aggregate = (base[...] + total[...] * gain_edge[...]).astype(BF16)
    hidden = silu(node_part[...] + dot(aggregate, w_node_in[features:])).astype(BF16)
    centred, scale = normal(dot(hidden, w_node_out[...]))
    node_new = (latent[...].astype(F32) + centred * scale * gain_node[...]).astype(BF16)
    node_out[...] = node_new
    flux = two_parts(dot_nt(w_decode[0:16], node_new)[1:2])
    flux = dot(flux, members(nodes, grid_row[...]))
    flux = atmosphere[0:16].astype(F32)[1:2] + flux[0:1] + flux[1:2]
    n_points = flux.shape[1]
    match = one_hot(iota((n_points, placed.shape[1]), 0) == placed[...])
    spread = dot(jnp.broadcast_to(flux, (8, n_points)).astype(BF16), match)
    rows = placed.shape[1] // W
    out = jnp.zeros((8, rows), F32)
    for o in range(W):
        out = jnp.where(iota((8, rows), 0) == o, spread[:, o * rows : (o + 1) * rows], out)
    flux_out[...] = jnp.concatenate([out, jnp.zeros((8, rows), F32)], axis=0).astype(BF16)


def two_parts(row):
    high = row.astype(BF16).astype(F32)
    return jnp.concatenate([high, row - high, jnp.zeros((6, row.shape[1]), F32)], axis=0).astype(BF16)


def decode_kernel(node_new, w_decode, grid_row, atmosphere, surface, state_out):
    change = dot_nt(w_decode[...], node_new[...])
    change_high = change.astype(BF16)
    change_low = (change - change_high.astype(F32)).astype(BF16)
    member = members(node_new.shape[0], grid_row[...])
    state = atmosphere[...].astype(F32)
    state = jnp.where(iota(state.shape, 0) == 0, surface[...].astype(BF16).astype(F32), state)
    state_out[...] = (state + dot(change_high, member) + dot(change_low, member)).astype(BF16)


def ready_kernel(heat, east, north, mask, inner, outer, field_out, wet_out, px_out, qx_out, py_out, qy_out, mix_out):
    columns, rows = mask.shape
    levels = heat.shape[1]
    pair = inner[...].astype(F32), outer[...].astype(F32)
    even = is_even()
    below, above = jnp.where(even, pair[1], pair[0]), jnp.where(even, pair[0], pair[1])
    own_wet = mask[...].astype(F32)

    def wide(source, at):
        left = [below[8 * (at * EDGE + c) : 8 * (at * EDGE + c) + 8] for c in range(EDGE)]
        right = [above[8 * (at * EDGE + c) : 8 * (at * EDGE + c) + 8] for c in range(EDGE)]
        return left + [source[c] for c in range(columns)] + right

    base = 3 * 8 * EDGE
    wet = [below[base + c : base + c + 1] for c in range(EDGE)]
    wet += [own_wet[c : c + 1] for c in range(columns)]
    wet += [above[base + c : base + c + 1] for c in range(EDGE)]
    wet = [jnp.broadcast_to(w, (levels, rows)) for w in wet]
    field, u, v = wide(heat, 0), wide(east, 1), wide(north, 2)
    lane = iota((levels, rows), 1)
    level = iota((levels, rows), 0)
    count = len(field)
    for c in range(count):
        field_out[c] = field[c]
        wet_out[c] = wet[c]
        mix_out[c] = jnp.where(level < levels - 1, COEFF_V * wet[c], 0.0)
        if c + 1 < count:
            opened = wet[c] * wet[c + 1]
            face = 0.25 * (u[c] + u[c + 1])
            px_out[c] = opened * (face + COEFF_H)
            qx_out[c] = opened * (face - COEFF_H)
        opened = jnp.where(lane < rows - 1, wet[c] * pltpu.roll(wet[c], rows - 1, 1), 0.0)
        face = 0.25 * (v[c] + pltpu.roll(v[c], rows - 1, 1))
        py_out[c] = opened * (face + COEFF_H)
        qy_out[c] = opened * (face - COEFF_H)


def ocean_kernel(before_1, before_3, far, after_1, near, here_flux, field_in, wet, px, qx, py, qy, mix, out):
    count, levels, rows = field_in.shape
    columns = count - 2 * EDGE
    triples = columns // 3
    span = rows // 3
    before_1, before_3, far, after_1, near, here_flux = (
        x[...].astype(F32) for x in (before_1, before_3, far, after_1, near, here_flux)
    )
    even = pair_is_even()
    before_2, after_2 = jnp.where(even, far, near), jnp.where(even, near, far)
    fluxes = [before_3, before_2, before_1, here_flux, after_1, after_2]

    def gathered(begin):
        return sum(fluxes[begin + o][o : o + 1] for o in range(W))

    own = gathered(1)
    blocks = [gathered(0)[:, (triples - 1) * span :]]
    blocks += [own[:, t * span : (t + 1) * span] for t in range(triples)]
    blocks += [gathered(2)[:, :span]]
    blocks += [jnp.zeros((16 - len(blocks), span), F32)]
    expand = one_hot(iota((span, rows), 1) // 3 == iota((span, rows), 0))
    cells = COEFF_Q * dot(jnp.concatenate(blocks, axis=0).astype(BF16), expand)
    level = iota((levels, rows), 0)
    surface = [
        jnp.where(level == 0, jnp.broadcast_to(cells[t : t + 1], (levels, rows)), 0.0)
        for t in range(triples + 2)
    ]
    field = [field_in[c] for c in range(count)]
    for step in range(STEPS):
        begin, end = step + 1, count - step - 1
        across = {c: px[c] * field[c] + qx[c] * field[c + 1] for c in range(begin - 1, end)}
        later = [None] * count
        for c in range(begin, end):
            here = field[c]
            along = py[c] * here + qy[c] * pltpu.roll(here, rows - 1, 1)
            mixed = mix[c] * (pltpu.roll(here, levels - 1, 0) - here)
            group = (c - EDGE + 3) // 3
            change = (
                (across[c - 1] - across[c])
                + (pltpu.roll(along, 1, 1) - along)
                + (mixed - pltpu.roll(mixed, 1, 0))
            )
            later[c] = wet[c] * (here + change + surface[group])
        field = later
    for c in range(columns):
        out[c] = field[EDGE + c]


VMEM = pl.BlockSpec(memory_space=pltpu.VMEM)
HBM = pl.BlockSpec(memory_space=pltpu.HBM)


def call(kernel, outs, inputs, spec=VMEM, scratch=(), flops=0, bytes_accessed=1 << 20, name=None):
    if spec is HBM:
        inputs = [pltpu.with_memory_space_constraint(x, pltpu.HBM) for x in inputs]
    return pl.pallas_call(
        kernel,
        out_shape=[jax.ShapeDtypeStruct(s, t) for s, t in outs],
        in_specs=[spec] * len(inputs),
        out_specs=[VMEM] * len(outs),
        scratch_shapes=list(scratch),
        compiler_params=pltpu.CompilerParams(vmem_limit_bytes=40 << 20),
        cost_estimate=pl.CostEstimate(flops=flops, bytes_accessed=bytes_accessed, transcendentals=0),
        name=name,
    )(*inputs)


def body(
    atmosphere,
    mesh_state,
    edge_geometry,
    neighbours,
    grid_node,
    ocean_heat_field,
    east_velocity,
    north_velocity,
    ocean_mask,
    intersection_points,
    intersection_counts,
    w_geometry,
    w_encode,
    w_edge_in,
    w_edge_out,
    w_node_in,
    w_node_out,
    w_decode,
    gain_edge,
    gain_node,
):
    levels, columns, rows = ocean_heat_field.shape
    nodes, features = mesh_state.shape
    n_points, channels = atmosphere.shape
    heat, east, north = (
        x.transpose(1, 0, 2) for x in (ocean_heat_field, east_velocity, north_velocity)
    )
    atmosphere_t = atmosphere.T
    slots = neighbours.T
    grid_row = grid_node.reshape(1, n_points)
    decode_t = w_decode.T
    ends = (3 * levels * EDGE + 16, rows)
    few = (16, rows)
    own_ocean = (columns, levels, rows)
    to_inner, to_outer, blocks = call(
        pack_kernel,
        [(ends, BF16), (ends, BF16), (few, BF16)],
        [intersection_counts, heat, east, north, ocean_mask],
        spec=HBM,
        scratch=[
            pltpu.SMEM((1, W), jnp.int32),
            pltpu.VMEM(own_ocean, F32),
            pltpu.VMEM(own_ocean, F32),
            pltpu.VMEM(own_ocean, F32),
            pltpu.VMEM((columns, rows), jnp.int32),
            pltpu.SemaphoreType.DMA((5,)),
        ],
        flops=2 * K * nodes * features * features,
        bytes_accessed=8 << 20,
        name="pack",
    )
    outer = sent(to_outer, OUTER)
    far = sent(blocks, (-2,))
    inner = sent(to_inner, INNER)
    (plain,) = call(
        plain_kernel,
        [((nodes, features), F32)],
        [atmosphere_t, w_encode, grid_row, mesh_state],
        flops=2 * K * nodes * features * features,
        bytes_accessed=8 << 20,
        name="plain",
    )
    latent, surface, placed = call(
        latent_kernel,
        [((nodes, features), BF16), ((1, n_points), F32), ((1, W * rows), jnp.int32)],
        [outer, far, inner, blocks, intersection_points[0], atmosphere_t, w_encode, grid_row, plain],
        name="latents",
    )
    latent_inner = sent(latent, INNER)
    latent_outer = sent(latent, OUTER)
    pre, base, node_part = call(
        own_kernel,
        [((K, nodes, features), BF16), ((nodes, features), F32), ((nodes, features), F32)],
        [latent, w_edge_in, edge_geometry, w_geometry, slots, w_node_in],
        scratch=[pltpu.VMEM((nodes, features), BF16), pltpu.VMEM((K * nodes, 128), F32)],
        flops=2 * K * nodes * (nodes + features) * features,
        bytes_accessed=10 << 20,
        name="own",
    )
    wide = (columns + 2 * EDGE, levels, rows)
    ready = call(
        ready_kernel,
        [(wide, F32)] * 7,
        [heat, east, north, ocean_mask, inner, outer],
        bytes_accessed=4 << 20,
        name="ready",
    )
    node_new, flux = call(
        mesh_kernel,
        [((nodes, features), BF16), (few, BF16)],
        [
            latent_inner, latent_outer, latent, w_edge_in, w_edge_out, pre, base, node_part, slots,
            w_node_in, w_node_out, decode_t, gain_edge.reshape(1, features),
            gain_node.reshape(1, features), grid_row, atmosphere_t, placed,
        ],
        scratch=[pltpu.VMEM((2 * nodes, features), BF16), pltpu.VMEM((nodes, features), F32)],
        flops=2 * K * nodes * 3 * nodes * features,
        bytes_accessed=10 << 20,
        name="mesh",
    )
    arrived = [sent(flux, route) for route in ((1,), (3,), FAR, (-1,), NEAR)]
    (state,) = call(
        decode_kernel,
        [((channels, n_points), BF16)],
        [node_new, decode_t, grid_row, atmosphere_t, surface],
        flops=6 * nodes * channels * n_points,
        name="decode",
    )
    (ocean_new,) = call(
        ocean_kernel,
        [(own_ocean, F32)],
        [*arrived, flux, *ready],
        bytes_accessed=4 << 20,
        name="ocean",
    )
    return (state.T, ocean_new.transpose(1, 0, 2))


def solution(mesh):
    ranges = ("member", "tile", "comp")
    placed = (
        P(ranges, None),
        P(ranges, None),
        P(None, ranges),
        P(ranges, None),
        P(ranges),
        P(None, ranges, None),
        P(None, ranges, None),
        P(None, ranges, None),
        P(ranges, None),
        P(ranges, None, None),
        P(ranges, None),
        P(),
        P(),
        P(),
        P(),
        P(),
        P(),
        P(),
        P(),
        P(),
    )
    return jax.shard_map(
        body,
        mesh=mesh,
        in_specs=placed,
        out_specs=(P(ranges, None), P(None, ranges, None)),
        check_vma=False,
    )
```

```python
import jax
import jax.numpy as jnp
from jax import lax
from jax.experimental import pallas as pl
from jax.experimental.pallas import tpu as pltpu
from jax.sharding import PartitionSpec as P

K = 8
STEPS = 4
W = 4
EDGE = 4

COEFF_H = 0.15
COEFF_V = 0.1
COEFF_Q = 0.5
EPSILON = 1e-05

F32 = jnp.float32
BF16 = jnp.bfloat16
AXES = ("tile", "comp")


INNER, OUTER = (1, -1), (-1, 1)
NEAR, FAR = (2, 2, -2, -2), (-2, -2, 2, 2)


def sent(block, offsets):
    count = lax.axis_size(AXES)
    route = [(i, (i + offsets[i % len(offsets)]) % count) for i in range(count)]
    return lax.ppermute(block, AXES, route)


def is_even():
    return lax.axis_index("comp") == 0


def pair_is_even():
    return lax.rem(lax.axis_index("tile"), 2) == 0


def dot(a, b):
    return jnp.dot(a, b, preferred_element_type=F32)


def dot_nt(a, b):
    return lax.dot_general(a, b, (((1,), (1,)), ((), ())), preferred_element_type=F32)


def silu(v):
    half = 0.5 * v
    return half + half * jnp.tanh(half)


def one_hot(test):
    return jnp.where(test, 1.0, 0.0).astype(BF16)


def iota(shape, dim):
    return lax.broadcasted_iota(jnp.int32, shape, dim)


def started(pairs, sems):
    copies = [pltpu.make_async_copy(a, b, sems.at[i]) for i, (a, b) in enumerate(pairs)]
    for copy in copies:
        copy.start()
    return copies


def pack_kernel(
    counts_in, heat_in, east_in, north_in, mask_in, inner_out, outer_out, blocks_out,
    counts, heat, east, north, mask, sems,
):
    copies = started(
        ((counts_in, counts), (heat_in, heat), (mask_in, mask), (east_in, east), (north_in, north)), sems
    )
    for copy in copies:
        copy.wait()
    columns, rows = mask.shape
    wet = mask[...].astype(F32)
    triples = columns // 3

    def over_columns(x):
        return jnp.concatenate([x[3 * t] + x[3 * t + 1] + x[3 * t + 2] for t in range(triples)], axis=0)

    wet_rows = [wet[c : c + 1] for c in range(columns)]
    sums = over_columns([heat[c, 0:1] * wet_rows[c] for c in range(columns)])
    first = sums.astype(BF16).astype(F32)
    second = (sums - first).astype(BF16).astype(F32)
    third = sums - first - second
    parts = jnp.concatenate(
        [first, second, third, over_columns(wet_rows), jnp.zeros((16 - 4 * triples, rows), F32)], axis=0
    ).astype(BF16)
    pick = one_hot(iota((rows, rows // 3), 0) // 3 == iota((rows, rows // 3), 1))
    folded = dot(parts, pick)

    def flat(x):
        return jnp.concatenate([x[t : t + 1] for t in range(triples)], axis=1)

    t = triples
    total = flat(folded[:t] + folded[t : 2 * t] + folded[2 * t : 3 * t])
    number = flat(folded[3 * t : 4 * t])
    mean = total / jnp.maximum(number, 1.0)
    mean_high = mean.astype(BF16).astype(F32)
    flags = jnp.where(number > 0.5, 1.0, 0.0)
    lane = iota((1, rows), 1)
    held = jnp.zeros((1, rows), F32)
    for o in range(W):
        held = jnp.where(lane == o, counts[0, o].astype(F32), held)
    bundle = jnp.concatenate(
        [mean_high, mean - mean_high, flags, held, jnp.zeros((4, rows), F32)], axis=0
    )
    blank = jnp.zeros((4, rows), F32)
    ends = []
    for begin in (0, columns - EDGE):
        pieces = [source[c] for source in (heat, east, north) for c in range(begin, begin + EDGE)]
        pieces += [wet[begin : begin + EDGE], blank, bundle]
        ends.append(jnp.concatenate(pieces, axis=0))
    even = is_even()
    inner_out[...] = jnp.where(even, ends[1], ends[0]).astype(BF16)
    outer_out[...] = jnp.where(even, ends[0], ends[1]).astype(BF16)
    blocks_out[...] = jnp.concatenate([bundle, jnp.zeros((8, rows), F32)], axis=0).astype(BF16)


def members(nodes, grid_row):
    return one_hot(iota((nodes, grid_row.shape[1]), 0) == grid_row)


def plain_kernel(after, atmosphere, w_encode, grid_row, mesh_state, plain_out, early_out):
    del after
    member = members(mesh_state.shape[0], grid_row[...])
    population = jnp.sum(member.astype(F32), axis=1, keepdims=True)
    state = atmosphere[...]
    state = jnp.where(iota(state.shape, 0) == 0, 0.0, state.astype(F32)).astype(BF16)
    pooled = dot_nt(member, state) / jnp.maximum(population, 1.0)
    pooled_high = pooled.astype(BF16)
    pooled_low = (pooled - pooled_high.astype(F32)).astype(BF16)
    encode = w_encode[...]
    plain = mesh_state[...].astype(F32) + dot(pooled_high, encode) + dot(pooled_low, encode)
    plain_out[...] = plain
    early_out[...] = plain.astype(BF16)


def rolled_points(points, starts):
    rows = 2 * points.shape[1]
    empty = jnp.full((1, rows - points.shape[1]), 1 << 20, jnp.int32)
    return [
        pltpu.roll(jnp.concatenate([points[o : o + 1, :], empty], axis=1), starts[o], 1) for o in range(W)
    ]


def before(bundle_rows, o):
    lane = iota((1, bundle_rows.shape[1]), 1)
    return jnp.sum(jnp.where(lane < o, bundle_rows[3:4], 0.0)).astype(jnp.int32)


def latent_kernel(
    outer, far, inner, own, points, atmosphere, w_encode, grid_row, plain,
    latent_out, share_out, surface_out, placed_out,
):
    pair = [x[...].astype(F32)[-8:] for x in (inner, outer)]
    even = is_even()
    parts = [
        far[...].astype(F32)[:8],
        jnp.where(even, pair[0], pair[1]),
        own[...].astype(F32)[:8],
        jnp.where(even, pair[1], pair[0]),
    ]
    starts = [0, before(parts[1], 1), before(parts[2], 2), before(parts[3], 3)]
    placed = jnp.concatenate(rolled_points(points, starts), axis=1)
    placed_out[...] = placed
    n_points = grid_row.shape[1]
    values = jnp.concatenate(parts, axis=1).astype(BF16)
    match = one_hot(iota((n_points, placed.shape[1]), 0) == placed)
    sums = dot_nt(values, match)
    total = sums[0:1] + sums[1:2]
    number = sums[2:3]
    surface = jnp.where(
        number > 0.5, total / jnp.maximum(number, 1.0), atmosphere[0:16].astype(F32)[0:1]
    )
    surface_out[...] = surface
    pair = jnp.concatenate([surface, jnp.ones((7, n_points), F32)], axis=0).astype(BF16)
    member = members(plain.shape[0], grid_row[...])
    pooled = dot_nt(pair, member)
    share = two_parts(pooled[0:1] / jnp.maximum(pooled[1:2], 1.0)).astype(F32)
    share_out[...] = jnp.concatenate([share, jnp.zeros(share.shape, F32)], axis=0).astype(BF16)
    pooled = dot_nt(member, pair)
    share = pooled[:, 0:1] / jnp.maximum(pooled[:, 1:2], 1.0)
    latent_out[...] = (plain[...] + share * w_encode[0:16].astype(F32)[0:1]).astype(BF16)


def listed_slots(neighbours):
    return neighbours[...].astype(F32).T


def slot_senders(listed, k):
    lane = iota(listed.shape, 1)
    return jnp.sum(jnp.where(lane == k, listed, 0.0), axis=1, keepdims=True).astype(jnp.int32)


def own_kernel(
    latent, w_in, geometry, w_geometry, neighbours, w_node_in, pre_out, base_out, node_out, sender, turned,
):
    nodes, features = latent.shape
    value = latent[...]
    sender[...] = dot(value, w_in[features : 2 * features]).astype(BF16)
    receiver = dot(value, w_in[2 * features :])
    node_out[...] = dot(value, w_node_in[:features])
    listed = listed_slots(neighbours)
    blank = jnp.zeros((4, geometry.shape[1]), F32)
    turned[:, :8] = jnp.concatenate([geometry[...].astype(F32), blank], axis=0).T
    blank = jnp.zeros((4, features), F32)
    w_geo = jnp.concatenate([w_geometry[...].astype(F32), blank], axis=0).astype(BF16)
    base = jnp.zeros((nodes, features), F32)
    for k in range(K):
        at = slot_senders(listed, k)
        edge = silu(dot(turned[pl.ds(k, nodes, stride=K), :8].astype(BF16), w_geo)).astype(BF16)
        match = one_hot(iota((nodes, nodes), 1) + nodes == at)
        joined = dot(edge, w_in[:features]) + dot(match, sender[...])
        pre_out[k] = (joined + receiver).astype(BF16)
        base = base + jnp.where(at < 3 * nodes, edge.astype(F32), 0.0)
    base_out[...] = base


def normal(values):
    average = jnp.mean(values, axis=-1, keepdims=True)
    centred = values - average
    variance = jnp.mean(centred * centred, axis=-1, keepdims=True)
    return centred, lax.rsqrt(variance + EPSILON)


def mesh_kernel(
    inner, outer, inner_share, outer_share, w_encode, latent, w_in, w_out, pre, base, node_part, neighbours, w_node_in, w_node_out, w_decode,
    gain_edge, gain_node, grid_row, atmosphere, placed, node_out, flux_out, sender, total,
):
    nodes, features = latent.shape
    w_sender = w_in[features : 2 * features]
    surface_sender = dot(w_encode[0:16], w_sender)[0:1]
    for begin, early, share in ((0, inner, inner_share), (nodes, outer, outer_share)):
        parts = share[...].astype(F32)[:8].T
        product = dot(early[...], w_sender) + (parts[:, 0:1] + parts[:, 1:2]) * surface_sender
        sender[begin : begin + nodes] = product.astype(BF16)
    below = jnp.where(is_even(), nodes, 0)
    above = nodes - below
    listed = listed_slots(neighbours)
    total[...] = jnp.zeros((nodes, features), F32)

    def step(k, carry):
        at = slot_senders(listed, k)
        place = jnp.where(at < nodes, at + below, jnp.where(at >= 2 * nodes, at - 2 * nodes + above, -1))
        place = jnp.where(at < 3 * nodes, place, -1)
        match = one_hot(iota((nodes, 2 * nodes), 1) == place)
        hidden = silu((pre[k].astype(F32) + dot(match, sender[...])).astype(BF16))
        centred, scale = normal(dot(hidden, w_out[...]))
        total[...] += centred * jnp.where(at < 3 * nodes, scale, 0.0)
        return carry

    lax.fori_loop(0, K, step, 0, unroll=True)
    aggregate = (base[...] + total[...] * gain_edge[...]).astype(BF16)
    hidden = silu(node_part[...] + dot(aggregate, w_node_in[features:])).astype(BF16)
    centred, scale = normal(dot(hidden, w_node_out[...]))
    node_new = (latent[...].astype(F32) + centred * scale * gain_node[...]).astype(BF16)
    node_out[...] = node_new
    flux = two_parts(dot_nt(w_decode[0:16], node_new)[1:2])
    flux = dot(flux, members(nodes, grid_row[...]))
    flux = atmosphere[0:16].astype(F32)[1:2] + flux[0:1] + flux[1:2]
    n_points = flux.shape[1]
    match = one_hot(iota((n_points, placed.shape[1]), 0) == placed[...])
    spread = dot(jnp.broadcast_to(flux, (8, n_points)).astype(BF16), match)
    rows = placed.shape[1] // W
    out = jnp.zeros((8, rows), F32)
    for o in range(W):
        out = jnp.where(iota((8, rows), 0) == o, spread[:, o * rows : (o + 1) * rows], out)
    flux_out[...] = jnp.concatenate([out, jnp.zeros((8, rows), F32)], axis=0).astype(BF16)


def two_parts(row):
    high = row.astype(BF16).astype(F32)
    return jnp.concatenate([high, row - high, jnp.zeros((6, row.shape[1]), F32)], axis=0).astype(BF16)


def decode_kernel(node_new, w_decode, grid_row, atmosphere, surface, state_out):
    change = dot_nt(w_decode[...], node_new[...])
    change_high = change.astype(BF16)
    change_low = (change - change_high.astype(F32)).astype(BF16)
    member = members(node_new.shape[0], grid_row[...])
    state = atmosphere[...].astype(F32)
    state = jnp.where(iota(state.shape, 0) == 0, surface[...].astype(BF16).astype(F32), state)
    state_out[...] = (state + dot(change_high, member) + dot(change_low, member)).astype(BF16)


def ready_kernel(heat, east, north, mask, inner, outer, field_out, wet_out, px_out, qx_out, py_out, qy_out, mix_out):
    columns, rows = mask.shape
    levels = heat.shape[1]
    pair = inner[...].astype(F32), outer[...].astype(F32)
    even = is_even()
    below, above = jnp.where(even, pair[1], pair[0]), jnp.where(even, pair[0], pair[1])
    own_wet = mask[...].astype(F32)

    def wide(source, at):
        left = [below[8 * (at * EDGE + c) : 8 * (at * EDGE + c) + 8] for c in range(EDGE)]
        right = [above[8 * (at * EDGE + c) : 8 * (at * EDGE + c) + 8] for c in range(EDGE)]
        return left + [source[c] for c in range(columns)] + right

    base = 3 * 8 * EDGE
    wet = [below[base + c : base + c + 1] for c in range(EDGE)]
    wet += [own_wet[c : c + 1] for c in range(columns)]
    wet += [above[base + c : base + c + 1] for c in range(EDGE)]
    wet = [jnp.broadcast_to(w, (levels, rows)) for w in wet]
    field, u, v = wide(heat, 0), wide(east, 1), wide(north, 2)
    lane = iota((levels, rows), 1)
    level = iota((levels, rows), 0)
    count = len(field)
    for c in range(count):
        field_out[c] = field[c]
        wet_out[c] = wet[c]
        mix_out[c] = jnp.where(level < levels - 1, COEFF_V * wet[c], 0.0)
        if c + 1 < count:
            opened = wet[c] * wet[c + 1]
            face = 0.25 * (u[c] + u[c + 1])
            px_out[c] = opened * (face + COEFF_H)
            qx_out[c] = opened * (face - COEFF_H)
        opened = jnp.where(lane < rows - 1, wet[c] * pltpu.roll(wet[c], rows - 1, 1), 0.0)
        face = 0.25 * (v[c] + pltpu.roll(v[c], rows - 1, 1))
        py_out[c] = opened * (face + COEFF_H)
        qy_out[c] = opened * (face - COEFF_H)


def ocean_kernel(far, after_1, near, before_1, before_3, here_flux, field_in, wet, px, qx, py, qy, mix, out):
    count, levels, rows = field_in.shape
    columns = count - 2 * EDGE
    triples = columns // 3
    span = rows // 3
    far, after_1, near, before_1, before_3, here_flux = (
        x[...].astype(F32) for x in (far, after_1, near, before_1, before_3, here_flux)
    )
    even = pair_is_even()
    before_2, after_2 = jnp.where(even, far, near), jnp.where(even, near, far)
    fluxes = [before_3, before_2, before_1, here_flux, after_1, after_2]

    def gathered(begin):
        return sum(fluxes[begin + o][o : o + 1] for o in range(W))

    own = gathered(1)
    blocks = [gathered(0)[:, (triples - 1) * span :]]
    blocks += [own[:, t * span : (t + 1) * span] for t in range(triples)]
    blocks += [gathered(2)[:, :span]]
    blocks += [jnp.zeros((16 - len(blocks), span), F32)]
    expand = one_hot(iota((span, rows), 1) // 3 == iota((span, rows), 0))
    cells = COEFF_Q * dot(jnp.concatenate(blocks, axis=0).astype(BF16), expand)
    level = iota((levels, rows), 0)
    surface = [
        jnp.where(level == 0, jnp.broadcast_to(cells[t : t + 1], (levels, rows)), 0.0)
        for t in range(triples + 2)
    ]
    field = [field_in[c] for c in range(count)]
    for step in range(STEPS):
        begin, end = step + 1, count - step - 1
        across = {c: px[c] * field[c] + qx[c] * field[c + 1] for c in range(begin - 1, end)}
        later = [None] * count
        for c in range(begin, end):
            here = field[c]
            along = py[c] * here + qy[c] * pltpu.roll(here, rows - 1, 1)
            mixed = mix[c] * (pltpu.roll(here, levels - 1, 0) - here)
            group = (c - EDGE + 3) // 3
            change = (
                (across[c - 1] - across[c])
                + (pltpu.roll(along, 1, 1) - along)
                + (mixed - pltpu.roll(mixed, 1, 0))
            )
            later[c] = wet[c] * (here + change + surface[group])
        field = later
    for c in range(columns):
        out[c] = field[EDGE + c]


VMEM = pl.BlockSpec(memory_space=pltpu.VMEM)
HBM = pl.BlockSpec(memory_space=pltpu.HBM)


def call(kernel, outs, inputs, spec=VMEM, scratch=(), flops=0, bytes_accessed=1 << 20, name=None):
    if spec is HBM:
        inputs = [pltpu.with_memory_space_constraint(x, pltpu.HBM) for x in inputs]
    return pl.pallas_call(
        kernel,
        out_shape=[jax.ShapeDtypeStruct(s, t) for s, t in outs],
        in_specs=[spec] * len(inputs),
        out_specs=[VMEM] * len(outs),
        scratch_shapes=list(scratch),
        compiler_params=pltpu.CompilerParams(vmem_limit_bytes=40 << 20),
        cost_estimate=pl.CostEstimate(flops=flops, bytes_accessed=bytes_accessed, transcendentals=0),
        name=name,
    )(*inputs)


def body(
    atmosphere,
    mesh_state,
    edge_geometry,
    neighbours,
    grid_node,
    ocean_heat_field,
    east_velocity,
    north_velocity,
    ocean_mask,
    intersection_points,
    intersection_counts,
    w_geometry,
    w_encode,
    w_edge_in,
    w_edge_out,
    w_node_in,
    w_node_out,
    w_decode,
    gain_edge,
    gain_node,
):
    levels, columns, rows = ocean_heat_field.shape
    nodes, features = mesh_state.shape
    n_points, channels = atmosphere.shape
    heat, east, north = (
        x.transpose(1, 0, 2) for x in (ocean_heat_field, east_velocity, north_velocity)
    )
    atmosphere_t = atmosphere.T
    slots = neighbours.T
    grid_row = grid_node.reshape(1, n_points)
    decode_t = w_decode.T
    ends = (3 * levels * EDGE + 16, rows)
    few = (16, rows)
    own_ocean = (columns, levels, rows)
    to_inner, to_outer, blocks = call(
        pack_kernel,
        [(ends, BF16), (ends, BF16), (few, BF16)],
        [intersection_counts, heat, east, north, ocean_mask],
        spec=HBM,
        scratch=[
            pltpu.SMEM((1, W), jnp.int32),
            pltpu.VMEM(own_ocean, F32),
            pltpu.VMEM(own_ocean, F32),
            pltpu.VMEM(own_ocean, F32),
            pltpu.VMEM((columns, rows), jnp.int32),
            pltpu.SemaphoreType.DMA((5,)),
        ],
        flops=2 * K * nodes * features * features,
        bytes_accessed=8 << 20,
        name="pack",
    )
    outer = sent(to_outer, OUTER)
    far = sent(blocks, (-2,))
    inner = sent(to_inner, INNER)
    plain, early = call(
        plain_kernel,
        [((nodes, features), F32), ((nodes, features), BF16)],
        [blocks, atmosphere_t, w_encode, grid_row, mesh_state],
        flops=2 * K * nodes * features * features,
        bytes_accessed=8 << 20,
        name="plain",
    )
    early_inner, early_outer = sent(early, INNER), sent(early, OUTER)
    latent, share, surface, placed = call(
        latent_kernel,
        [((nodes, features), BF16), ((16, nodes), BF16), ((1, n_points), F32), ((1, W * rows), jnp.int32)],
        [outer, far, inner, blocks, intersection_points[0], atmosphere_t, w_encode, grid_row, plain],
        flops=8 * K * nodes * features * features,
        name="latents",
    )
    share_inner, share_outer = sent(share, INNER), sent(share, OUTER)
    pre, base, node_part = call(
        own_kernel,
        [((K, nodes, features), BF16), ((nodes, features), F32), ((nodes, features), F32)],
        [latent, w_edge_in, edge_geometry, w_geometry, slots, w_node_in],
        scratch=[pltpu.VMEM((nodes, features), BF16), pltpu.VMEM((K * nodes, 128), F32)],
        flops=8 * 2 * K * nodes * (nodes + features) * features,
        bytes_accessed=10 << 20,
        name="own",
    )
    wide = (columns + 2 * EDGE, levels, rows)
    ready = call(
        ready_kernel,
        [(wide, F32)] * 7,
        [heat, east, north, ocean_mask, inner, outer],
        bytes_accessed=4 << 20,
        name="ready",
    )
    node_new, flux = call(
        mesh_kernel,
        [((nodes, features), BF16), (few, BF16)],
        [
            early_inner, early_outer, share_inner, share_outer, w_encode, latent, w_edge_in, w_edge_out, pre, base, node_part, slots,
            w_node_in, w_node_out, decode_t, gain_edge.reshape(1, features),
            gain_node.reshape(1, features), grid_row, atmosphere_t, placed,
        ],
        scratch=[pltpu.VMEM((2 * nodes, features), BF16), pltpu.VMEM((nodes, features), F32)],
        flops=2 * K * nodes * 3 * nodes * features,
        bytes_accessed=10 << 20,
        name="mesh",
    )
    arrived = [sent(flux, route) for route in (FAR, (-1,), NEAR, (1,), (3,))]
    (state,) = call(
        decode_kernel,
        [((channels, n_points), BF16)],
        [node_new, decode_t, grid_row, atmosphere_t, surface],
        flops=6 * nodes * channels * n_points,
        name="decode",
    )
    (ocean_new,) = call(
        ocean_kernel,
        [(own_ocean, F32)],
        [*arrived, flux, *ready],
        bytes_accessed=4 << 20,
        name="ocean",
    )
    return (state.T, ocean_new.transpose(1, 0, 2))


def solution(mesh):
    ranges = ("member", "tile", "comp")
    placed = (
        P(ranges, None),
        P(ranges, None),
        P(None, ranges),
        P(ranges, None),
        P(ranges),
        P(None, ranges, None),
        P(None, ranges, None),
        P(None, ranges, None),
        P(ranges, None),
        P(ranges, None, None),
        P(ranges, None),
        P(),
        P(),
        P(),
        P(),
        P(),
        P(),
        P(),
        P(),
        P(),
    )
    return jax.shard_map(
        body,
        mesh=mesh,
        in_specs=placed,
        out_specs=(P(ranges, None), P(None, ranges, None)),
        check_vma=False,
    )
```

```python
import jax
import jax.numpy as jnp
from jax import lax
from jax.experimental import pallas as pl
from jax.experimental.pallas import tpu as pltpu
from jax.sharding import PartitionSpec as P

K = 8
STEPS = 4
W = 4
EDGE = 4

COEFF_H = 0.15
COEFF_V = 0.1
COEFF_Q = 0.5
EPSILON = 1e-05

F32 = jnp.float32
BF16 = jnp.bfloat16
AXES = ("tile", "comp")


INNER, OUTER = (1, -1), (-1, 1)
NEAR, FAR = (2, 2, -2, -2), (-2, -2, 2, 2)


def sent(block, offsets):
    count = lax.axis_size(AXES)
    route = [(i, (i + offsets[i % len(offsets)]) % count) for i in range(count)]
    return lax.ppermute(block, AXES, route)


def is_even():
    return lax.axis_index("comp") == 0


def pair_is_even():
    return lax.rem(lax.axis_index("tile"), 2) == 0


def dot(a, b):
    return jnp.dot(a, b, preferred_element_type=F32)


def dot_nt(a, b):
    return lax.dot_general(a, b, (((1,), (1,)), ((), ())), preferred_element_type=F32)


def silu(v):
    half = 0.5 * v
    return half + half * jnp.tanh(half)


def one_hot(test):
    return jnp.where(test, 1.0, 0.0).astype(BF16)


def iota(shape, dim):
    return lax.broadcasted_iota(jnp.int32, shape, dim)


def started(pairs, sems):
    copies = [pltpu.make_async_copy(a, b, sems.at[i]) for i, (a, b) in enumerate(pairs)]
    for copy in copies:
        copy.start()
    return copies


def pack_kernel(
    counts_in, heat_in, east_in, north_in, mask_in, inner_out, outer_out, blocks_out,
    counts, heat, east, north, mask, sems,
):
    copies = started(
        ((counts_in, counts), (heat_in, heat), (mask_in, mask), (east_in, east), (north_in, north)), sems
    )
    for copy in copies:
        copy.wait()
    columns, rows = mask.shape
    wet = mask[...].astype(F32)
    triples = columns // 3

    def over_columns(x):
        return jnp.concatenate([x[3 * t] + x[3 * t + 1] + x[3 * t + 2] for t in range(triples)], axis=0)

    wet_rows = [wet[c : c + 1] for c in range(columns)]
    sums = over_columns([heat[c, 0:1] * wet_rows[c] for c in range(columns)])
    first = sums.astype(BF16).astype(F32)
    second = (sums - first).astype(BF16).astype(F32)
    third = sums - first - second
    parts = jnp.concatenate(
        [first, second, third, over_columns(wet_rows), jnp.zeros((16 - 4 * triples, rows), F32)], axis=0
    ).astype(BF16)
    pick = one_hot(iota((rows, rows // 3), 0) // 3 == iota((rows, rows // 3), 1))
    folded = dot(parts, pick)

    def flat(x):
        return jnp.concatenate([x[t : t + 1] for t in range(triples)], axis=1)

    t = triples
    total = flat(folded[:t] + folded[t : 2 * t] + folded[2 * t : 3 * t])
    number = flat(folded[3 * t : 4 * t])
    mean = total / jnp.maximum(number, 1.0)
    mean_high = mean.astype(BF16).astype(F32)
    flags = jnp.where(number > 0.5, 1.0, 0.0)
    lane = iota((1, rows), 1)
    held = jnp.zeros((1, rows), F32)
    for o in range(W):
        held = jnp.where(lane == o, counts[0, o].astype(F32), held)
    bundle = jnp.concatenate(
        [mean_high, mean - mean_high, flags, held, jnp.zeros((4, rows), F32)], axis=0
    )
    blank = jnp.zeros((4, rows), F32)
    ends = []
    for begin in (0, columns - EDGE):
        pieces = [source[c] for source in (heat, east, north) for c in range(begin, begin + EDGE)]
        pieces += [wet[begin : begin + EDGE], blank, bundle]
        ends.append(jnp.concatenate(pieces, axis=0))
    even = is_even()
    inner_out[...] = jnp.where(even, ends[1], ends[0]).astype(BF16)
    outer_out[...] = jnp.where(even, ends[0], ends[1]).astype(BF16)
    blocks_out[...] = jnp.concatenate([bundle, jnp.zeros((8, rows), F32)], axis=0).astype(BF16)


def members(nodes, grid_row):
    return one_hot(iota((nodes, grid_row.shape[1]), 0) == grid_row)


def plain_kernel(atmosphere, w_encode, grid_row, mesh_state, plain_out):
    member = members(mesh_state.shape[0], grid_row[...])
    population = jnp.sum(member.astype(F32), axis=1, keepdims=True)
    state = atmosphere[...]
    state = jnp.where(iota(state.shape, 0) == 0, 0.0, state.astype(F32)).astype(BF16)
    pooled = dot_nt(member, state) / jnp.maximum(population, 1.0)
    pooled_high = pooled.astype(BF16)
    pooled_low = (pooled - pooled_high.astype(F32)).astype(BF16)
    encode = w_encode[...]
    plain_out[...] = mesh_state[...].astype(F32) + dot(pooled_high, encode) + dot(pooled_low, encode)


def rolled_points(points, starts):
    rows = 2 * points.shape[1]
    empty = jnp.full((1, rows - points.shape[1]), 1 << 20, jnp.int32)
    return [
        pltpu.roll(jnp.concatenate([points[o : o + 1, :], empty], axis=1), starts[o], 1) for o in range(W)
    ]


def before(bundle_rows, o):
    lane = iota((1, bundle_rows.shape[1]), 1)
    return jnp.sum(jnp.where(lane < o, bundle_rows[3:4], 0.0)).astype(jnp.int32)


def latent_kernel(
    outer, far, inner, own, points, atmosphere, w_encode, grid_row, plain,
    latent_out, surface_out, placed_out,
):
    pair = [x[...].astype(F32)[-8:] for x in (inner, outer)]
    even = is_even()
    parts = [
        far[...].astype(F32)[:8],
        jnp.where(even, pair[0], pair[1]),
        own[...].astype(F32)[:8],
        jnp.where(even, pair[1], pair[0]),
    ]
    starts = [0, before(parts[1], 1), before(parts[2], 2), before(parts[3], 3)]
    placed = jnp.concatenate(rolled_points(points, starts), axis=1)
    placed_out[...] = placed
    n_points = grid_row.shape[1]
    values = jnp.concatenate(parts, axis=1).astype(BF16)
    match = one_hot(iota((n_points, placed.shape[1]), 0) == placed)
    sums = dot_nt(values, match)
    total = sums[0:1] + sums[1:2]
    number = sums[2:3]
    surface = jnp.where(
        number > 0.5, total / jnp.maximum(number, 1.0), atmosphere[0:16].astype(F32)[0:1]
    )
    surface_out[...] = surface
    pair = jnp.concatenate([surface, jnp.ones((7, n_points), F32)], axis=0).astype(BF16)
    pooled = dot_nt(members(plain.shape[0], grid_row[...]), pair)
    share = pooled[:, 0:1] / jnp.maximum(pooled[:, 1:2], 1.0)
    latent_out[...] = (plain[...] + share * w_encode[0:16].astype(F32)[0:1]).astype(BF16)


def listed_slots(neighbours):
    return neighbours[...].astype(F32).T


def slot_senders(listed, k):
    lane = iota(listed.shape, 1)
    return jnp.sum(jnp.where(lane == k, listed, 0.0), axis=1, keepdims=True).astype(jnp.int32)


def own_kernel(
    latent, w_in, geometry, w_geometry, neighbours, w_node_in, pre_out, base_out, node_out, sender, turned,
):
    nodes, features = latent.shape
    value = latent[...]
    sender[...] = dot(value, w_in[features : 2 * features]).astype(BF16)
    receiver = dot(value, w_in[2 * features :])
    node_out[...] = dot(value, w_node_in[:features])
    listed = listed_slots(neighbours)
    blank = jnp.zeros((4, geometry.shape[1]), F32)
    turned[:, :8] = jnp.concatenate([geometry[...].astype(F32), blank], axis=0).T
    blank = jnp.zeros((4, features), F32)
    w_geo = jnp.concatenate([w_geometry[...].astype(F32), blank], axis=0).astype(BF16)
    base = jnp.zeros((nodes, features), F32)
    for k in range(K):
        at = slot_senders(listed, k)
        edge = silu(dot(turned[pl.ds(k, nodes, stride=K), :8].astype(BF16), w_geo)).astype(BF16)
        match = one_hot(iota((nodes, nodes), 1) + nodes == at)
        joined = dot(edge, w_in[:features]) + dot(match, sender[...])
        pre_out[k] = (joined + receiver).astype(BF16)
        base = base + jnp.where(at < 3 * nodes, edge.astype(F32), 0.0)
    base_out[...] = base


def normal(values):
    average = jnp.mean(values, axis=-1, keepdims=True)
    centred = values - average
    variance = jnp.mean(centred * centred, axis=-1, keepdims=True)
    return centred, lax.rsqrt(variance + EPSILON)


def mesh_kernel(
    outer, inner, latent, w_in, w_out, pre, base, node_part, neighbours, w_node_in, w_node_out, w_decode,
    gain_edge, gain_node, grid_row, atmosphere, placed, node_out, flux_out, sender, total,
):
    nodes, features = latent.shape
    w_sender = w_in[features : 2 * features]
    sender[:nodes] = dot(inner[...], w_sender).astype(BF16)
    sender[nodes:] = dot(outer[...], w_sender).astype(BF16)
    below = jnp.where(is_even(), nodes, 0)
    above = nodes - below
    listed = listed_slots(neighbours)
    total[...] = jnp.zeros((nodes, features), F32)

    def step(k, carry):
        at = slot_senders(listed, k)
        place = jnp.where(at < nodes, at + below, jnp.where(at >= 2 * nodes, at - 2 * nodes + above, -1))
        place = jnp.where(at < 3 * nodes, place, -1)
        match = one_hot(iota((nodes, 2 * nodes), 1) == place)
        hidden = silu((pre[k].astype(F32) + dot(match, sender[...])).astype(BF16))
        centred, scale = normal(dot(hidden, w_out[...]))
        total[...] += centred * jnp.where(at < 3 * nodes, scale, 0.0)
        return carry

    lax.fori_loop(0, K, step, 0, unroll=True)
    aggregate = (base[...] + total[...] * gain_edge[...]).astype(BF16)
    hidden = silu(node_part[...] + dot(aggregate, w_node_in[features:])).astype(BF16)
    centred, scale = normal(dot(hidden, w_node_out[...]))
    node_new = (latent[...].astype(F32) + centred * scale * gain_node[...]).astype(BF16)
    node_out[...] = node_new
    flux = two_parts(dot_nt(w_decode[0:16], node_new)[1:2])
    flux = dot(flux, members(nodes, grid_row[...]))
    flux = atmosphere[0:16].astype(F32)[1:2] + flux[0:1] + flux[1:2]
    n_points = flux.shape[1]
    match = one_hot(iota((n_points, placed.shape[1]), 0) == placed[...])
    spread = dot(jnp.broadcast_to(flux, (8, n_points)).astype(BF16), match)
    rows = placed.shape[1] // W
    out = jnp.zeros((8, rows), F32)
    for o in range(W):
        out = jnp.where(iota((8, rows), 0) == o, spread[:, o * rows : (o + 1) * rows], out)
    flux_out[...] = jnp.concatenate([out, jnp.zeros((8, rows), F32)], axis=0).astype(BF16)


def two_parts(row):
    high = row.astype(BF16).astype(F32)
    return jnp.concatenate([high, row - high, jnp.zeros((6, row.shape[1]), F32)], axis=0).astype(BF16)


def decode_kernel(node_new, w_decode, grid_row, atmosphere, surface, state_out):
    change = dot_nt(w_decode[...], node_new[...])
    change_high = change.astype(BF16)
    change_low = (change - change_high.astype(F32)).astype(BF16)
    member = members(node_new.shape[0], grid_row[...])
    state = atmosphere[...].astype(F32)
    state = jnp.where(iota(state.shape, 0) == 0, surface[...].astype(BF16).astype(F32), state)
    state_out[...] = (state + dot(change_high, member) + dot(change_low, member)).astype(BF16)


def ready_kernel(heat, east, north, mask, inner, outer, field_out, wet_out, px_out, qx_out, py_out, qy_out, mix_out):
    columns, rows = mask.shape
    levels = heat.shape[1]
    pair = inner[...].astype(F32), outer[...].astype(F32)
    even = is_even()
    below, above = jnp.where(even, pair[1], pair[0]), jnp.where(even, pair[0], pair[1])
    own_wet = mask[...].astype(F32)

    def wide(source, at):
        left = [below[8 * (at * EDGE + c) : 8 * (at * EDGE + c) + 8] for c in range(EDGE)]
        right = [above[8 * (at * EDGE + c) : 8 * (at * EDGE + c) + 8] for c in range(EDGE)]
        return left + [source[c] for c in range(columns)] + right

    base = 3 * 8 * EDGE
    wet = [below[base + c : base + c + 1] for c in range(EDGE)]
    wet += [own_wet[c : c + 1] for c in range(columns)]
    wet += [above[base + c : base + c + 1] for c in range(EDGE)]
    wet = [jnp.broadcast_to(w, (levels, rows)) for w in wet]
    field, u, v = wide(heat, 0), wide(east, 1), wide(north, 2)
    lane = iota((levels, rows), 1)
    level = iota((levels, rows), 0)
    count = len(field)
    for c in range(count):
        field_out[c] = field[c]
        wet_out[c] = wet[c]
        mix_out[c] = jnp.where(level < levels - 1, COEFF_V * wet[c], 0.0)
        if c + 1 < count:
            opened = wet[c] * wet[c + 1]
            face = 0.25 * (u[c] + u[c + 1])
            px_out[c] = opened * (face + COEFF_H)
            qx_out[c] = opened * (face - COEFF_H)
        opened = jnp.where(lane < rows - 1, wet[c] * pltpu.roll(wet[c], rows - 1, 1), 0.0)
        face = 0.25 * (v[c] + pltpu.roll(v[c], rows - 1, 1))
        py_out[c] = opened * (face + COEFF_H)
        qy_out[c] = opened * (face - COEFF_H)


def ocean_kernel(before_1, before_3, far, after_1, near, here_flux, field_in, wet, px, qx, py, qy, mix, out):
    count, levels, rows = field_in.shape
    columns = count - 2 * EDGE
    triples = columns // 3
    span = rows // 3
    before_1, before_3, far, after_1, near, here_flux = (
        x[...].astype(F32) for x in (before_1, before_3, far, after_1, near, here_flux)
    )
    even = pair_is_even()
    before_2, after_2 = jnp.where(even, far, near), jnp.where(even, near, far)
    fluxes = [before_3, before_2, before_1, here_flux, after_1, after_2]

    def gathered(begin):
        return sum(fluxes[begin + o][o : o + 1] for o in range(W))

    own = gathered(1)
    blocks = [gathered(0)[:, (triples - 1) * span :]]
    blocks += [own[:, t * span : (t + 1) * span] for t in range(triples)]
    blocks += [gathered(2)[:, :span]]
    blocks += [jnp.zeros((16 - len(blocks), span), F32)]
    expand = one_hot(iota((span, rows), 1) // 3 == iota((span, rows), 0))
    cells = COEFF_Q * dot(jnp.concatenate(blocks, axis=0).astype(BF16), expand)
    level = iota((levels, rows), 0)
    surface = [
        jnp.where(level == 0, jnp.broadcast_to(cells[t : t + 1], (levels, rows)), 0.0)
        for t in range(triples + 2)
    ]
    field = [field_in[c] for c in range(count)]
    for step in range(STEPS):
        begin, end = step + 1, count - step - 1
        across = {c: px[c] * field[c] + qx[c] * field[c + 1] for c in range(begin - 1, end)}
        later = [None] * count
        for c in range(begin, end):
            here = field[c]
            along = py[c] * here + qy[c] * pltpu.roll(here, rows - 1, 1)
            mixed = mix[c] * (pltpu.roll(here, levels - 1, 0) - here)
            group = (c - EDGE + 3) // 3
            change = (
                (across[c - 1] - across[c])
                + (pltpu.roll(along, 1, 1) - along)
                + (mixed - pltpu.roll(mixed, 1, 0))
            )
            later[c] = wet[c] * (here + change + surface[group])
        field = later
    for c in range(columns):
        out[c] = field[EDGE + c]


VMEM = pl.BlockSpec(memory_space=pltpu.VMEM)
HBM = pl.BlockSpec(memory_space=pltpu.HBM)


def call(kernel, outs, inputs, spec=VMEM, scratch=(), flops=0, bytes_accessed=1 << 20, name=None):
    if spec is HBM:
        inputs = [pltpu.with_memory_space_constraint(x, pltpu.HBM) for x in inputs]
    return pl.pallas_call(
        kernel,
        out_shape=[jax.ShapeDtypeStruct(s, t) for s, t in outs],
        in_specs=[spec] * len(inputs),
        out_specs=[VMEM] * len(outs),
        scratch_shapes=list(scratch),
        compiler_params=pltpu.CompilerParams(vmem_limit_bytes=40 << 20),
        cost_estimate=pl.CostEstimate(flops=flops, bytes_accessed=bytes_accessed, transcendentals=0),
        name=name,
    )(*inputs)


def body(
    atmosphere,
    mesh_state,
    edge_geometry,
    neighbours,
    grid_node,
    ocean_heat_field,
    east_velocity,
    north_velocity,
    ocean_mask,
    intersection_points,
    intersection_counts,
    w_geometry,
    w_encode,
    w_edge_in,
    w_edge_out,
    w_node_in,
    w_node_out,
    w_decode,
    gain_edge,
    gain_node,
):
    levels, columns, rows = ocean_heat_field.shape
    nodes, features = mesh_state.shape
    n_points, channels = atmosphere.shape
    heat, east, north = (
        x.transpose(1, 0, 2) for x in (ocean_heat_field, east_velocity, north_velocity)
    )
    atmosphere_t = atmosphere.T
    slots = neighbours.T
    grid_row = grid_node.reshape(1, n_points)
    decode_t = w_decode.T
    ends = (3 * levels * EDGE + 16, rows)
    few = (16, rows)
    own_ocean = (columns, levels, rows)
    to_inner, to_outer, blocks = call(
        pack_kernel,
        [(ends, BF16), (ends, BF16), (few, BF16)],
        [intersection_counts, heat, east, north, ocean_mask],
        spec=HBM,
        scratch=[
            pltpu.SMEM((1, W), jnp.int32),
            pltpu.VMEM(own_ocean, F32),
            pltpu.VMEM(own_ocean, F32),
            pltpu.VMEM(own_ocean, F32),
            pltpu.VMEM((columns, rows), jnp.int32),
            pltpu.SemaphoreType.DMA((5,)),
        ],
        flops=2 * K * nodes * features * features,
        bytes_accessed=8 << 20,
        name="pack",
    )
    outer = sent(to_outer, OUTER)
    far = sent(blocks, (-2,))
    inner = sent(to_inner, INNER)
    (plain,) = call(
        plain_kernel,
        [((nodes, features), F32)],
        [atmosphere_t, w_encode, grid_row, mesh_state],
        flops=2 * K * nodes * features * features,
        bytes_accessed=8 << 20,
        name="plain",
    )
    latent, surface, placed = call(
        latent_kernel,
        [((nodes, features), BF16), ((1, n_points), F32), ((1, W * rows), jnp.int32)],
        [outer, far, inner, blocks, intersection_points[0], atmosphere_t, w_encode, grid_row, plain],
        name="latents",
    )
    latent_outer = sent(latent, OUTER)
    latent_inner = sent(latent, INNER)
    pre, base, node_part = call(
        own_kernel,
        [((K, nodes, features), BF16), ((nodes, features), F32), ((nodes, features), F32)],
        [latent, w_edge_in, edge_geometry, w_geometry, slots, w_node_in],
        scratch=[pltpu.VMEM((nodes, features), BF16), pltpu.VMEM((K * nodes, 128), F32)],
        flops=2 * K * nodes * (nodes + features) * features,
        bytes_accessed=10 << 20,
        name="own",
    )
    wide = (columns + 2 * EDGE, levels, rows)
    ready = call(
        ready_kernel,
        [(wide, F32)] * 7,
        [heat, east, north, ocean_mask, inner, outer],
        bytes_accessed=4 << 20,
        name="ready",
    )
    node_new, flux = call(
        mesh_kernel,
        [((nodes, features), BF16), (few, BF16)],
        [
            latent_outer, latent_inner, latent, w_edge_in, w_edge_out, pre, base, node_part, slots,
            w_node_in, w_node_out, decode_t, gain_edge.reshape(1, features),
            gain_node.reshape(1, features), grid_row, atmosphere_t, placed,
        ],
        scratch=[pltpu.VMEM((2 * nodes, features), BF16), pltpu.VMEM((nodes, features), F32)],
        flops=2 * K * nodes * 3 * nodes * features,
        bytes_accessed=10 << 20,
        name="mesh",
    )
    arrived = [sent(flux, route) for route in ((1,), (3,), FAR, (-1,), NEAR)]
    (state,) = call(
        decode_kernel,
        [((channels, n_points), BF16)],
        [node_new, decode_t, grid_row, atmosphere_t, surface],
        flops=6 * nodes * channels * n_points,
        name="decode",
    )
    (ocean_new,) = call(
        ocean_kernel,
        [(own_ocean, F32)],
        [*arrived, flux, *ready],
        bytes_accessed=4 << 20,
        name="ocean",
    )
    return (state.T, ocean_new.transpose(1, 0, 2))


def solution(mesh):
    ranges = ("member", "tile", "comp")
    placed = (
        P(ranges, None),
        P(ranges, None),
        P(None, ranges),
        P(ranges, None),
        P(ranges),
        P(None, ranges, None),
        P(None, ranges, None),
        P(None, ranges, None),
        P(ranges, None),
        P(ranges, None, None),
        P(ranges, None),
        P(),
        P(),
        P(),
        P(),
        P(),
        P(),
        P(),
        P(),
        P(),
    )
    return jax.shard_map(
        body,
        mesh=mesh,
        in_specs=placed,
        out_specs=(P(ranges, None), P(None, ranges, None)),
        check_vma=False,
    )
```
